32 devices in a mesh: leaf: 4 (over y, core), front: 8 (over z, x).
Axes of the slice: x: 2, y: 2, z: 4, core: 2. Of those that a mesh axis runs over, the one named last changes fastest.
Arguments:
- leaf_source: float32 [4, 2048, 128], P('leaf', 'front'), may hold values from -6 to 6
- mid_source: float32 [4, 2048, 128], P('leaf', 'front'), may hold values from -6 to 6
- root_source: float32 [8192, 128], P('front'), may hold values from -6 to 6
- leaf_inverse: float32 [4, 2, 2048, 2048], P('leaf', None, 'front'), may hold values from -0.09375 to 0.09375
- leaf_coupling: float32 [4, 2, 4096, 2048], P('leaf', None, None, 'front'), may hold values from -0.09375 to 0.09375
- mid_inverse: float32 [4, 2, 2048, 4096], P('leaf', None, None, 'front'), may hold values from -0.0625 to 0.0625
- mid_coupling: float32 [4, 2, 8192, 2048], P('leaf', None, None, 'front'), may hold values from -0.0625 to 0.0625
- root_inverse: float32 [2, 8192, 8192], P(None, 'leaf', 'front'), may hold values from -0.046875 to 0.046875
- leaf_blocks: int32 [4, 32], P('leaf'), may hold values from 0 to 31, as said below
- mid_blocks: int32 [2, 64], replicated, may hold values from 0 to 63, as said below
Outputs:
- leaf_solution: float32 [4, 2048, 128], P('leaf', 'front')
- mid_solution: float32 [4, 2048, 128], P('leaf', 'front')
- root_solution: float32 [8192, 128], P('front')
The draws below stay inside these ranges and needn't reach their ends.
Inputs may be any that keep to these rules, and one draw needn't show every extreme that they name: `leaf_blocks`: each row holds every block number of a level-1 separator exactly once. `mid_blocks`: each row holds every block number of the root separator exactly once.
All inputs are finite; a program needn't handle non-finite values.
Results may differ from the reference program's by a relative error of at most 0.00015.
Values sent between devices are 32-bit elements; how exact they have to be, the bound alone decides.
No kernel may reach another device: no remote copies, remote signals or barrier semaphores. Data moves between devices by JAX's collectives and lax.ppermute only.
A program may use at most 192 MiB of HBM per device.

```python
import jax
import jax.numpy as jnp
from jax import lax

S2 = 2048
S1 = 4096
S0 = 8192
NR = 64
N_LEAF = 4
N_FRONT = 8


def draw_leaf_blocks(key, part):
    rows = [jax.random.permutation(jax.random.fold_in(key, 101 + r), jnp.arange(S1 // 128, dtype=jnp.int32)) for r in range(N_LEAF)]
    return jnp.stack(rows).astype(jnp.int32)


def draw_mid_blocks(key, part):
    rows = [jax.random.permutation(jax.random.fold_in(key, 211 + r), jnp.arange(S0 // 128, dtype=jnp.int32)) for r in range(2)]
    return jnp.stack(rows).astype(jnp.int32)


def level_of(stream_key, extent, shards, least, high):
    gain, own = 1.0, jax.random.fold_in(stream_key, 6)
    for dim, shards_of in shards:
        steps = jnp.exp(jax.random.uniform(jax.random.fold_in(own, dim), (shards_of,), jnp.float32, least / len(shards), high / len(shards)))
        gain = gain * jnp.repeat(steps, extent[dim] // shards_of).reshape([-1 if axis == dim else 1 for axis in range(len(extent))])
    return gain


def gaussian(stream_key, extent, deviation, reach, shards=(), held_as=jnp.bfloat16):
    result = jax.random.normal(stream_key, extent, jnp.float32) * deviation
    if len(shards) > 0:
        result = level_of(stream_key, extent, shards, -0.22, 0.18) * result
    return jnp.clip(result, min=-reach, max=reach).astype(held_as)


def setup_inputs(seed: int = 0) -> dict:
    streams_of = jax.random.split(jax.random.key(seed), 11)
    leaf_source = gaussian(streams_of[0], (N_LEAF, S2, 2 * NR), 1.0, 6.0, ((0, 4), (1, 8)), jnp.float32)
    mid_source = gaussian(streams_of[1], (N_LEAF, S1 // 2, 2 * NR), 1.0, 6.0, ((0, 4), (1, 8)), jnp.float32)
    root_source = gaussian(streams_of[2], (S0, 2 * NR), 1.0, 6.0, ((0, 8),), jnp.float32)
    leaf_inverse = gaussian(streams_of[3], (N_LEAF, 2, S2, S2), (2 * S2) ** -0.5, 0.09375, ((0, 4), (2, 8)), jnp.float32)
    leaf_coupling = gaussian(streams_of[4], (N_LEAF, 2, S1, S2), (2 * S2) ** -0.5, 0.09375, ((0, 4), (3, 8)), jnp.float32)
    mid_inverse = gaussian(streams_of[5], (N_LEAF, 2, S1 // 2, S1), (2 * S1) ** -0.5, 0.0625, ((0, 4), (3, 8)), jnp.float32)
    mid_coupling = gaussian(streams_of[6], (N_LEAF, 2, S0, S1 // 2), (2 * S1) ** -0.5, 0.0625, ((0, 4), (3, 8)), jnp.float32)
    root_inverse = gaussian(streams_of[7], (2, S0, S0), (2 * S0) ** -0.5, 0.046875, ((1, 4), (2, 8)), jnp.float32)
    leaf_blocks = draw_leaf_blocks(jax.random.fold_in(streams_of[10], 71), 0)
    mid_blocks = draw_mid_blocks(jax.random.fold_in(streams_of[10], 71), 0)
    return {"leaf_source": leaf_source, "mid_source": mid_source, "root_source": root_source, "leaf_inverse": leaf_inverse, "leaf_coupling": leaf_coupling, "mid_inverse": mid_inverse, "mid_coupling": mid_coupling, "root_inverse": root_inverse, "leaf_blocks": leaf_blocks, "mid_blocks": mid_blocks}


exact_precision = lax.Precision.HIGHEST


def complex_apply(matrix, vectors):
    width = vectors.shape[1] // 2
    real_part = jnp.dot(matrix[0], vectors, precision=exact_precision, preferred_element_type=jnp.float32)
    imag_part = jnp.dot(matrix[1], vectors, precision=exact_precision, preferred_element_type=jnp.float32)
    return jnp.concatenate([real_part[:, :width] - imag_part[:, width:], real_part[:, width:] + imag_part[:, :width]], axis=1)


def complex_transposed(matrix, vectors):
    width = vectors.shape[1] // 2
    dims = (((0,), (0,)), ((), ()))
    real_part = lax.dot_general(matrix[0], vectors, dims, precision=exact_precision, preferred_element_type=jnp.float32)
    imag_part = lax.dot_general(matrix[1], vectors, dims, precision=exact_precision, preferred_element_type=jnp.float32)
    return jnp.concatenate([real_part[:, :width] - imag_part[:, width:], real_part[:, width:] + imag_part[:, :width]], axis=1)


def to_parent(values, blocks):
    inverse_order = jnp.argsort(blocks)
    count = values.shape[0] // 128
    return values.reshape(count, 128, values.shape[1])[inverse_order].reshape(values.shape)


def to_child(values, blocks):
    count = values.shape[0] // 128
    return values.reshape(count, 128, values.shape[1])[blocks].reshape(values.shape)


def reference(leaf_source, mid_source, root_source, leaf_inverse, leaf_coupling, mid_inverse, mid_coupling, root_inverse, leaf_blocks, mid_blocks):
    width2 = leaf_source.shape[2]
    half_rows = S1 // N_FRONT // 2
    solved_two = [complex_apply(leaf_inverse[c], leaf_source[c]) for c in range(N_LEAF)]
    mid_factor = []
    mid_couple = []
    solved_one = []
    for front_id in range(2):
        factor = jnp.concatenate([mid_inverse[2 * front_id], mid_inverse[2 * front_id + 1]], axis=1)
        couple = jnp.concatenate([mid_coupling[2 * front_id], mid_coupling[2 * front_id + 1]], axis=2)
        pair = mid_source[2 * front_id:2 * front_id + 2].reshape(2, N_FRONT, half_rows, width2)
        source_one = jnp.transpose(pair, (1, 0, 2, 3)).reshape(S1, width2)
        for child in (2 * front_id, 2 * front_id + 1):
            source_one = source_one - to_parent(complex_apply(leaf_coupling[child], solved_two[child]), leaf_blocks[child])
        mid_factor.append(factor)
        mid_couple.append(couple)
        solved_one.append(complex_apply(factor, source_one))
    reduced_root = root_source
    for front_id in range(2):
        reduced_root = reduced_root - to_parent(complex_apply(mid_couple[front_id], solved_one[front_id]), mid_blocks[front_id])
    solved_root = complex_apply(root_inverse, reduced_root)
    root_solution = complex_transposed(root_inverse, solved_root)
    mid_full = []
    mid_pieces = []
    for front_id in range(2):
        rest = solved_one[front_id] - complex_transposed(mid_couple[front_id], to_child(root_solution, mid_blocks[front_id]))
        solution_one = complex_transposed(mid_factor[front_id], rest)
        mid_full.append(solution_one)
        split = jnp.transpose(solution_one.reshape(N_FRONT, 2, half_rows, width2), (1, 0, 2, 3)).reshape(2, S1 // 2, width2)
        mid_pieces.append(split)
    mid_solution = jnp.concatenate(mid_pieces, axis=0)
    leaf_out = []
    for child in range(N_LEAF):
        rest = solved_two[child] - complex_transposed(leaf_coupling[child], to_child(mid_full[child // 2], leaf_blocks[child]))
        leaf_out.append(complex_transposed(leaf_inverse[child], rest))
    leaf_solution = jnp.stack(leaf_out, axis=0)
    return leaf_solution, mid_solution, root_solution
```

```python
import functools

import jax
import jax.numpy as jnp
from jax import lax
from jax.experimental import pallas as pl
from jax.experimental.pallas import tpu as pltpu
from jax.sharding import PartitionSpec as P

exact_precision = lax.Precision.HIGHEST
BLOCK = 128
VMEM = pltpu.VMEM


def halves(values):
    high = values.astype(jnp.bfloat16)
    low = (values - high.astype(jnp.float32)).astype(jnp.bfloat16)
    return high, low


def turned_columns(vectors):
    width = vectors.shape[1] // 2
    return jnp.concatenate([-vectors[:, width:], vectors[:, :width]], axis=1)


def turned_rows(vectors):
    width = vectors.shape[0] // 2
    return jnp.concatenate([-vectors[width:], vectors[:width]], axis=0)


def dot32(left, right):
    return jnp.dot(left, right, preferred_element_type=jnp.float32)


def call(kernel, scalars, operands, matrix, outs, scratch, flops):
    bytes_moved = 4 * sum(a.size for a in [*operands, matrix]) + 4 * sum(o.size for o in outs)
    return pl.pallas_call(
        kernel,
        out_shape=outs,
        in_specs=[pl.BlockSpec(memory_space=pltpu.SMEM)] * len(scalars)
        + [pl.BlockSpec(memory_space=VMEM)] * len(operands)
        + [pl.BlockSpec(memory_space=pl.ANY)],
        out_specs=[pl.BlockSpec(memory_space=VMEM)] * len(outs),
        scratch_shapes=scratch,
        compiler_params=pltpu.CompilerParams(vmem_limit_bytes=48 * 1024 * 1024),
        cost_estimate=pl.CostEstimate(flops=flops, bytes_accessed=bytes_moved, transcendentals=0),
    )(*scalars, *operands, matrix)


def tile_of(slots, index):
    real_high, real_low = halves(slots[index, 0])
    imag_high, imag_low = halves(slots[index, 1])
    return real_high, imag_high, real_low, imag_low


def lift_kernel(parts, counts, unit, starts, places, *refs):
    chunk_refs, (matrix, *rest) = refs[:parts], refs[parts:]
    outs, (slots, natural, weights, sems) = rest[: len(counts)], rest[len(counts) :]
    rows, depth = slots.shape[2], slots.shape[3]
    per = rows // unit
    total = sum(counts)

    def fetch(index):
        slot, inner = index // per, index % per
        start = pl.multiple_of(starts[index], unit)
        return pltpu.make_async_copy(
            matrix.at[:, pl.ds(start, unit), :],
            slots.at[slot, :, pl.ds(pl.multiple_of(inner * unit, unit), unit), :],
            sems.at[index],
        )

    @pl.loop(0, total * per)
    def _(index):
        fetch(index).start()

    step = chunk_refs[0].shape[0]
    for part in range(parts):
        place = pl.multiple_of(places[part], step)
        natural[pl.ds(place, step), :] = chunk_refs[part][...]
    for half, values in enumerate((natural[...], turned_columns(natural[...]))):
        high, low = halves(values)
        weights[half * depth : (half + 1) * depth, :BLOCK] = high
        weights[half * depth : (half + 1) * depth, BLOCK:] = low

    done = 0
    for out, count in zip(outs, counts):

        @pl.loop(0, count)
        def _(index, out=out, done=done):
            slot = index + done
            for inner in range(per):
                fetch(slot * per + inner).wait()
            real_high, imag_high, real_low, imag_low = tile_of(slots, slot)
            wide = dot32(jnp.concatenate([real_high, imag_high], axis=1), weights[...])
            thin = dot32(jnp.concatenate([real_low, imag_low], axis=1), weights[:, :BLOCK])
            out[index] = wide[:, :BLOCK] + wide[:, BLOCK:] + thin

        done += count


def lift(matrix, chunks, places, starts, unit, rows, counts):
    parts, depth, width = len(chunks), matrix.shape[2], chunks[0].shape[1]
    total = sum(counts)
    outs = [jax.ShapeDtypeStruct((count, rows, width), jnp.float32) for count in counts]
    if depth % BLOCK or width != BLOCK or chunks[0].shape[0] % BLOCK or unit % BLOCK:
        vectors = jnp.zeros((depth, width), jnp.float32)
        for part in range(parts):
            vectors = lax.dynamic_update_slice(vectors, chunks[part], (places[part], 0))
        picked = (starts[:, None] + jnp.arange(unit, dtype=jnp.int32)).reshape(-1)
        taken = jnp.take(matrix, picked, axis=1)
        dot = functools.partial(jnp.dot, precision=exact_precision)
        whole = dot(taken[0], vectors) + dot(taken[1], turned_columns(vectors))
        whole = whole.reshape(total, rows, width)
        ends = [sum(counts[: i + 1]) for i in range(len(counts))]
        return [whole[end - count : end] for end, count in zip(ends, counts)]
    return call(
        functools.partial(lift_kernel, parts, counts, unit),
        [starts, places],
        chunks,
        matrix,
        outs,
        [
            VMEM((total, 2, rows, depth), jnp.float32),
            VMEM((depth, BLOCK), jnp.float32),
            VMEM((2 * depth, 2 * BLOCK), jnp.bfloat16),
            pltpu.SemaphoreType.DMA((total * (rows // unit),)),
        ],
        2 * 4 * total * rows * depth * 2 * BLOCK,
    )


def fold_kernel(parts, columns, *refs):
    chunk_refs, (matrix, out, slots, total, sems) = refs[:parts], refs[parts:]
    depth = slots.shape[3]

    def fetch(part):
        column = pl.multiple_of(columns[part], depth)
        return pltpu.make_async_copy(
            matrix.at[:, :, pl.ds(column, depth)], slots.at[part], sems.at[part]
        )

    for part in range(parts):
        fetch(part).start()
    for part in range(parts):
        values = chunk_refs[part][...]
        high, low = halves(values)
        turned_high, turned_low = halves(turned_columns(values))
        highs = jnp.concatenate([high, turned_high], axis=0)
        both = jnp.concatenate([highs, jnp.concatenate([low, turned_low], axis=0)], axis=1)
        fetch(part).wait()
        real_high, imag_high, real_low, imag_low = tile_of(slots, part)
        wide = dot32(jnp.concatenate([real_high, imag_high], axis=1), both)
        thin = dot32(jnp.concatenate([real_low, imag_low], axis=1), highs)
        term = wide[:, :BLOCK] + wide[:, BLOCK:] + thin
        total[...] = term if part == 0 else total[...] + term
    out[...] = total[...]


def fold(matrix, chunks, columns):
    parts, rows, (depth, width) = len(chunks), matrix.shape[1], chunks[0].shape
    if depth % BLOCK or width != BLOCK or rows % BLOCK:
        picked = (columns[:, None] + jnp.arange(depth, dtype=jnp.int32)).reshape(-1)
        taken = jnp.take(matrix, picked, axis=2)
        vectors = jnp.concatenate(chunks, axis=0)
        dot = functools.partial(jnp.dot, precision=exact_precision)
        return dot(taken[0], vectors) + dot(taken[1], turned_columns(vectors))
    return call(
        functools.partial(fold_kernel, parts),
        [columns],
        chunks,
        matrix,
        [jax.ShapeDtypeStruct((rows, BLOCK), jnp.float32)],
        [
            VMEM((parts, 2, rows, depth), jnp.float32),
            VMEM((rows, BLOCK), jnp.float32),
            pltpu.SemaphoreType.DMA((parts,)),
        ],
        2 * 4 * parts * rows * depth * 2 * BLOCK,
    )[0]


def pull_kernel(parts, pieces, unit, starts, places, *refs):
    chunk_refs, (matrix, *rest) = refs[:parts], refs[parts:]
    outs, (slots, vectors, total, sems) = rest[:pieces], rest[pieces:]
    depth, columns = slots.shape[2], slots.shape[3]
    per = depth // unit

    def fetch(index):
        slot, inner = index // per, index % per
        start = pl.multiple_of(starts[index], unit)
        return pltpu.make_async_copy(
            matrix.at[:, pl.ds(start, unit), :],
            slots.at[slot, :, pl.ds(pl.multiple_of(inner * unit, unit), unit), :],
            sems.at[index],
        )

    @pl.loop(0, parts * per)
    def _(index):
        fetch(index).start()

    for part in range(parts):
        values = chunk_refs[part][...]
        for half, side in enumerate((values, turned_rows(values))):
            high, low = halves(side)
            vectors[part, :BLOCK, half * depth : (half + 1) * depth] = high
            vectors[part, BLOCK:, half * depth : (half + 1) * depth] = low

    total[...] = jnp.zeros_like(total)

    @pl.loop(0, parts)
    def _(slot):
        for inner in range(per):
            fetch(slot * per + inner).wait()
        for at in range(0, columns, 256):
            here = slice(at, min(at + 256, columns))
            real_high, real_low = halves(slots[slot, 0, :, here])
            imag_high, imag_low = halves(slots[slot, 1, :, here])
            wide = dot32(vectors[slot], jnp.concatenate([real_high, imag_high], axis=0))
            thin = dot32(vectors[slot, :BLOCK], jnp.concatenate([real_low, imag_low], axis=0))
            total[:, here] += wide[:BLOCK] + wide[BLOCK:] + thin

    for piece, out in enumerate(outs):
        place = pl.multiple_of(places[piece], out.shape[1])
        out[...] = total[:, pl.ds(place, out.shape[1])]


def pull(matrix, chunks, starts, unit, places, size):
    parts, columns, (width, depth) = len(chunks), matrix.shape[2], chunks[0].shape
    pieces = places.shape[0]
    if depth % BLOCK or width != BLOCK or columns % BLOCK or size % BLOCK or unit % BLOCK:
        picked = (starts[:, None] + jnp.arange(unit, dtype=jnp.int32)).reshape(-1)
        taken = jnp.take(matrix, picked, axis=1)
        vectors = jnp.concatenate(chunks, axis=1)
        dot = functools.partial(jnp.dot, precision=exact_precision)
        whole = dot(vectors, taken[0]) + dot(turned_rows(vectors), taken[1])
        return [
            lax.dynamic_slice(whole, (0, places[piece]), (width, size)) for piece in range(pieces)
        ]
    return call(
        functools.partial(pull_kernel, parts, pieces, unit),
        [starts, places],
        chunks,
        matrix,
        [jax.ShapeDtypeStruct((BLOCK, size), jnp.float32)] * pieces,
        [
            VMEM((parts, 2, depth, columns), jnp.float32),
            VMEM((parts, 2 * BLOCK, 2 * depth), jnp.bfloat16),
            VMEM((BLOCK, columns), jnp.float32),
            pltpu.SemaphoreType.DMA((parts * (depth // unit),)),
        ],
        2 * 3 * parts * depth * columns * 2 * BLOCK,
    )


def spread_kernel(columns, vectors, matrix, *refs):
    pieces = len(refs) - 2
    outs, (slots, sems) = refs[:pieces], refs[pieces:]
    size = slots.shape[3]

    def fetch(piece):
        column = pl.multiple_of(columns[piece], size)
        return pltpu.make_async_copy(
            matrix.at[:, :, pl.ds(column, size)], slots.at[piece], sems.at[piece]
        )

    for piece in range(pieces):
        fetch(piece).start()
    values = vectors[...]
    high, low = halves(values)
    turned_high, turned_low = halves(turned_rows(values))
    highs = jnp.concatenate([high, turned_high], axis=1)
    both = jnp.concatenate([highs, jnp.concatenate([low, turned_low], axis=1)], axis=0)
    for piece in range(pieces):
        fetch(piece).wait()
        real_high, imag_high, real_low, imag_low = tile_of(slots, piece)
        wide = dot32(both, jnp.concatenate([real_high, imag_high], axis=0))
        thin = dot32(highs, jnp.concatenate([real_low, imag_low], axis=0))
        outs[piece][...] = wide[:BLOCK] + wide[BLOCK:] + thin


def spread(matrix, vectors, columns, size):
    pieces, depth, width = columns.shape[0], matrix.shape[1], vectors.shape[0]
    if depth % BLOCK or width != BLOCK or size % BLOCK:
        dot = functools.partial(jnp.dot, precision=exact_precision)
        whole = dot(vectors, matrix[0]) + dot(turned_rows(vectors), matrix[1])
        return [
            lax.dynamic_slice(whole, (0, columns[piece]), (width, size)) for piece in range(pieces)
        ]
    return call(
        spread_kernel,
        [columns],
        [vectors],
        matrix,
        [jax.ShapeDtypeStruct((BLOCK, size), jnp.float32)] * pieces,
        [VMEM((pieces, 2, depth, size), jnp.float32), pltpu.SemaphoreType.DMA((pieces,))],
        2 * 3 * pieces * depth * size * 2 * BLOCK,
    )


def move(value, route):
    groups, fronts = lax.axis_size("leaf"), lax.axis_size("front")
    pairs = []
    for leaf in range(groups):
        for front in range(fronts):
            to_leaf, to_front = route(leaf, front)
            pairs.append((leaf * fronts + front, to_leaf * fronts + to_front % fronts))
    return lax.ppermute(value, ("leaf", "front"), pairs)


def onward(value):
    return move(value, lambda leaf, front: (leaf, front + 2))


def across(value):
    return move(value, lambda leaf, front: (leaf, front ^ 1))


def sibling(value):
    return move(value, lambda leaf, front: (leaf ^ 1, front))


def opposite(value):
    return move(value, lambda leaf, front: (leaf ^ 2, front))


def first_way(leaf, front):
    return (leaf ^ 2, front) if leaf % 2 else (leaf, front ^ 1)


def second_way(leaf, front):
    return (leaf, front ^ 1) if leaf % 2 else (leaf ^ 2, front)


def gather_front(own):
    held, chunks = own, []
    rounds = lax.axis_size("front") // 2
    for step in range(rounds):
        after = onward(held) if step < rounds - 1 else None
        chunks += [held, across(held)]
        held = after
    return chunks


def front_sources(front):
    fronts = lax.axis_size("front")
    own = (front - 2 * jnp.arange(fronts // 2, dtype=jnp.int32)) % fronts
    return jnp.stack([own, own ^ 1], axis=1).reshape(-1)


def front_targets(front):
    fronts = lax.axis_size("front")
    own = (front - 2 - 2 * jnp.arange(fronts // 2, dtype=jnp.int32)) % fronts
    return jnp.stack([own ^ 1, own], axis=1).reshape(-1)


def scatter_front(pieces):
    carried = None
    for step in range(len(pieces) // 2):
        given, kept = pieces[2 * step], pieces[2 * step + 1]
        summed = kept + across(given)
        if carried is not None:
            summed = summed + carried
        if step < len(pieces) // 2 - 1:
            carried = onward(summed)
    return summed


def body(
    leaf_source,
    mid_source,
    root_source,
    leaf_inverse,
    leaf_coupling,
    mid_inverse,
    mid_coupling,
    root_inverse,
    leaf_blocks,
    mid_blocks,
):
    fronts = lax.axis_size("front")
    rounds = fronts // 2
    group, front = lax.axis_index("leaf"), lax.axis_index("front")
    side = group % 2
    source_two, source_one = leaf_source[0], mid_source[0]
    inverse_two, coupling_two = leaf_inverse[0], leaf_coupling[0]
    inverse_one, coupling_one = mid_inverse[0], mid_coupling[0]
    rows_two = source_two.shape[0]
    half = source_one.shape[0]
    block_rows = 2 * half
    root_block = root_source.shape[0]
    quarter = root_block // lax.axis_size("leaf")
    root_rows = root_inverse.shape[1]

    def backwards(order):
        count = order.shape[0]
        numbers = jnp.arange(count, dtype=jnp.int32)
        hits = order[None, :] == numbers[:, None]
        return jnp.sum(jnp.where(hits, numbers[None, :], 0), axis=1, dtype=jnp.int32)

    child_two = backwards(leaf_blocks[0])
    child_one = backwards(lax.dynamic_index_in_dim(mid_blocks, group // 2, 0, keepdims=False))

    def unit_rows(parent_rows, rows, child):
        unit = min(BLOCK, rows)
        units = (
            parent_rows[:, None] + unit * jnp.arange(rows // unit, dtype=jnp.int32)[None, :]
        ).reshape(-1)
        return child[units // BLOCK] * BLOCK + units % BLOCK, unit

    sources = front_sources(front)
    targets = front_targets(front)
    nothing = jnp.zeros((1,), jnp.int32)

    solved_two = fold(inverse_two, gather_front(source_two), sources * rows_two)

    lift_rows = jnp.concatenate(
        [targets * block_rows + (1 - side) * half, targets * block_rows + side * half]
    )
    starts, unit = unit_rows(lift_rows, half, child_two)
    lifted = lift(coupling_two, [solved_two], nothing, starts, unit, half, [2] * (2 * rounds))
    pieces = []
    for step in range(rounds):
        met = lifted[rounds + step] + sibling(lifted[step])
        pieces += [met[0], met[1]]
    own_half = source_one - scatter_front(pieces)

    halves_of = jnp.stack([side * half, (1 - side) * half])
    parts = lift(
        inverse_one,
        [own_half, sibling(own_half)],
        halves_of,
        targets * half,
        half,
        half,
        [1] * fronts,
    )
    solved_one = scatter_front([part[0] for part in parts])

    def quarter_rows(leaf, front_ids):
        core = leaf % 2
        beside = front_ids ^ 1
        over = leaf ^ 2
        first = jnp.where(core == 0, beside * root_block + leaf * quarter, front_ids * root_block + over * quarter)
        second = jnp.where(core == 0, front_ids * root_block + over * quarter, beside * root_block + leaf * quarter)
        return jnp.stack(
            [front_ids * root_block + leaf * quarter, first, second, beside * root_block + over * quarter],
            axis=1,
        ).reshape(-1)

    ring_targets = targets[1::2]
    lift_rows = jnp.concatenate(
        [quarter_rows(group ^ 1, ring_targets), quarter_rows(group, ring_targets)]
    )
    starts, unit = unit_rows(lift_rows, quarter, child_one)
    lifted = lift(coupling_one, [solved_one], nothing, starts, unit, quarter, [4] * (2 * rounds))
    carried = None
    for step in range(rounds):
        mine, theirs = lifted[rounds + step], sibling(lifted[step])
        far = move(mine[3] + theirs[3], second_way)
        first = move(mine[1] + theirs[1] + far, first_way)
        second = move(mine[2] + theirs[2], second_way)
        summed = mine[0] + theirs[0] + first + second
        if carried is not None:
            summed = summed + carried
        if step < rounds - 1:
            carried = onward(summed)
    own_source = lax.dynamic_slice_in_dim(root_source, group * quarter, quarter, 0)
    own_quarter = own_source - summed
    over_quarter = opposite(own_quarter)
    quarters = [own_quarter, over_quarter, sibling(own_quarter), sibling(over_quarter)]
    leaves_of = jnp.stack([group, group ^ 2, group ^ 1, group ^ 3])

    parts = lift(
        root_inverse,
        quarters,
        leaves_of * quarter,
        targets * (root_rows // fronts),
        root_rows // fronts,
        root_rows // fronts,
        [1] * fronts,
    )
    whole_piece = scatter_front([part[0] for part in parts])
    root_chunks = gather_front(whole_piece.T)
    theirs_own, theirs_over, mine_own, mine_over = pull(
        root_inverse,
        root_chunks,
        sources * (root_rows // fronts),
        root_rows // fronts,
        jnp.stack([group ^ 1, group ^ 3, group, group ^ 2]) * quarter,
        quarter,
    )
    own = mine_own + sibling(theirs_own)
    over = mine_over + sibling(theirs_over)
    own_quarter = own + opposite(over)

    held, mine = own_quarter, []
    for step in range(rounds):
        after = onward(held) if step < rounds - 1 else None
        first = move(held, first_way)
        second = move(held, second_way)
        mine += [held, first, second, move(first, second_way)]
        held = after
    theirs = [sibling(chunk) for chunk in mine]
    beside_core = side == 0
    quarters = jnp.stack(
        [
            mine[0],
            theirs[0],
            jnp.where(beside_core, mine[2], mine[1]),
            jnp.where(beside_core, theirs[1], theirs[2]),
        ]
    )
    natural = jnp.take(quarters, jnp.arange(4, dtype=jnp.int32) ^ group, axis=0)
    root_solution = jnp.transpose(natural, (0, 2, 1)).reshape(root_block, natural.shape[1])

    ring_sources = sources[0::2]
    pull_rows = jnp.concatenate(
        [quarter_rows(group, ring_sources), quarter_rows(group ^ 1, ring_sources)]
    )
    starts, unit = unit_rows(pull_rows, quarter, child_one)
    pulled_one = pull(coupling_one, mine + theirs, starts, unit, nothing, coupling_one.shape[2])[0]
    rest_one = solved_one.T - pulled_one
    theirs, mine = pull(
        inverse_one,
        gather_front(rest_one),
        sources * half,
        half,
        jnp.stack([1 - side, side]) * half,
        half,
    )
    mid_columns = mine + sibling(theirs)
    mid_solution = mid_columns.T

    mine = gather_front(mid_columns)
    theirs = [sibling(chunk) for chunk in mine]
    pull_rows = jnp.concatenate(
        [sources * block_rows + side * half, sources * block_rows + (1 - side) * half]
    )
    starts, unit = unit_rows(pull_rows, half, child_two)
    pulled_two = pull(coupling_two, mine + theirs, starts, unit, nothing, rows_two)[0]
    rest_two = solved_two.T - pulled_two
    parts = spread(inverse_two, rest_two, targets * rows_two, rows_two)
    leaf_solution = scatter_front(parts).T
    return (leaf_solution[None], mid_solution[None], root_solution)


def solution(mesh):
    placed = (
        P("leaf", "front", None),
        P("leaf", "front", None),
        P("front", None),
        P("leaf", None, "front", None),
        P("leaf", None, None, "front"),
        P("leaf", None, None, "front"),
        P("leaf", None, None, "front"),
        P(None, "leaf", "front"),
        P("leaf", None),
        P(),
    )
    return jax.shard_map(
        body,
        mesh=mesh,
        in_specs=placed,
        out_specs=(P("leaf", "front", None), P("leaf", "front", None), P("front", None)),
        check_vma=False,
    )
```

```python
import functools
import math

import jax
import jax.numpy as jnp
from jax import lax
from jax.experimental import pallas as pl
from jax.experimental.pallas import tpu as pltpu
from jax.sharding import PartitionSpec as P

exact_precision = lax.Precision.HIGHEST
BLOCK = 128
VMEM = pltpu.VMEM


def halves(values):
    high = values.astype(jnp.bfloat16)
    low = (values - high.astype(jnp.float32)).astype(jnp.bfloat16)
    return high, low


def turned_columns(vectors):
    width = vectors.shape[1] // 2
    return jnp.concatenate([-vectors[:, width:], vectors[:, :width]], axis=1)


def turned_rows(vectors):
    width = vectors.shape[0] // 2
    return jnp.concatenate([-vectors[width:], vectors[:width]], axis=0)


def dot32(left, right):
    return jnp.dot(left, right, preferred_element_type=jnp.float32)


def call(kernel, scalars, operands, matrix, outs, scratch, flops):
    bytes_held = 4 * sum(a.size for a in [*operands, matrix]) + 4 * sum(o.size for o in outs)
    scratch_bytes = sum(math.prod(s.shape) * s.dtype.itemsize for s in scratch)
    return pl.pallas_call(
        kernel,
        out_shape=outs,
        in_specs=[pl.BlockSpec(memory_space=pltpu.SMEM)] * len(scalars)
        + [pl.BlockSpec(memory_space=VMEM)] * (len(operands) + 1),
        out_specs=[pl.BlockSpec(memory_space=VMEM)] * len(outs),
        scratch_shapes=scratch,
        compiler_params=pltpu.CompilerParams(
            vmem_limit_bytes=bytes_held + scratch_bytes + 8 * 1024 * 1024
        ),
        cost_estimate=pl.CostEstimate(flops=flops, bytes_accessed=bytes_held, transcendentals=0),
    )(*scalars, *operands, matrix)


def wide_of(real, imag):
    real_high, real_low = halves(real)
    imag_high, imag_low = halves(imag)
    return jnp.concatenate([real_high, imag_high, real_low, imag_low], axis=1)


def lift_kernel(parts, counts, unit, rows, starts, places, *refs):
    chunk_refs, (matrix, *rest) = refs[:parts], refs[parts:]
    outs, (natural, weights) = rest[: len(counts)], rest[len(counts) :]
    depth = matrix.shape[2]
    per = rows // unit
    step = chunk_refs[0].shape[0]
    for part in range(parts):
        place = pl.multiple_of(places[part], step)
        natural[pl.ds(place, step), :] = chunk_refs[part][...]
    for half, values in enumerate((natural[...], turned_columns(natural[...]))):
        high, low = halves(values)
        both = jnp.concatenate([high, low], axis=1)
        weights[half * depth : (half + 1) * depth, :] = both
        weights[(half + 2) * depth : (half + 3) * depth, :] = both

    done = 0
    for out, count in zip(outs, counts):
        together = 2 if count % 2 == 0 else 1
        for index in range(0, count, together):
            units = [
                pl.multiple_of(starts[(done + index) * per + inner], unit)
                for inner in range(per * together)
            ]
            real = jnp.concatenate([matrix[0, pl.ds(at, unit), :] for at in units], axis=0)
            imag = jnp.concatenate([matrix[1, pl.ds(at, unit), :] for at in units], axis=0)
            wide = dot32(wide_of(real, imag), weights[...])
            whole = wide[:, :BLOCK] + wide[:, BLOCK:]
            out[index : index + together] = whole.reshape(together, rows, BLOCK)
        done += count


def lift(matrix, chunks, places, starts, unit, rows, counts):
    parts, depth, width = len(chunks), matrix.shape[2], chunks[0].shape[1]
    total = sum(counts)
    outs = [jax.ShapeDtypeStruct((count, rows, width), jnp.float32) for count in counts]
    if depth % BLOCK or width != BLOCK or chunks[0].shape[0] % BLOCK or unit % BLOCK:
        vectors = jnp.zeros((depth, width), jnp.float32)
        for part in range(parts):
            vectors = lax.dynamic_update_slice(vectors, chunks[part], (places[part], 0))
        picked = (starts[:, None] + jnp.arange(unit, dtype=jnp.int32)).reshape(-1)
        taken = jnp.take(matrix, picked, axis=1)
        dot = functools.partial(jnp.dot, precision=exact_precision)
        whole = dot(taken[0], vectors) + dot(taken[1], turned_columns(vectors))
        whole = whole.reshape(total, rows, width)
        ends = [sum(counts[: i + 1]) for i in range(len(counts))]
        return [whole[end - count : end] for end, count in zip(ends, counts)]
    return call(
        functools.partial(lift_kernel, parts, counts, unit, rows),
        [starts, places],
        chunks,
        matrix,
        outs,
        [VMEM((depth, BLOCK), jnp.float32), VMEM((4 * depth, 2 * BLOCK), jnp.bfloat16)],
        2 * 4 * total * rows * depth * 2 * BLOCK,
    )


def fold_kernel(parts, columns, *refs):
    chunk_refs, (matrix, out) = refs[:parts], refs[parts:]
    depth = chunk_refs[0].shape[0]
    total = None
    for part in range(parts):
        values = chunk_refs[part][...]
        high, low = halves(values)
        turned_high, turned_low = halves(turned_columns(values))
        both = jnp.concatenate(
            [
                jnp.concatenate([high, low], axis=1),
                jnp.concatenate([turned_high, turned_low], axis=1),
            ],
            axis=0,
        )
        here = pl.ds(pl.multiple_of(columns[part], depth), depth)
        wide = dot32(
            wide_of(matrix[0, :, here], matrix[1, :, here]), jnp.concatenate([both, both], axis=0)
        )
        term = wide[:, :BLOCK] + wide[:, BLOCK:]
        total = term if total is None else total + term
    out[...] = total


def fold(matrix, chunks, columns):
    parts, rows, (depth, width) = len(chunks), matrix.shape[1], chunks[0].shape
    if depth % BLOCK or width != BLOCK or rows % BLOCK:
        picked = (columns[:, None] + jnp.arange(depth, dtype=jnp.int32)).reshape(-1)
        taken = jnp.take(matrix, picked, axis=2)
        vectors = jnp.concatenate(chunks, axis=0)
        dot = functools.partial(jnp.dot, precision=exact_precision)
        return dot(taken[0], vectors) + dot(taken[1], turned_columns(vectors))
    return call(
        functools.partial(fold_kernel, parts),
        [columns],
        chunks,
        matrix,
        [jax.ShapeDtypeStruct((rows, BLOCK), jnp.float32)],
        [],
        2 * 4 * parts * rows * depth * 2 * BLOCK,
    )[0]


def pull_kernel(parts, pieces, unit, starts, places, *refs):
    chunk_refs, (matrix, *rest) = refs[:parts], refs[parts:]
    outs, (vectors, total) = rest[:pieces], rest[pieces:]
    depth, columns = chunk_refs[0].shape[1], matrix.shape[2]
    per = depth // unit
    for part in range(parts):
        values = chunk_refs[part][...]
        for half, side in enumerate((values, turned_rows(values))):
            high, low = halves(side)
            vectors[part, :BLOCK, half * depth : (half + 1) * depth] = high
            vectors[part, BLOCK:, half * depth : (half + 1) * depth] = low

    total[...] = jnp.zeros_like(total)

    @pl.loop(0, parts, unroll=2)
    def _(slot):
        units = [pl.multiple_of(starts[slot * per + inner], unit) for inner in range(per)]
        for at in range(0, columns, 256):
            here = slice(at, min(at + 256, columns))
            split = [
                halves(matrix[part, pl.ds(start, unit), here]) for part in (0, 1) for start in units
            ]
            highs = jnp.concatenate([high for high, _ in split], axis=0)
            lows = jnp.concatenate([low for _, low in split], axis=0)
            wide = dot32(vectors[slot], highs)
            thin = dot32(vectors[slot, :BLOCK], lows)
            total[:, here] += wide[:BLOCK] + wide[BLOCK:] + thin

    for piece, out in enumerate(outs):
        place = pl.multiple_of(places[piece], out.shape[1])
        out[...] = total[:, pl.ds(place, out.shape[1])]


def pull(matrix, chunks, starts, unit, places, size):
    parts, columns, (width, depth) = len(chunks), matrix.shape[2], chunks[0].shape
    pieces = places.shape[0]
    if depth % BLOCK or width != BLOCK or columns % BLOCK or size % BLOCK or unit % BLOCK:
        picked = (starts[:, None] + jnp.arange(unit, dtype=jnp.int32)).reshape(-1)
        taken = jnp.take(matrix, picked, axis=1)
        vectors = jnp.concatenate(chunks, axis=1)
        dot = functools.partial(jnp.dot, precision=exact_precision)
        whole = dot(vectors, taken[0]) + dot(turned_rows(vectors), taken[1])
        return [
            lax.dynamic_slice(whole, (0, places[piece]), (width, size)) for piece in range(pieces)
        ]
    return call(
        functools.partial(pull_kernel, parts, pieces, unit),
        [starts, places],
        chunks,
        matrix,
        [jax.ShapeDtypeStruct((BLOCK, size), jnp.float32)] * pieces,
        [
            VMEM((parts, 2 * BLOCK, 2 * depth), jnp.bfloat16),
            VMEM((BLOCK, columns), jnp.float32),
        ],
        2 * 3 * parts * depth * columns * 2 * BLOCK,
    )


def spread_kernel(columns, vectors, matrix, *outs):
    size = outs[0].shape[1]
    values = vectors[...]
    high, low = halves(values)
    turned_high, turned_low = halves(turned_rows(values))
    highs = jnp.concatenate([high, turned_high], axis=1)
    both = jnp.concatenate([highs, jnp.concatenate([low, turned_low], axis=1)], axis=0)
    for piece, out in enumerate(outs):
        here = pl.ds(pl.multiple_of(columns[piece], size), size)
        real_high, real_low = halves(matrix[0, :, here])
        imag_high, imag_low = halves(matrix[1, :, here])
        wide = dot32(both, jnp.concatenate([real_high, imag_high], axis=0))
        thin = dot32(highs, jnp.concatenate([real_low, imag_low], axis=0))
        out[...] = wide[:BLOCK] + wide[BLOCK:] + thin


def spread(matrix, vectors, columns, size):
    pieces, depth, width = columns.shape[0], matrix.shape[1], vectors.shape[0]
    if depth % BLOCK or width != BLOCK or size % BLOCK:
        dot = functools.partial(jnp.dot, precision=exact_precision)
        whole = dot(vectors, matrix[0]) + dot(turned_rows(vectors), matrix[1])
        return [
            lax.dynamic_slice(whole, (0, columns[piece]), (width, size)) for piece in range(pieces)
        ]
    return call(
        spread_kernel,
        [columns],
        [vectors],
        matrix,
        [jax.ShapeDtypeStruct((BLOCK, size), jnp.float32)] * pieces,
        [],
        2 * 3 * pieces * depth * size * 2 * BLOCK,
    )


def move(value, route):
    groups, fronts = lax.axis_size("leaf"), lax.axis_size("front")
    pairs = []
    for leaf in range(groups):
        for front in range(fronts):
            to_leaf, to_front = route(leaf, front)
            pairs.append((leaf * fronts + front, to_leaf * fronts + to_front % fronts))
    return lax.ppermute(value, ("leaf", "front"), pairs)


def along(value, apart):
    return move(value, lambda leaf, front: (leaf, front ^ 2 * apart))


def across(value):
    return move(value, lambda leaf, front: (leaf, front ^ 1))


def sibling(value):
    return move(value, lambda leaf, front: (leaf ^ 1, front))


def opposite(value):
    return move(value, lambda leaf, front: (leaf ^ 2, front))


def first_way(leaf, front):
    return (leaf ^ 2, front) if leaf % 2 else (leaf, front ^ 1)


def second_way(leaf, front):
    return (leaf, front ^ 1) if leaf % 2 else (leaf ^ 2, front)


def chain_places():
    return list(range(lax.axis_size("front") // 2))


def spread_chain(own):
    held, count = {0: own}, lax.axis_size("front") // 2
    apart = count // 2
    while apart:
        held.update({place | apart: along(value, apart) for place, value in held.items()})
        apart //= 2
    return held


def sum_chain(held):
    held, apart = dict(held), 1
    while apart < len(held):
        for place in range(apart, len(held), 2 * apart):
            held[place - apart] = held[place - apart] + along(held[place], apart)
        apart *= 2
    return held[0]


def gather_front(own):
    held = spread_chain(own)
    return [chunk for place in chain_places() for chunk in (held[place], across(held[place]))]


def front_sources(front):
    return front ^ jnp.arange(lax.axis_size("front"), dtype=jnp.int32)


def front_targets(front):
    return front ^ jnp.arange(lax.axis_size("front"), dtype=jnp.int32)[::-1]


def scatter_front(pieces):
    count = len(pieces) // 2
    given, kept = pieces[0::2], pieces[1::2]
    return sum_chain({count - 1 - i: kept[i] + across(given[i]) for i in range(count)})


def body(
    leaf_source,
    mid_source,
    root_source,
    leaf_inverse,
    leaf_coupling,
    mid_inverse,
    mid_coupling,
    root_inverse,
    leaf_blocks,
    mid_blocks,
):
    fronts = lax.axis_size("front")
    rounds = fronts // 2
    group, front = lax.axis_index("leaf"), lax.axis_index("front")
    side = group % 2
    source_two, source_one = leaf_source[0], mid_source[0]
    inverse_two, coupling_two = leaf_inverse[0], leaf_coupling[0]
    inverse_one, coupling_one = mid_inverse[0], mid_coupling[0]
    rows_two = source_two.shape[0]
    half = source_one.shape[0]
    block_rows = 2 * half
    root_block = root_source.shape[0]
    quarter = root_block // lax.axis_size("leaf")
    root_rows = root_inverse.shape[1]

    def backwards(order):
        count = order.shape[0]
        numbers = jnp.arange(count, dtype=jnp.int32)
        hits = order[None, :] == numbers[:, None]
        return jnp.sum(jnp.where(hits, numbers[None, :], 0), axis=1, dtype=jnp.int32)

    child_two = backwards(leaf_blocks[0])
    child_one = backwards(lax.dynamic_index_in_dim(mid_blocks, group // 2, 0, keepdims=False))

    def unit_rows(parent_rows, rows, child):
        unit = min(BLOCK, rows)
        units = (
            parent_rows[:, None] + unit * jnp.arange(rows // unit, dtype=jnp.int32)[None, :]
        ).reshape(-1)
        return child[units // BLOCK] * BLOCK + units % BLOCK, unit

    sources = front_sources(front)
    targets = front_targets(front)
    nothing = jnp.zeros((1,), jnp.int32)

    solved_two = fold(inverse_two, gather_front(source_two), sources * rows_two)

    lift_rows = jnp.concatenate(
        [targets * block_rows + (1 - side) * half, targets * block_rows + side * half]
    )
    starts, unit = unit_rows(lift_rows, half, child_two)
    lifted = lift(coupling_two, [solved_two], nothing, starts, unit, half, [2] * (2 * rounds))
    pieces = []
    for step in range(rounds):
        met = lifted[rounds + step] + sibling(lifted[step])
        pieces += [met[0], met[1]]
    own_half = source_one - scatter_front(pieces)

    halves_of = jnp.stack([side * half, (1 - side) * half])
    parts = lift(
        inverse_one,
        [own_half, sibling(own_half)],
        halves_of,
        targets * half,
        half,
        half,
        [1] * fronts,
    )
    solved_one = scatter_front([part[0] for part in parts])

    def quarter_rows(leaf, front_ids):
        core = leaf % 2
        beside = front_ids ^ 1
        over = leaf ^ 2
        first = jnp.where(core == 0, beside * root_block + leaf * quarter, front_ids * root_block + over * quarter)
        second = jnp.where(core == 0, front_ids * root_block + over * quarter, beside * root_block + leaf * quarter)
        return jnp.stack(
            [front_ids * root_block + leaf * quarter, first, second, beside * root_block + over * quarter],
            axis=1,
        ).reshape(-1)

    ring_targets = targets[1::2]
    lift_rows = jnp.concatenate(
        [quarter_rows(group ^ 1, ring_targets), quarter_rows(group, ring_targets)]
    )
    starts, unit = unit_rows(lift_rows, quarter, child_one)
    lifted = lift(coupling_one, [solved_one], nothing, starts, unit, quarter, [4] * (2 * rounds))
    held = {}
    for step in range(rounds):
        mine, theirs = lifted[rounds + step], sibling(lifted[step])
        far = move(mine[3] + theirs[3], second_way)
        first = move(mine[1] + theirs[1] + far, first_way)
        second = move(mine[2] + theirs[2], second_way)
        held[rounds - 1 - step] = mine[0] + theirs[0] + first + second
    own_source = lax.dynamic_slice_in_dim(root_source, group * quarter, quarter, 0)
    own_quarter = own_source - sum_chain(held)
    over_quarter = opposite(own_quarter)
    quarters = [own_quarter, over_quarter, sibling(own_quarter), sibling(over_quarter)]
    leaves_of = jnp.stack([group, group ^ 2, group ^ 1, group ^ 3])

    parts = lift(
        root_inverse,
        quarters,
        leaves_of * quarter,
        targets * (root_rows // fronts),
        root_rows // fronts,
        root_rows // fronts,
        [1] * fronts,
    )
    whole_piece = scatter_front([part[0] for part in parts])
    root_chunks = gather_front(whole_piece.T)
    theirs_own, theirs_over, mine_own, mine_over = pull(
        root_inverse,
        root_chunks,
        sources * (root_rows // fronts),
        root_rows // fronts,
        jnp.stack([group ^ 1, group ^ 3, group, group ^ 2]) * quarter,
        quarter,
    )
    own = mine_own + sibling(theirs_own)
    over = mine_over + sibling(theirs_over)
    own_quarter = own + opposite(over)

    held, mine = spread_chain(own_quarter), []
    for place in chain_places():
        first = move(held[place], first_way)
        second = move(held[place], second_way)
        mine += [held[place], first, second, move(first, second_way)]
    theirs = [sibling(chunk) for chunk in mine]
    beside_core = side == 0
    quarters = jnp.stack(
        [
            mine[0],
            theirs[0],
            jnp.where(beside_core, mine[2], mine[1]),
            jnp.where(beside_core, theirs[1], theirs[2]),
        ]
    )
    natural = jnp.take(quarters, jnp.arange(4, dtype=jnp.int32) ^ group, axis=0)
    root_solution = jnp.transpose(natural, (0, 2, 1)).reshape(root_block, natural.shape[1])

    ring_sources = sources[0::2]
    pull_rows = jnp.concatenate(
        [quarter_rows(group, ring_sources), quarter_rows(group ^ 1, ring_sources)]
    )
    starts, unit = unit_rows(pull_rows, quarter, child_one)
    pulled_one = pull(coupling_one, mine + theirs, starts, unit, nothing, coupling_one.shape[2])[0]
    rest_one = solved_one.T - pulled_one
    theirs, mine = pull(
        inverse_one,
        gather_front(rest_one),
        sources * half,
        half,
        jnp.stack([1 - side, side]) * half,
        half,
    )
    mid_columns = mine + sibling(theirs)
    mid_solution = mid_columns.T

    mine = gather_front(mid_columns)
    theirs = [sibling(chunk) for chunk in mine]
    pull_rows = jnp.concatenate(
        [sources * block_rows + side * half, sources * block_rows + (1 - side) * half]
    )
    starts, unit = unit_rows(pull_rows, half, child_two)
    pulled_two = pull(coupling_two, mine + theirs, starts, unit, nothing, rows_two)[0]
    rest_two = solved_two.T - pulled_two
    parts = spread(inverse_two, rest_two, targets * rows_two, rows_two)
    leaf_solution = scatter_front(parts).T
    return (leaf_solution[None], mid_solution[None], root_solution)


def solution(mesh):
    placed = (
        P("leaf", "front", None),
        P("leaf", "front", None),
        P("front", None),
        P("leaf", None, "front", None),
        P("leaf", None, None, "front"),
        P("leaf", None, None, "front"),
        P("leaf", None, None, "front"),
        P(None, "leaf", "front"),
        P("leaf", None),
        P(),
    )
    return jax.shard_map(
        body,
        mesh=mesh,
        in_specs=placed,
        out_specs=(P("leaf", "front", None), P("leaf", "front", None), P("front", None)),
        check_vma=False,
    )
```

```python
import functools
import math

import jax
import jax.numpy as jnp
from jax import lax
from jax.experimental import pallas as pl
from jax.experimental.pallas import tpu as pltpu
from jax.sharding import PartitionSpec as P

BLOCK = 128
VMEM = pltpu.VMEM
exact_dot = functools.partial(jnp.dot, precision=lax.Precision.HIGHEST)


def halves(values):
    high = values.astype(jnp.bfloat16)
    low = (values - high.astype(jnp.float32)).astype(jnp.bfloat16)
    return high, low


def turned_columns(vectors):
    width = vectors.shape[1] // 2
    return jnp.concatenate([-vectors[:, width:], vectors[:, :width]], axis=1)


def turned_rows(vectors):
    width = vectors.shape[0] // 2
    return jnp.concatenate([-vectors[width:], vectors[:width]], axis=0)


def dot32(left, right):
    return jnp.dot(left, right, preferred_element_type=jnp.float32)


def fast(*extents):
    return all(extent % BLOCK == 0 for extent in extents)


def call(kernel, operands, outs, scratch=(), flops=0):
    arrays, spaces = zip(*operands)
    size = lambda a: math.prod(a.shape) * a.dtype.itemsize
    held = sum(size(a) for a, space in operands if space == VMEM) + sum(size(o) for o in outs)
    scratch_bytes = sum(size(s) for s in scratch if hasattr(s, "shape") and s.memory_space == VMEM)
    moved = held if any(space == VMEM for space in spaces) else 2 * held
    return pl.pallas_call(
        kernel,
        out_shape=outs,
        in_specs=[pl.BlockSpec(memory_space=space) for space in spaces],
        out_specs=[pl.BlockSpec(memory_space=VMEM)] * len(outs),
        scratch_shapes=scratch,
        compiler_params=pltpu.CompilerParams(
            vmem_limit_bytes=held + scratch_bytes + 6 * 1024 * 1024
        ),
        cost_estimate=pl.CostEstimate(flops=flops, bytes_accessed=moved, transcendentals=0),
    )(*arrays)


class Place:
    def __init__(self, ids, child):
        self.ids, self.child = ids, child

    def starts(self, start_of, chunks, rows):
        group, front = self.ids[0], self.ids[1]
        unit = rows if self.child is None else min(BLOCK, rows)
        for chunk in chunks:
            start = start_of(group, front, *chunk)
            for inner in range(0, rows, unit):
                row = start + inner
                if self.child is not None:
                    row = self.child[row // BLOCK] * BLOCK + row % BLOCK
                yield row


def hold_kernel(start_of, chunks, rows, unit, with_child, ids, *refs):
    child = refs[0] if with_child else None
    _, matrix, out, slots, sems = refs[with_child:]
    copies = []
    for index, row in enumerate(Place(ids, child).starts(start_of, chunks, rows)):
        copy = pltpu.make_async_copy(
            matrix.at[:, pl.ds(pl.multiple_of(row, unit), unit), :],
            slots.at[index],
            sems.at[index],
        )
        copy.start()
        copies.append(copy)
    for index, copy in enumerate(copies):
        copy.wait()
        here = slice(index * unit, (index + 1) * unit)
        for part in (0, 1):
            out[part, here], out[2 + part, here] = halves(slots[index, part])


def hold(matrix, ids, child, start_of, chunks, rows, token):
    columns, count = matrix.shape[2], len(chunks) * rows
    unit = rows if child is None else min(BLOCK, rows)
    if not fast(rows, columns):
        starts = jnp.stack(list(Place(ids, child).starts(start_of, chunks, rows)))
        picked = (starts[:, None] + jnp.arange(unit, dtype=jnp.int32)).reshape(-1)
        return jnp.take(matrix, picked, axis=1)
    orders = [(ids, pltpu.SMEM)] + ([] if child is None else [(child, pltpu.SMEM)])
    return call(
        functools.partial(hold_kernel, start_of, chunks, rows, unit, child is not None),
        [*orders, (token, pl.ANY), (pltpu.with_memory_space_constraint(matrix, pltpu.HBM), pl.ANY)],
        [jax.ShapeDtypeStruct((4, count, columns), jnp.bfloat16)],
        [
            VMEM((count // unit, 2, unit, columns), jnp.float32),
            pltpu.SemaphoreType.DMA((count // unit,)),
        ],
    )[0]


def lift_kernel(start_of, parts, rows, counts, turned, ids, *refs):
    chunk_refs, (held, *rest) = refs[: len(parts)], refs[len(parts) :]
    outs, (natural, weights) = rest[: len(counts)], rest[len(counts) :]
    depth = natural.shape[0]
    step = chunk_refs[0].shape[0]
    for part, chunk in zip(parts, chunk_refs):
        place = pl.multiple_of(start_of(ids[0], *part), step)
        natural[pl.ds(place, step), :] = chunk[...]
    for half, values in enumerate((natural[...], turned_columns(natural[...]))):
        high, low = halves(values)
        both = jnp.concatenate([high, low], axis=1)
        weights[half * depth : (half + 1) * depth, :] = both
        weights[(half + 2) * depth : (half + 3) * depth, :] = both
    done = 0
    for out, count in zip(outs, counts):
        for index in range(count):
            here = slice((done + index) * rows, (done + index + 1) * rows)
            tile = jnp.concatenate([held[part, here] for part in range(4)], axis=1)
            wide = dot32(tile, weights[...])
            whole = wide[:, :BLOCK] + wide[:, BLOCK:]
            out[index] = whole.T if turned else whole
        done += count


def lift(held, ids, vectors, start_of, parts, rows, counts, turned=False):
    depth, width = held.shape[2], vectors[0].shape[1]
    if held.dtype != jnp.bfloat16:
        whole = jnp.zeros((depth, width), jnp.float32)
        for part, chunk in zip(parts, vectors):
            whole = lax.dynamic_update_slice(whole, chunk, (start_of(ids[0], *part), 0))
        result = exact_dot(held[0], whole) + exact_dot(held[1], turned_columns(whole))
        result = result.reshape(-1, rows, width)
        result = jnp.transpose(result, (0, 2, 1)) if turned else result
        ends = [sum(counts[: i + 1]) for i in range(len(counts))]
        return [result[end - count : end] for end, count in zip(ends, counts)]
    shape = (width, rows) if turned else (rows, width)
    return call(
        functools.partial(lift_kernel, start_of, parts, rows, counts, turned),
        [(ids, pltpu.SMEM), *((chunk, VMEM) for chunk in vectors), (held, VMEM)],
        [jax.ShapeDtypeStruct((count, *shape), jnp.float32) for count in counts],
        [VMEM((depth, BLOCK), jnp.float32), VMEM((4 * depth, 2 * BLOCK), jnp.bfloat16)],
        2 * 4 * sum(counts) * rows * depth * 2 * BLOCK,
    )


def fold_kernel(start_of, chunks, has_total, turned, ids, *refs):
    chunk_refs, (held, *rest) = refs[: len(chunks)], refs[len(chunks) :]
    outs = rest[-2:] if turned else rest[-1:]
    total = rest[0][...] if has_total else None
    depth = chunk_refs[0].shape[0]
    for chunk, chunk_ref in zip(chunks, chunk_refs):
        values = chunk_ref[...]
        high, low = halves(values)
        turned_high, turned_low = halves(turned_columns(values))
        both = jnp.concatenate(
            [
                jnp.concatenate([high, low], axis=1),
                jnp.concatenate([turned_high, turned_low], axis=1),
            ],
            axis=0,
        )
        here = pl.ds(pl.multiple_of(start_of(ids[0], ids[1], *chunk), depth), depth)
        tile = jnp.concatenate([held[part, :, here] for part in range(4)], axis=1)
        wide = dot32(tile, jnp.concatenate([both, both], axis=0))
        term = wide[:, :BLOCK] + wide[:, BLOCK:]
        total = term if total is None else total + term
    outs[0][...] = total
    if turned:
        outs[1][...] = total.T


def fold(held, ids, vectors, start_of, chunks, total, tokens=(), turned=False):
    rows, (depth, width) = held.shape[1], vectors[0].shape
    if held.dtype != jnp.bfloat16:
        for chunk, values in zip(chunks, vectors):
            column = start_of(ids[0], ids[1], *chunk)
            taken = lax.dynamic_slice(held, (0, 0, column), (2, rows, depth))
            term = exact_dot(taken[0], values) + exact_dot(taken[1], turned_columns(values))
            total = term if total is None else total + term
        return (total, total.T) if turned else total
    before = [] if total is None else [(total, VMEM)]
    shapes = [(rows, width), (width, rows)] if turned else [(rows, width)]
    outs = call(
        functools.partial(fold_kernel, start_of, chunks, total is not None, turned),
        [
            (ids, pltpu.SMEM),
            *((chunk, VMEM) for chunk in vectors),
            (held, VMEM),
            *before,
            *((token, pl.ANY) for token in tokens),
        ],
        [jax.ShapeDtypeStruct(shape, jnp.float32) for shape in shapes],
        [],
        2 * 4 * len(chunks) * rows * depth * 2 * BLOCK,
    )
    return outs if turned else outs[0]


def pull_kernel(count, has_total, minus, start_of, pieces, ids, *refs):
    chunk_refs, (held, *rest) = refs[:count], refs[count:]
    outs, total = rest[-1 - max(1, len(pieces)) : -1], rest[-1]
    depth, columns = chunk_refs[0].shape[1], held.shape[2]
    lefts = []
    for chunk in chunk_refs:
        values = chunk[...]
        high, low = halves(values)
        turned_high, turned_low = halves(turned_rows(values))
        lefts.append((jnp.concatenate([high, low], axis=0), jnp.concatenate([turned_high, turned_low], axis=0)))
    left = [jnp.concatenate(side, axis=1) for side in zip(*lefts)]
    for at in range(0, columns, 256):
        here = slice(at, min(at + 256, columns))
        term = rest[0][:, here] if has_total else None
        for side, part in ((0, 0), (1, 1)):
            wide = dot32(left[side], held[part, :, here])
            thin = dot32(left[side][:BLOCK], held[2 + part, :, here])
            both = wide[:BLOCK] + wide[BLOCK:] + thin
            term = both if term is None else term - both if minus else term + both
        total[:, here] = term
    if not pieces:
        outs[0][...] = total[...]
    for piece, out in zip(pieces, outs):
        place = pl.multiple_of(start_of(ids[0], *piece), out.shape[1])
        out[...] = total[:, pl.ds(place, out.shape[1])]


def pull(held, ids, vectors, total, start_of=None, pieces=(), size=0, minus=False, tokens=()):
    columns, (width, depth) = held.shape[2], vectors[0].shape
    if held.dtype != jnp.bfloat16:
        values = jnp.concatenate(vectors, axis=1)
        term = exact_dot(values, held[0]) + exact_dot(turned_rows(values), held[1])
        total = term if total is None else total - term if minus else total + term
        if not pieces:
            return total
        return [
            lax.dynamic_slice(total, (0, start_of(ids[0], *piece)), (width, size))
            for piece in pieces
        ]
    before = [] if total is None else [(total, VMEM)]
    shapes = [(width, size)] * len(pieces) if pieces else [(width, columns)]
    outs = call(
        functools.partial(pull_kernel, len(vectors), total is not None, minus, start_of, pieces),
        [
            (ids, pltpu.SMEM),
            *((chunk, VMEM) for chunk in vectors),
            (held, VMEM),
            *before,
            *((token, pl.ANY) for token in tokens),
        ],
        [jax.ShapeDtypeStruct(shape, jnp.float32) for shape in shapes],
        [VMEM((width, columns), jnp.float32)],
        2 * 3 * len(vectors) * depth * columns * 2 * BLOCK,
    )
    return outs if pieces else outs[0]


def spread_kernel(start_of, chunks, ids, vectors, held, *outs):
    size = outs[0].shape[0]
    values = vectors[...]
    high, low = halves(values)
    turned_high, turned_low = halves(turned_rows(values))
    left = (jnp.concatenate([high, low], axis=0), jnp.concatenate([turned_high, turned_low], axis=0))
    for chunk, out in zip(chunks, outs):
        here = pl.ds(pl.multiple_of(start_of(ids[0], ids[1], *chunk), size), size)
        term = None
        for part in (0, 1):
            wide = dot32(left[part], held[part, :, here])
            thin = dot32(left[part][:BLOCK], held[2 + part, :, here])
            both = wide[:BLOCK] + wide[BLOCK:] + thin
            term = both if term is None else term + both
        out[...] = term.T


def spread(held, ids, vectors, start_of, chunks, size):
    width, depth = vectors.shape
    if held.dtype != jnp.bfloat16 or not fast(size):
        whole = exact_dot(vectors, held[0]) + exact_dot(turned_rows(vectors), held[1])
        return [
            lax.dynamic_slice(whole, (0, start_of(ids[0], ids[1], *chunk)), (width, size)).T
            for chunk in chunks
        ]
    return call(
        functools.partial(spread_kernel, start_of, chunks),
        [(ids, pltpu.SMEM), (vectors, VMEM), (held, VMEM)],
        [jax.ShapeDtypeStruct((size, width), jnp.float32)] * len(chunks),
        [],
        2 * 3 * len(chunks) * depth * size * 2 * BLOCK,
    )


def add_kernel(indices, has_base, turned, *refs):
    outs = refs[-2:] if turned else refs[-1:]
    total = None
    for index, ref in zip(indices, refs[has_base:]):
        term = ref[...] if index is None else ref[index]
        total = term if total is None else total + term
    total = refs[0][...] - total if has_base else total
    outs[0][...] = total
    if turned:
        outs[1][...] = total.T


def add(terms, base=None, tokens=(), turned=False):
    arrays, indices = zip(*terms)
    shape = base.shape if base is not None else arrays[0].shape[-2:]
    if not fast(*shape):
        total = sum(array if index is None else array[index] for array, index in terms)
        total = total if base is None else base - total
        return (total, total.T) if turned else total
    bases = [] if base is None else [base]
    shapes = [shape, shape[::-1]] if turned else [shape]
    outs = call(
        functools.partial(add_kernel, indices, len(bases), turned),
        [*((array, VMEM) for array in (*bases, *arrays)), *((token, pl.ANY) for token in tokens)],
        [jax.ShapeDtypeStruct(extent, jnp.float32) for extent in shapes],
    )
    return outs if turned else outs[0]


def settle_kernel(ids, *refs):
    out = refs[-1]
    for leaf, chunk in enumerate(refs[:-1]):
        rows = chunk.shape[1]
        place = pl.multiple_of((ids[0] ^ leaf) * rows, rows)
        out[pl.ds(place, rows), :] = chunk[...].T


def settle(ids, chunks):
    width, rows = chunks[0].shape
    if not fast(width, rows):
        natural = jnp.take(jnp.stack(chunks), jnp.arange(len(chunks), dtype=jnp.int32) ^ ids[0], axis=0)
        return jnp.transpose(natural, (0, 2, 1)).reshape(-1, width)
    return call(
        settle_kernel,
        [(ids, pltpu.SMEM), *((chunk, VMEM) for chunk in chunks)],
        [jax.ShapeDtypeStruct((len(chunks) * rows, width), jnp.float32)],
    )[0]


def swap(value, leaf_bits, front_bits):
    groups, fronts = lax.axis_size("leaf"), lax.axis_size("front")
    pairs = [
        (leaf * fronts + front, (leaf ^ leaf_bits) * fronts + (front ^ front_bits))
        for leaf in range(groups)
        for front in range(fronts)
    ]
    return lax.ppermute(value, ("leaf", "front"), pairs)


def across(value):
    return swap(value, 0, 1)


def along(value, apart):
    return swap(value, 0, 2 * apart)


def sibling(value):
    return swap(value, 1, 0)


def opposite(value):
    return swap(value, 2, 0)


def spread_chain(own):
    held, count = {0: own}, lax.axis_size("front") // 2
    apart = count // 2
    while apart:
        held.update({place | apart: along(value, apart) for place, value in held.items()})
        apart //= 2
    return held


def sum_chain(terms, tokens, **last):
    terms, apart = {place: list(held) for place, held in terms.items()}, 1
    while apart < len(terms):
        for place in reversed(range(apart, len(terms), 2 * apart)):
            summed = add(terms[place], tokens=tokens.get(place, ()))
            terms[place - apart].append((along(summed, apart), None))
        apart *= 2
    return add(terms[0], tokens=tokens.get(0, ()), **last)


def ways(place):
    return ((across, opposite), (1, 0), (0, 2)) if place % 2 else ((opposite, across), (0, 2), (1, 0))


def body(
    leaf_source,
    mid_source,
    root_source,
    leaf_inverse,
    leaf_coupling,
    mid_inverse,
    mid_coupling,
    root_inverse,
    leaf_blocks,
    mid_blocks,
):
    fronts = lax.axis_size("front")
    places = list(range(fronts // 2))
    downward = places[::-1]
    group, front = lax.axis_index("leaf"), lax.axis_index("front")
    ids = jnp.stack([group, front]).astype(jnp.int32)
    side = group % 2
    source_two, source_one = leaf_source[0], mid_source[0]
    inverse_two, coupling_two = leaf_inverse[0], leaf_coupling[0]
    inverse_one, coupling_one = mid_inverse[0], mid_coupling[0]
    rows_two = source_two.shape[0]
    half = source_one.shape[0]
    root_block = root_source.shape[0]
    quarter = root_block // lax.axis_size("leaf")
    root_rows = root_inverse.shape[1] // fronts

    def backwards(order):
        numbers = jnp.arange(order.shape[0], dtype=jnp.int32)
        hits = order[None, :] == numbers[:, None]
        return jnp.sum(jnp.where(hits, numbers[None, :], 0), axis=1, dtype=jnp.int32)

    child_two = backwards(leaf_blocks[0])
    child_one = backwards(lax.dynamic_index_in_dim(mid_blocks, group // 2, 0, keepdims=False))

    def two_start(group, front, leaf_bits, front_bits):
        return (front ^ front_bits) * rows_two

    def half_start(group, front, leaf_bits, front_bits):
        return (front ^ front_bits) * (2 * half) + ((group ^ leaf_bits) % 2) * half

    def one_start(group, front, leaf_bits, front_bits):
        return (front ^ front_bits) * half

    def quarter_start(group, front, leaf_bits, front_bits):
        return (front ^ front_bits) * root_block + (group ^ leaf_bits) * quarter

    def root_start(group, front, leaf_bits, front_bits):
        return (front ^ front_bits) * root_rows

    def whole_start(group, front):
        return 0

    def first_row(group):
        return 0

    def side_row(group, bits):
        return ((group ^ bits) % 2) * half

    def leaf_row(group, bits):
        return (group ^ bits) * quarter

    pair = lambda place: [(0, 2 * place + 1), (0, 2 * place)]
    pair_both = lambda place: [(1, front_bits) for _, front_bits in pair(place)] + pair(place)

    def square(place):
        _, first, second = ways(place)
        return [
            (first[1] | second[1], 2 * place + (first[0] | second[0])),
            (first[1], 2 * place + first[0]),
            (second[1], 2 * place + second[0]),
            (0, 2 * place),
        ]

    square_both = lambda place: [(bits ^ 1, other) for bits, other in square(place)] + square(place)

    def share(held):
        early, late = downward[: len(places) // 2], downward[len(places) // 2 :]
        return {
            len(places) // 2: [held[place] for place in early],
            0: [held[place] for place in late],
        }

    def later(held, place):
        return [held[at] for at in places if (at // 2 + 1) == place]

    held_inverse = hold(inverse_two, ids, None, whole_start, [()], inverse_two.shape[1], source_two)
    chain = spread_chain(source_two)
    held_two = {
        place: hold(coupling_two, ids, child_two, half_start, pair_both(place), half, source_two)
        for place in downward
    }
    total = None
    for place in places:
        vectors = [across(chain[place]), chain[place]]
        last = place == places[-1]
        tokens = later(held_two, place)
        total = fold(held_inverse, ids, vectors, two_start, pair(place), total, tokens, last)
    solved_two, solved_two_turned = total

    held_one = {
        place: hold(inverse_one, ids, None, one_start, pair(place), half, solved_two)
        for place in downward
    }
    sums = {}
    for place in downward:
        theirs, mine = lift(held_two[place], ids, [solved_two], first_row, [()], half, [2, 2])
        theirs = sibling(theirs)
        given = add([(mine, 0), (theirs, 0)])
        sums[place] = [(mine, 1), (theirs, 1), (across(given), None)]
    own_half = sum_chain(sums, share(held_one), base=source_one)

    halves_one = [own_half, sibling(own_half)]
    sums, token = {}, None
    for place in downward:
        given, kept = lift(held_one[place], ids, halves_one, side_row, [(0,), (1,)], half, [1, 1])
        sums[place] = [(kept, 0), (across(given[0]), None)]
        token = kept if token is None else token
    held_one = {
        place: hold(coupling_one, ids, child_one, quarter_start, square_both(place), quarter, token)
        for place in downward
    }
    solved_one, solved_one_turned = sum_chain(sums, share(held_one), turned=True)

    sums, token = {}, None
    for place in downward:
        (first_way, second_way), _, _ = ways(place)
        theirs, mine = lift(held_one[place], ids, [solved_one], first_row, [()], quarter, [4, 4])
        theirs = sibling(theirs)
        outer = first_way(mine[:2] + theirs[:2])
        inner = second_way(add([(mine, 2), (theirs, 2), (outer, 0)]))
        sums[place] = [(mine, 3), (theirs, 3), (outer, 1), (inner, None)]
        token = mine if token is None else token
    held_root = {
        place: hold(root_inverse, ids, None, root_start, pair(place), root_rows, token)
        for place in downward
    }
    own_source = lax.dynamic_slice_in_dim(root_source, group * quarter, quarter, 0)
    own_quarter = sum_chain(sums, share(held_root), base=own_source)
    over_quarter = opposite(own_quarter)
    quarters = [own_quarter, over_quarter, sibling(own_quarter), sibling(over_quarter)]

    sums, parts = {}, [(0,), (2,), (1,), (3,)]
    for place in downward:
        given, kept = lift(
            held_root[place], ids, quarters, leaf_row, parts, root_rows, [1, 1], True
        )
        sums[place] = [(kept, 0), (across(given[0]), None)]
    whole_root = sum_chain(sums, {})
    held_one = {
        place: hold(coupling_one, ids, child_one, quarter_start, square_both(place), quarter, whole_root)
        for place in places
    }
    chain = spread_chain(whole_root)
    total = None
    for place in places:
        vectors = [across(chain[place]), chain[place]]
        pieces = [(1,), (3,), (0,), (2,)] if place == places[-1] else ()
        tokens = later(held_one, place)
        total = pull(
            held_root[place], ids, vectors, total, leaf_row, pieces, quarter, tokens=tokens
        )
    theirs_own, theirs_over, mine_own, mine_over = total
    over = add([(mine_over, None), (sibling(theirs_over), None)])
    theirs_own = sibling(theirs_own)
    own_quarter = add([(mine_own, None), (theirs_own, None), (opposite(over), None)])

    held_inner = {
        place: hold(inverse_one, ids, None, one_start, pair(place), half, mine_own)
        for place in places
    }
    chain = spread_chain(own_quarter)
    rest_one = solved_one_turned
    for place in places:
        (first_way, second_way), _, _ = ways(place)
        first, second = first_way(chain[place]), second_way(chain[place])
        mine = [second_way(first), first, second, chain[place]]
        theirs = [sibling(chunk) for chunk in mine]
        if place == 0:
            over, their_over = (first, theirs[1]) if ways(place)[1][1] else (second, theirs[2])
            root_solution = settle(ids, [mine[3], theirs[3], over, their_over])
        tokens = later(held_inner, place)
        rest_one = pull(held_one[place], ids, theirs + mine, rest_one, minus=True, tokens=tokens)
    held_two = {
        place: hold(coupling_two, ids, child_two, half_start, pair_both(place), half, rest_one)
        for place in places
    }
    chain = spread_chain(rest_one)
    total = None
    for place in places:
        vectors = [across(chain[place]), chain[place]]
        pieces = [(1,), (0,)] if place == places[-1] else ()
        tokens = later(held_two, place) if place else [root_solution]
        total = pull(held_inner[place], ids, vectors, total, side_row, pieces, half, tokens=tokens)
    theirs, mine = total
    mid_columns, mid_solution = add([(mine, None), (sibling(theirs), None)], turned=True)

    held_inverse = hold(inverse_two, ids, None, whole_start, [()], inverse_two.shape[1], mine)
    chain = spread_chain(mid_columns)
    rest_two = solved_two_turned
    for place in places:
        mine = [across(chain[place]), chain[place]]
        theirs = [sibling(chunk) for chunk in mine]
        tokens = [held_inverse] if place == 1 else []
        rest_two = pull(held_two[place], ids, theirs + mine, rest_two, minus=True, tokens=tokens)
    sums = {}
    for place in downward:
        given, kept = spread(held_inverse, ids, rest_two, two_start, pair(place), rows_two)
        sums[place] = [(kept, None), (across(given), None)]
    leaf_solution = sum_chain(sums, {})
    return (leaf_solution[None], mid_solution[None], root_solution)


def solution(mesh):
    placed = (
        P("leaf", "front", None),
        P("leaf", "front", None),
        P("front", None),
        P("leaf", None, "front", None),
        P("leaf", None, None, "front"),
        P("leaf", None, None, "front"),
        P("leaf", None, None, "front"),
        P(None, "leaf", "front"),
        P("leaf", None),
        P(),
    )
    return jax.shard_map(
        body,
        mesh=mesh,
        in_specs=placed,
        out_specs=(P("leaf", "front", None), P("leaf", "front", None), P("front", None)),
        check_vma=False,
    )
```

```python
import functools
import math

import jax
import jax.numpy as jnp
from jax import lax
from jax.experimental import pallas as pl
from jax.experimental.pallas import tpu as pltpu
from jax.sharding import PartitionSpec as P

BLOCK = 128
VMEM = pltpu.VMEM
exact_dot = functools.partial(jnp.dot, precision=lax.Precision.HIGHEST)


def halves(values):
    high = values.astype(jnp.bfloat16)
    low = (values - high.astype(jnp.float32)).astype(jnp.bfloat16)
    return high, low


def turned_columns(vectors):
    width = vectors.shape[1] // 2
    return jnp.concatenate([-vectors[:, width:], vectors[:, :width]], axis=1)


def turned_rows(vectors):
    width = vectors.shape[0] // 2
    return jnp.concatenate([-vectors[width:], vectors[:width]], axis=0)


def dot32(left, right):
    return jnp.dot(left, right, preferred_element_type=jnp.float32)


def fast(*extents):
    return all(extent % BLOCK == 0 for extent in extents)


def call(kernel, operands, outs, scratch=(), flops=0):
    arrays, spaces = zip(*operands)
    size = lambda a: math.prod(a.shape) * a.dtype.itemsize
    held = sum(size(a) for a, space in operands if space == VMEM) + sum(size(o) for o in outs)
    scratch_bytes = sum(size(s) for s in scratch if hasattr(s, "shape") and s.memory_space == VMEM)
    moved = held if any(space == VMEM for space in spaces) else 2 * held
    return pl.pallas_call(
        kernel,
        out_shape=outs,
        in_specs=[pl.BlockSpec(memory_space=space) for space in spaces],
        out_specs=[pl.BlockSpec(memory_space=VMEM)] * len(outs),
        scratch_shapes=scratch,
        compiler_params=pltpu.CompilerParams(
            vmem_limit_bytes=scratch_bytes + 10 * 1024 * 1024
        ),
        cost_estimate=pl.CostEstimate(flops=flops, bytes_accessed=moved, transcendentals=0),
    )(*arrays)


class Place:
    def __init__(self, ids, child):
        self.ids, self.child = ids, child

    def starts(self, start_of, chunks, rows):
        group, front = self.ids[0], self.ids[1]
        unit = rows if self.child is None else min(BLOCK, rows)
        for chunk in chunks:
            start = start_of(group, front, *chunk)
            for inner in range(0, rows, unit):
                row = start + inner
                if self.child is not None:
                    row = self.child[row // BLOCK] * BLOCK + row % BLOCK
                yield row


def fetch_kernel(start_of, chunks, rows, unit, with_child, ids, *refs):
    child = refs[0] if with_child else None
    matrix, out, sems = refs[-3:]
    copies = []
    for index, row in enumerate(Place(ids, child).starts(start_of, chunks, rows)):
        copy = pltpu.make_async_copy(
            matrix.at[:, pl.ds(pl.multiple_of(row, unit), unit), :],
            out.at[:, pl.ds(index * unit, unit), :],
            sems.at[index],
        )
        copy.start()
        copies.append(copy)
    for copy in copies:
        copy.wait()


def fetch(matrix, ids, child, start_of, chunks, rows, token):
    columns, count = matrix.shape[2], len(chunks) * rows
    unit = rows if child is None else min(BLOCK, rows)
    if not fast(rows, columns):
        starts = jnp.stack(list(Place(ids, child).starts(start_of, chunks, rows)))
        picked = (starts[:, None] + jnp.arange(unit, dtype=jnp.int32)).reshape(-1)
        return jnp.take(matrix, picked, axis=1)
    orders = [(ids, pltpu.SMEM)] + ([] if child is None else [(child, pltpu.SMEM)])
    pinned = pltpu.with_memory_space_constraint(matrix, pltpu.HBM)
    return call(
        functools.partial(fetch_kernel, start_of, chunks, rows, unit, child is not None),
        [*orders, (token, pl.ANY), (pinned, pl.ANY)],
        [jax.ShapeDtypeStruct((2, count, columns), jnp.float32)],
        [pltpu.SemaphoreType.DMA((count // unit,))],
    )[0]


def pass_kernel(*refs):
    del refs


def after(value, tokens):
    if not tokens or not fast(*value.shape[-2:]):
        return value
    return pl.pallas_call(
        pass_kernel,
        out_shape=jax.ShapeDtypeStruct(value.shape, value.dtype),
        in_specs=[pl.BlockSpec(memory_space=pl.ANY)] * (1 + len(tokens)),
        out_specs=pl.BlockSpec(memory_space=pl.ANY),
        input_output_aliases={0: 0},
        cost_estimate=pl.CostEstimate(flops=0, bytes_accessed=1024, transcendentals=0),
    )(value, *tokens)


def wide_of(real, imag):
    real_high, real_low = halves(real)
    imag_high, imag_low = halves(imag)
    return jnp.concatenate([real_high, imag_high, real_low, imag_low], axis=1)


def lift_kernel(start_of, parts, rows, begin, counts, turned, ids, *refs):
    chunk_refs, (held, *rest) = refs[: len(parts)], refs[len(parts) :]
    outs, (natural, weights) = rest[-2 - len(counts) : -2], rest[-2:]
    depth = natural.shape[0]
    step = chunk_refs[0].shape[0]
    for part, chunk in zip(parts, chunk_refs):
        place = pl.multiple_of(start_of(ids[0], *part), step)
        natural[pl.ds(place, step), :] = chunk[...]
    for half, values in enumerate((natural[...], turned_columns(natural[...]))):
        high, low = halves(values)
        both = jnp.concatenate([high, low], axis=1)
        weights[half * depth : (half + 1) * depth, :] = both
        weights[(half + 2) * depth : (half + 3) * depth, :] = both
    for out, count in zip(outs, counts):
        together = 1 if turned or count % 2 else 2
        for index in range(0, count, together):
            here = slice((begin + index) * rows, (begin + index + together) * rows)
            wide = dot32(wide_of(held[0, here], held[1, here]), weights[...])
            whole = wide[:, :BLOCK] + wide[:, BLOCK:]
            if turned:
                out[index] = whole.T
            else:
                out[index : index + together] = whole.reshape(together, rows, BLOCK)
        begin += count


def lift(held, ids, vectors, start_of, parts, rows, begin, counts, turned=False):
    depth, width = held.shape[2], vectors[0].shape[1]
    if not fast(rows, depth, vectors[0].shape[0]):
        whole = jnp.zeros((depth, width), jnp.float32)
        for part, chunk in zip(parts, vectors):
            whole = lax.dynamic_update_slice(whole, chunk, (start_of(ids[0], *part), 0))
        held = held[:, begin * rows : (begin + sum(counts)) * rows]
        result = exact_dot(held[0], whole) + exact_dot(held[1], turned_columns(whole))
        result = result.reshape(-1, rows, width)
        result = jnp.transpose(result, (0, 2, 1)) if turned else result
        ends = [sum(counts[: i + 1]) for i in range(len(counts))]
        return [result[end - count : end] for end, count in zip(ends, counts)]
    shape = (width, rows) if turned else (rows, width)
    return call(
        functools.partial(lift_kernel, start_of, parts, rows, begin, counts, turned),
        [
            (ids, pltpu.SMEM),
            *((chunk, VMEM) for chunk in vectors),
            (held, VMEM),
        ],
        [jax.ShapeDtypeStruct((count, *shape), jnp.float32) for count in counts],
        [VMEM((depth, BLOCK), jnp.float32), VMEM((4 * depth, 2 * BLOCK), jnp.bfloat16)],
        2 * 4 * sum(counts) * rows * depth * 2 * BLOCK,
    )


def fold_kernel(start_of, chunks, has_total, turned, ids, *refs):
    chunk_refs, (held, *rest) = refs[: len(chunks)], refs[len(chunks) :]
    outs = rest[-2:] if turned else rest[-1:]
    total = rest[0][...] if has_total else None
    depth = chunk_refs[0].shape[0]
    for chunk, chunk_ref in zip(chunks, chunk_refs):
        values = chunk_ref[...]
        high, low = halves(values)
        turned_high, turned_low = halves(turned_columns(values))
        both = jnp.concatenate(
            [
                jnp.concatenate([high, low], axis=1),
                jnp.concatenate([turned_high, turned_low], axis=1),
            ],
            axis=0,
        )
        here = pl.ds(pl.multiple_of(start_of(ids[0], ids[1], *chunk), depth), depth)
        tile = wide_of(held[0, :, here], held[1, :, here])
        wide = dot32(tile, jnp.concatenate([both, both], axis=0))
        term = wide[:, :BLOCK] + wide[:, BLOCK:]
        total = term if total is None else total + term
    outs[0][...] = total
    if turned:
        outs[1][...] = total.T


def fold(held, ids, vectors, start_of, chunks, total, turned=False):
    rows, (depth, width) = held.shape[1], vectors[0].shape
    if not fast(rows, depth):
        for chunk, values in zip(chunks, vectors):
            column = start_of(ids[0], ids[1], *chunk)
            taken = lax.dynamic_slice(held, (0, 0, column), (2, rows, depth))
            term = exact_dot(taken[0], values) + exact_dot(taken[1], turned_columns(values))
            total = term if total is None else total + term
        return (total, total.T) if turned else total
    before = [] if total is None else [(total, VMEM)]
    shapes = [(rows, width), (width, rows)] if turned else [(rows, width)]
    outs = call(
        functools.partial(fold_kernel, start_of, chunks, total is not None, turned),
        [(ids, pltpu.SMEM), *((chunk, VMEM) for chunk in vectors), (held, VMEM), *before],
        [jax.ShapeDtypeStruct(shape, jnp.float32) for shape in shapes],
        [],
        2 * 4 * len(chunks) * rows * depth * 2 * BLOCK,
    )
    return outs if turned else outs[0]


def pull_kernel(begin, count, has_total, minus, start_of, pieces, ids, *refs):
    chunk_refs, (held, *rest) = refs[:count], refs[count:]
    outs, total = rest[has_total:-1], rest[-1]
    depth, columns = chunk_refs[0].shape[1], held.shape[2]
    lefts = []
    for chunk in chunk_refs:
        values = chunk[...]
        high, low = halves(values)
        turned_high, turned_low = halves(turned_rows(values))
        lefts.append(
            (
                jnp.concatenate([high, low], axis=0),
                jnp.concatenate([turned_high, turned_low], axis=0),
            )
        )
    left = [jnp.concatenate(side, axis=1) for side in zip(*lefts)]
    rows = slice(begin * depth, (begin + count) * depth)
    for at in range(0, columns, 256):
        here = slice(at, min(at + 256, columns))
        term = rest[0][:, here] if has_total else None
        for part in (0, 1):
            high, low = halves(held[part, rows, here])
            wide = dot32(left[part], high)
            thin = dot32(left[part][:BLOCK], low)
            both = wide[:BLOCK] + wide[BLOCK:] + thin
            term = both if term is None else term - both if minus else term + both
        total[:, here] = term
    if not pieces:
        outs[0][...] = total[...]
    for piece, out in zip(pieces, outs):
        place = pl.multiple_of(start_of(ids[0], *piece), out.shape[1])
        out[...] = total[:, pl.ds(place, out.shape[1])]


def pull(held, ids, vectors, begin, total, start_of=None, pieces=(), size=0, minus=False):
    columns, (width, depth) = held.shape[2], vectors[0].shape
    if not fast(columns, depth):
        values = jnp.concatenate(vectors, axis=1)
        held = held[:, begin * depth : (begin + len(vectors)) * depth]
        term = exact_dot(values, held[0]) + exact_dot(turned_rows(values), held[1])
        total = term if total is None else total - term if minus else total + term
        if not pieces:
            return total
        return [
            lax.dynamic_slice(total, (0, start_of(ids[0], *piece)), (width, size))
            for piece in pieces
        ]
    before = [] if total is None else [(total, VMEM)]
    shapes = [(width, size)] * len(pieces) if pieces else [(width, columns)]
    outs = call(
        functools.partial(
            pull_kernel, begin, len(vectors), total is not None, minus, start_of, pieces
        ),
        [(ids, pltpu.SMEM), *((chunk, VMEM) for chunk in vectors), (held, VMEM), *before],
        [jax.ShapeDtypeStruct(shape, jnp.float32) for shape in shapes],
        [VMEM((width, columns), jnp.float32)],
        2 * 3 * len(vectors) * depth * columns * 2 * BLOCK,
    )
    return outs if pieces else outs[0]


def spread_kernel(start_of, chunks, ids, vectors, held, *refs):
    outs = refs[-len(chunks) :]
    size = outs[0].shape[0]
    values = vectors[...]
    high, low = halves(values)
    turned_high, turned_low = halves(turned_rows(values))
    left = (
        jnp.concatenate([high, low], axis=0),
        jnp.concatenate([turned_high, turned_low], axis=0),
    )
    for chunk, out in zip(chunks, outs):
        here = pl.ds(pl.multiple_of(start_of(ids[0], ids[1], *chunk), size), size)
        term = None
        for part in (0, 1):
            high, low = halves(held[part, :, here])
            wide = dot32(left[part], high)
            thin = dot32(left[part][:BLOCK], low)
            both = wide[:BLOCK] + wide[BLOCK:] + thin
            term = both if term is None else term + both
        out[...] = term.T


def spread(held, ids, vectors, start_of, chunks, size):
    width, depth = vectors.shape
    if not fast(depth, size):
        whole = exact_dot(vectors, held[0]) + exact_dot(turned_rows(vectors), held[1])
        return [
            lax.dynamic_slice(whole, (0, start_of(ids[0], ids[1], *chunk)), (width, size)).T
            for chunk in chunks
        ]
    return call(
        functools.partial(spread_kernel, start_of, chunks),
        [(ids, pltpu.SMEM), (vectors, VMEM), (held, VMEM)],
        [jax.ShapeDtypeStruct((size, width), jnp.float32)] * len(chunks),
        [],
        2 * 3 * len(chunks) * depth * size * 2 * BLOCK,
    )


def add_kernel(indices, has_base, turned, *refs):
    outs = refs[-2:] if turned else refs[-1:]
    total = None
    for index, ref in zip(indices, refs[has_base:]):
        term = ref[...] if index is None else ref[index]
        total = term if total is None else total + term
    total = refs[0][...] - total if has_base else total
    outs[0][...] = total
    if turned:
        outs[1][...] = total.T


def add(terms, base=None, tokens=(), turned=False):
    arrays, indices = zip(*terms)
    shape = base.shape if base is not None else arrays[0].shape[-2:]
    if not fast(*shape):
        total = sum(array if index is None else array[index] for array, index in terms)
        total = total if base is None else base - total
        return (total, total.T) if turned else total
    bases = [] if base is None else [base]
    shapes = [shape, shape[::-1]] if turned else [shape]
    outs = call(
        functools.partial(add_kernel, indices, len(bases), turned),
        [*((array, VMEM) for array in (*bases, *arrays)), *((token, pl.ANY) for token in tokens)],
        [jax.ShapeDtypeStruct(extent, jnp.float32) for extent in shapes],
    )
    return outs if turned else outs[0]


def settle_kernel(ids, *refs):
    out = refs[-1]
    for leaf, chunk in enumerate(refs[:-1]):
        rows = chunk.shape[1]
        place = pl.multiple_of((ids[0] ^ leaf) * rows, rows)
        out[pl.ds(place, rows), :] = chunk[...].T


def settle(ids, chunks):
    width, rows = chunks[0].shape
    if not fast(width, rows):
        natural = jnp.take(jnp.stack(chunks), jnp.arange(len(chunks), dtype=jnp.int32) ^ ids[0], axis=0)
        return jnp.transpose(natural, (0, 2, 1)).reshape(-1, width)
    return call(
        settle_kernel,
        [(ids, pltpu.SMEM), *((chunk, VMEM) for chunk in chunks)],
        [jax.ShapeDtypeStruct((len(chunks) * rows, width), jnp.float32)],
    )[0]


def swap(value, leaf_bits, front_bits):
    groups, fronts = lax.axis_size("leaf"), lax.axis_size("front")
    pairs = [
        (leaf * fronts + front, (leaf ^ leaf_bits) * fronts + (front ^ front_bits))
        for leaf in range(groups)
        for front in range(fronts)
    ]
    return lax.ppermute(value, ("leaf", "front"), pairs)


def across(value):
    return swap(value, 0, 1)


def along(value, apart):
    return swap(value, 0, 2 * apart)


def sibling(value):
    return swap(value, 1, 0)


def opposite(value):
    return swap(value, 2, 0)


def spread_chain(own, errands=(), with_beside=True):
    held, apart = {0: own}, lax.axis_size("front") // 4
    errands, done, beside = list(errands), [], {}
    while apart:
        far = {place | apart: along(value, apart) for place, value in held.items()}
        ready = errands.pop(0)(own) if errands else []
        done.append(ready)
        if with_beside:
            place = apart if len(done) > 1 else 0
            beside[place] = across(held[place] if place in held else far[place])
            ready = [*ready, beside[place]]
        far[max(far)] = after(far[max(far)], ready)
        held.update(far)
        apart //= 2
    if with_beside:
        beside = {place: beside[place] if place in beside else across(held[place]) for place in held}
    return held, beside, done


def sum_chain(terms, errands=(), first=(), **last):
    terms, apart, errands, done = dict(terms), 1, list(errands), []
    ready = list(first)
    while apart < len(terms):
        top = max(place for place in range(apart, len(terms), 2 * apart))
        for place in reversed(range(apart, len(terms), 2 * apart)):
            summed = add(terms[place], tokens=ready if place == top else ())
            token = summed if place == top else token
            terms[place - apart] = [*terms[place - apart], (along(summed, apart), None)]
        ready = errands.pop(0)(token) if errands else []
        done.append(ready)
        apart *= 2
    return add(terms[0], tokens=ready, **last), done


def ways(place):
    return ((across, opposite), (1, 0), (0, 2)) if place % 2 else ((opposite, across), (0, 2), (1, 0))


def body(
    leaf_source,
    mid_source,
    root_source,
    leaf_inverse,
    leaf_coupling,
    mid_inverse,
    mid_coupling,
    root_inverse,
    leaf_blocks,
    mid_blocks,
):
    fronts = lax.axis_size("front")
    places = list(range(fronts // 2))
    downward = places[::-1]
    group, front = lax.axis_index("leaf"), lax.axis_index("front")
    ids = jnp.stack([group, front]).astype(jnp.int32)
    side = group % 2
    source_two, source_one = leaf_source[0], mid_source[0]
    inverse_two, coupling_two = leaf_inverse[0], leaf_coupling[0]
    inverse_one, coupling_one = mid_inverse[0], mid_coupling[0]
    rows_two = source_two.shape[0]
    half = source_one.shape[0]
    root_block = root_source.shape[0]
    quarter = root_block // lax.axis_size("leaf")
    root_rows = root_inverse.shape[1] // fronts

    def backwards(order):
        numbers = jnp.arange(order.shape[0], dtype=jnp.int32)
        hits = order[None, :] == numbers[:, None]
        return jnp.sum(jnp.where(hits, numbers[None, :], 0), axis=1, dtype=jnp.int32)

    child_two = backwards(leaf_blocks[0])
    child_one = backwards(lax.dynamic_index_in_dim(mid_blocks, group // 2, 0, keepdims=False))

    def two_start(group, front, leaf_bits, front_bits):
        return (front ^ front_bits) * rows_two

    def half_start(group, front, leaf_bits, front_bits):
        return (front ^ front_bits) * (2 * half) + ((group ^ leaf_bits) % 2) * half

    def one_start(group, front, leaf_bits, front_bits):
        return (front ^ front_bits) * half

    def quarter_start(group, front, leaf_bits, front_bits):
        return (front ^ front_bits) * root_block + (group ^ leaf_bits) * quarter

    def root_start(group, front, leaf_bits, front_bits):
        return (front ^ front_bits) * root_rows

    def whole_start(group, front):
        return 0

    def first_row(group):
        return 0

    def side_row(group, bits):
        return ((group ^ bits) % 2) * half

    def leaf_row(group, bits):
        return (group ^ bits) * quarter

    def pair(place, leaf_bits=0):
        return [(leaf_bits, 2 * place + 1), (leaf_bits, 2 * place)]

    def arrivals(place, groups=(0,)):
        return [(leaf_bits, 2 * place + other) for other in (0, 1) for leaf_bits in groups]

    def square(place):
        _, first, second = ways(place)
        return [
            (first[1] | second[1], 2 * place + (first[0] | second[0])),
            (first[1], 2 * place + first[0]),
            (second[1], 2 * place + second[0]),
            (0, 2 * place),
        ]

    def square_both(place):
        return [(bits ^ 1, other) for bits, other in square(place)] + square(place)

    def square_arrivals(place):
        return [(bits ^ other, at) for bits, at in square(place)[::-1] for other in (0, 1)]

    count = len(places)
    early, late = downward[: count // 2], downward[count // 2 :]
    near, far = places[: count // 2], places[count // 2 :]

    def chunks_of(which, chunks):
        return [chunk for place in which for chunk in chunks(place)]

    def leaf_inverse_rows(token):
        return fetch(inverse_two, ids, None, whole_start, [()], inverse_two.shape[1], token)

    def leaf_lift_rows(which, token):
        chunks = chunks_of(which, lambda place: pair(place, 1)) + chunks_of(which, pair)
        return fetch(coupling_two, ids, child_two, half_start, chunks, half, token)

    def mid_lift_rows(which, token):
        return fetch(inverse_one, ids, None, one_start, chunks_of(which, pair), half, token)

    def root_lift_rows(which, token):
        chunks = chunks_of(which, square_both)
        return fetch(coupling_one, ids, child_one, quarter_start, chunks, quarter, token)

    def root_rows_of(which, token):
        return fetch(root_inverse, ids, None, root_start, chunks_of(which, pair), root_rows, token)

    def root_pull_rows(which, token):
        chunks = chunks_of(which, square_arrivals)
        return fetch(coupling_one, ids, child_one, quarter_start, chunks, quarter, token)

    def mid_pull_rows(which, token):
        return fetch(inverse_one, ids, None, one_start, chunks_of(which, arrivals), half, token)

    def leaf_pull_rows(which, token):
        chunks = chunks_of(which, lambda place: arrivals(place, (0, 1)))
        return fetch(coupling_two, ids, child_two, half_start, chunks, half, token)

    chain, beside, ((rows_inverse,), (rows_early, rows_late), *_) = spread_chain(
        source_two,
        [
            lambda token: [leaf_inverse_rows(token)],
            lambda token: [leaf_lift_rows(early, token), leaf_lift_rows(late, token)],
        ],
    )
    coming = [vector for place in places for vector in (chain[place], beside[place])]
    coming_chunks = chunks_of(places, arrivals)
    total = None
    for first, end in ((0, fronts // 2), (fronts // 2, fronts - 1), (fronts - 1, fronts)):
        total = fold(
            rows_inverse, ids, coming[first:end], two_start, coming_chunks[first:end], total, end == fronts
        )
    solved_two, solved_two_turned = total

    def leaf_lift(held, which):
        size = 2 * len(which)
        theirs, mine = lift(held, ids, [solved_two], first_row, [()], half, 0, [size, size])
        theirs, terms = sibling(theirs), {}
        for at, place in enumerate(which):
            given = add([(mine, 2 * at), (theirs, 2 * at)])
            terms[place] = [(mine, 2 * at + 1), (theirs, 2 * at + 1), (across(given), None)]
        return terms, mine

    terms, _ = leaf_lift(rows_early, early)
    more, token = leaf_lift(rows_late, late)
    own_half, ((rows_one_early,), (rows_one_late,), *_) = sum_chain(
        {**terms, **more},
        [
            lambda token: [mid_lift_rows(early, token)],
            lambda token: [mid_lift_rows(late, token)],
        ],
        [token],
        base=source_one,
    )

    halves_one = [own_half, sibling(own_half)]

    def paired(which, parts):
        return {
            place: [(kept, 0 if kept.ndim > 2 else None), (across(given.reshape(given.shape[-2:])), None)]
            for place, given, kept in zip(which, parts[0::2], parts[1::2])
        }

    def mid_lift(held, which):
        ones = [1] * (2 * len(which))
        return lift(held, ids, halves_one, side_row, [(0,), (1,)], half, 0, ones)

    parts, more = mid_lift(rows_one_early, early), mid_lift(rows_one_late, late)
    (solved_one, solved_one_turned), ((rows_early,), (rows_late,), *_) = sum_chain(
        {**paired(early, parts), **paired(late, more)},
        [
            lambda token: [root_lift_rows(early, token)],
            lambda token: [root_lift_rows(late, token)],
        ],
        more[:1],
        turned=True,
    )

    def corner_terms(place, theirs, mine, tokens=()):
        (first_way, second_way), _, _ = ways(place)
        theirs = sibling(theirs)
        if place == places[-1]:
            corner = first_way(add([(mine, 0), (theirs, 0)]))
            first = (first_way(add([(mine, 1), (theirs, 1)])), None)
            inner = add([(mine, 2), (theirs, 2), (corner, None)], tokens=tokens)
        else:
            outer = first_way(mine[:2] + theirs[:2])
            first = (outer, 1)
            inner = add([(mine, 2), (theirs, 2), (outer, 0)])
        return [(mine, 3), (theirs, 3), first, (second_way(inner), None)]

    def root_lift(held, begin, which):
        fours = [4] * (2 * len(which))
        return lift(held, ids, [solved_one], first_row, [()], quarter, 8 * begin, fours)

    parts = [part for at in range(len(early)) for part in root_lift(rows_early, at, early[at : at + 1])]
    parts += root_lift(rows_late, 0, late)
    own_source = lax.dynamic_slice_in_dim(root_source, group * quarter, quarter, 0)
    own_quarter, ((rows_root_early,), (rows_root_late,), *_) = sum_chain(
        {
            place: corner_terms(place, theirs, mine, parts[-1:])
            for place, theirs, mine in zip(downward, parts[0::2], parts[1::2])
        },
        [
            lambda token: [root_rows_of(early, token)],
            lambda token: [root_rows_of(late, token)],
        ],
        base=own_source,
    )
    over_quarter = opposite(own_quarter)
    quarters = [own_quarter, over_quarter, sibling(own_quarter), sibling(over_quarter)]

    def root_apply(held, which):
        ones, parts = [1] * (2 * len(which)), [(0,), (2,), (1,), (3,)]
        return lift(held, ids, quarters, leaf_row, parts, root_rows, 0, ones, turned=True)

    parts, more = root_apply(rows_root_early, early), root_apply(rows_root_late, late)
    whole_root, (_, (rows_near,), *_) = sum_chain(
        {**paired(early, parts), **paired(late, more)},
        [lambda token: [], lambda token: [root_pull_rows(near, token)]],
        more[:1],
    )
    chain, beside, ((rows_far,), (rows_one_near,), *_) = spread_chain(
        whole_root,
        [
            lambda token: [root_pull_rows(far, token)],
            lambda token: [mid_pull_rows(near, token)],
        ],
    )
    late_vectors = [vector for place in late for vector in (beside[place], chain[place])]
    early_vectors = [vector for place in early for vector in (beside[place], chain[place])]
    total = pull(rows_root_late, ids, late_vectors, 0, None)
    total = pull(rows_root_early, ids, early_vectors[1:], 1, total)
    theirs_own, theirs_over, mine_own, mine_over = pull(
        rows_root_early, ids, early_vectors[:1], 0, total, leaf_row, [(1,), (3,), (0,), (2,)], quarter
    )
    rows_one_far = mid_pull_rows(far, mine_own)
    over = add([(mine_over, None), (sibling(theirs_over), None)])
    theirs_own = sibling(theirs_own)
    own_quarter = add(
        [(mine_own, None), (theirs_own, None), (opposite(over), None)], tokens=[rows_one_far]
    )

    chain, _, _ = spread_chain(own_quarter, with_beside=False)
    rest_one = solved_one_turned
    for place in places:
        (first_way, second_way), _, _ = ways(place)
        first, second = first_way(chain[place]), second_way(chain[place])
        mine = [chain[place], second, first, second_way(first)]
        vectors = [vector for chunk in mine for vector in (chunk, sibling(chunk))]
        if place == 0:
            at = 4 if ways(place)[1][1] else 2
            root_solution = settle(ids, vectors[:2] + vectors[at : at + 2])
        held, begin = (rows_near, 8 * place) if place in near else (rows_far, 8 * (place - len(near)))
        for first, end in ((0, 8),) if place < places[-1] else ((0, 4), (4, 8)):
            rest_one = pull(held, ids, vectors[first:end], begin + first, rest_one, minus=True)
    chain, beside, ((rows_near,), (rows_far, *_), *_) = spread_chain(
        rest_one,
        [
            lambda token: [leaf_pull_rows(near, token)],
            lambda token: [leaf_pull_rows(far, token), root_solution],
        ],
    )
    near_vectors = [vector for place in near for vector in (chain[place], beside[place])]
    far_vectors = [vector for place in far for vector in (chain[place], beside[place])]
    total = pull(rows_one_near, ids, near_vectors, 0, None)
    total = pull(rows_one_far, ids, far_vectors[:-1], 0, total)
    theirs, mine = pull(
        rows_one_far, ids, far_vectors[-1:], len(far_vectors) - 1, total, side_row, [(1,), (0,)], half
    )
    mid_columns, mid_solution = add([(mine, None), (sibling(theirs), None)], turned=True)

    chain, beside, ((rows_inverse,), *_) = spread_chain(
        mid_columns, [lambda token: [leaf_inverse_rows(token)]]
    )
    vectors = {}
    for place in places:
        mine = [chain[place], beside[place]]
        vectors[place] = [vector for chunk in mine for vector in (chunk, sibling(chunk))]
    near_vectors = [vector for place in near for vector in vectors[place]]
    far_vectors = [vector for place in far for vector in vectors[place]]
    rest_two = pull(rows_near, ids, near_vectors, 0, solved_two_turned, minus=True)
    rest_two = pull(rows_far, ids, far_vectors[:-2], 0, rest_two, minus=True)
    rest_two = pull(
        rows_far, ids, far_vectors[-2:], len(far_vectors) - 2, rest_two, minus=True
    )

    def leaf_spread(which):
        return spread(rows_inverse, ids, rest_two, two_start, chunks_of(which, pair), rows_two)

    parts, more = leaf_spread(early), leaf_spread(late)
    leaf_solution, _ = sum_chain({**paired(early, parts), **paired(late, more)}, (), more[:1])
    return (leaf_solution[None], mid_solution[None], root_solution)


def solution(mesh):
    placed = (
        P("leaf", "front", None),
        P("leaf", "front", None),
        P("front", None),
        P("leaf", None, "front", None),
        P("leaf", None, None, "front"),
        P("leaf", None, None, "front"),
        P("leaf", None, None, "front"),
        P(None, "leaf", "front"),
        P("leaf", None),
        P(),
    )
    return jax.shard_map(
        body,
        mesh=mesh,
        in_specs=placed,
        out_specs=(P("leaf", "front", None), P("leaf", "front", None), P("front", None)),
        check_vma=False,
    )
```

```python
import functools
import math

import jax
import jax.numpy as jnp
from jax import lax
from jax.experimental import pallas as pl
from jax.experimental.pallas import tpu as pltpu
from jax.sharding import PartitionSpec as P

BLOCK = 128
VMEM = pltpu.VMEM
exact_dot = functools.partial(jnp.dot, precision=lax.Precision.HIGHEST)


def halves(values):
    high = values.astype(jnp.bfloat16)
    low = (values - high.astype(jnp.float32)).astype(jnp.bfloat16)
    return high, low


def turned_columns(vectors):
    width = vectors.shape[1] // 2
    return jnp.concatenate([-vectors[:, width:], vectors[:, :width]], axis=1)


def turned_rows(vectors):
    width = vectors.shape[0] // 2
    return jnp.concatenate([-vectors[width:], vectors[:width]], axis=0)


def dot32(left, right):
    return jnp.dot(left, right, preferred_element_type=jnp.float32)


def fast(*extents):
    return all(extent % BLOCK == 0 for extent in extents)


def call(kernel, operands, outs, scratch=(), flops=0, room=10):
    arrays, spaces = zip(*operands)
    size = lambda a: math.prod(a.shape) * a.dtype.itemsize
    held = sum(size(a) for a, space in operands if space == VMEM) + sum(size(o) for o in outs)
    scratch_bytes = sum(size(s) for s in scratch if hasattr(s, "shape") and s.memory_space == VMEM)
    moved = held if any(space == VMEM for space in spaces) else 2 * held
    return pl.pallas_call(
        kernel,
        out_shape=outs,
        in_specs=[pl.BlockSpec(memory_space=space) for space in spaces],
        out_specs=[pl.BlockSpec(memory_space=VMEM)] * len(outs),
        scratch_shapes=scratch,
        compiler_params=pltpu.CompilerParams(
            vmem_limit_bytes=scratch_bytes + room * 1024 * 1024
        ),
        cost_estimate=pl.CostEstimate(flops=flops, bytes_accessed=moved, transcendentals=0),
    )(*arrays)


class Place:
    def __init__(self, ids, child):
        self.ids, self.child = ids, child

    def starts(self, start_of, chunks, rows):
        group, front = self.ids[0], self.ids[1]
        unit = rows if self.child is None else min(BLOCK, rows)
        for chunk in chunks:
            start = start_of(group, front, *chunk)
            for inner in range(0, rows, unit):
                row = start + inner
                if self.child is not None:
                    row = self.child[row // BLOCK] * BLOCK + row % BLOCK
                yield row


def fetch_kernel(start_of, chunks, rows, unit, with_child, ids, *refs):
    child = refs[0] if with_child else None
    matrix, out, sems = refs[-3:]
    copies = []
    for index, row in enumerate(Place(ids, child).starts(start_of, chunks, rows)):
        copy = pltpu.make_async_copy(
            matrix.at[:, pl.ds(pl.multiple_of(row, unit), unit), :],
            out.at[:, pl.ds(index * unit, unit), :],
            sems.at[index],
        )
        copy.start()
        copies.append(copy)
    for copy in copies:
        copy.wait()


def fetch(matrix, ids, child, start_of, chunks, rows, token):
    columns, count = matrix.shape[2], len(chunks) * rows
    unit = rows if child is None else min(BLOCK, rows)
    if not fast(rows, columns):
        starts = jnp.stack(list(Place(ids, child).starts(start_of, chunks, rows)))
        picked = (starts[:, None] + jnp.arange(unit, dtype=jnp.int32)).reshape(-1)
        return jnp.take(matrix, picked, axis=1)
    orders = [(ids, pltpu.SMEM)] + ([] if child is None else [(child, pltpu.SMEM)])
    pinned = pltpu.with_memory_space_constraint(matrix, pltpu.HBM)
    return call(
        functools.partial(fetch_kernel, start_of, chunks, rows, unit, child is not None),
        [*orders, (token, pl.ANY), (pinned, pl.ANY)],
        [jax.ShapeDtypeStruct((2, count, columns), jnp.float32)],
        [pltpu.SemaphoreType.DMA((count // unit,))],
        room=1,
    )[0]


def pass_kernel(*refs):
    del refs


def after(value, tokens):
    if not tokens or not fast(*value.shape[-2:]):
        return value
    return pl.pallas_call(
        pass_kernel,
        out_shape=jax.ShapeDtypeStruct(value.shape, value.dtype),
        in_specs=[pl.BlockSpec(memory_space=pl.ANY)] * (1 + len(tokens)),
        out_specs=pl.BlockSpec(memory_space=pl.ANY),
        input_output_aliases={0: 0},
        compiler_params=pltpu.CompilerParams(vmem_limit_bytes=1024 * 1024),
        cost_estimate=pl.CostEstimate(flops=0, bytes_accessed=1024, transcendentals=0),
    )(value, *tokens)


def wide_of(real, imag):
    real_high, real_low = halves(real)
    imag_high, imag_low = halves(imag)
    return jnp.concatenate([real_high, imag_high, real_low, imag_low], axis=1)


def lift_kernel(start_of, parts, rows, begin, counts, turned, ids, *refs):
    chunk_refs, (held, *rest) = refs[: len(parts)], refs[len(parts) :]
    outs, (natural, weights) = rest[-2 - len(counts) : -2], rest[-2:]
    depth = natural.shape[0]
    step = chunk_refs[0].shape[0]
    for part, chunk in zip(parts, chunk_refs):
        place = pl.multiple_of(start_of(ids[0], *part), step)
        natural[pl.ds(place, step), :] = chunk[...]
    for half, values in enumerate((natural[...], turned_columns(natural[...]))):
        high, low = halves(values)
        both = jnp.concatenate([high, low], axis=1)
        weights[half * depth : (half + 1) * depth, :] = both
        weights[(half + 2) * depth : (half + 3) * depth, :] = both
    for out, count in zip(outs, counts):
        together = 1 if turned or count % 2 else 2
        for index in range(0, count, together):
            here = slice((begin + index) * rows, (begin + index + together) * rows)
            wide = dot32(wide_of(held[0, here], held[1, here]), weights[...])
            whole = wide[:, :BLOCK] + wide[:, BLOCK:]
            if turned:
                out[index] = whole.T
            else:
                out[index : index + together] = whole.reshape(together, rows, BLOCK)
        begin += count


def lift(held, ids, vectors, start_of, parts, rows, begin, counts, turned=False):
    depth, width = held.shape[2], vectors[0].shape[1]
    if not fast(rows, depth, vectors[0].shape[0]):
        whole = jnp.zeros((depth, width), jnp.float32)
        for part, chunk in zip(parts, vectors):
            whole = lax.dynamic_update_slice(whole, chunk, (start_of(ids[0], *part), 0))
        held = held[:, begin * rows : (begin + sum(counts)) * rows]
        result = exact_dot(held[0], whole) + exact_dot(held[1], turned_columns(whole))
        result = result.reshape(-1, rows, width)
        result = jnp.transpose(result, (0, 2, 1)) if turned else result
        ends = [sum(counts[: i + 1]) for i in range(len(counts))]
        return [result[end - count : end] for end, count in zip(ends, counts)]
    shape = (width, rows) if turned else (rows, width)
    return call(
        functools.partial(lift_kernel, start_of, parts, rows, begin, counts, turned),
        [
            (ids, pltpu.SMEM),
            *((chunk, VMEM) for chunk in vectors),
            (held, VMEM),
        ],
        [jax.ShapeDtypeStruct((count, *shape), jnp.float32) for count in counts],
        [VMEM((depth, BLOCK), jnp.float32), VMEM((4 * depth, 2 * BLOCK), jnp.bfloat16)],
        2 * 4 * sum(counts) * rows * depth * 2 * BLOCK,
    )


def fold_kernel(start_of, chunks, has_total, turned, ids, *refs):
    chunk_refs, (held, *rest) = refs[: len(chunks)], refs[len(chunks) :]
    outs = rest[-2:] if turned else rest[-1:]
    total = rest[0][...] if has_total else None
    depth = chunk_refs[0].shape[0]
    for chunk, chunk_ref in zip(chunks, chunk_refs):
        values = chunk_ref[...]
        high, low = halves(values)
        turned_high, turned_low = halves(turned_columns(values))
        both = jnp.concatenate(
            [
                jnp.concatenate([high, low], axis=1),
                jnp.concatenate([turned_high, turned_low], axis=1),
            ],
            axis=0,
        )
        here = pl.ds(pl.multiple_of(start_of(ids[0], ids[1], *chunk), depth), depth)
        tile = wide_of(held[0, :, here], held[1, :, here])
        wide = dot32(tile, jnp.concatenate([both, both], axis=0))
        term = wide[:, :BLOCK] + wide[:, BLOCK:]
        total = term if total is None else total + term
    outs[0][...] = total
    if turned:
        outs[1][...] = total.T


def fold(held, ids, vectors, start_of, chunks, total, turned=False):
    rows, (depth, width) = held.shape[1], vectors[0].shape
    if not fast(rows, depth):
        for chunk, values in zip(chunks, vectors):
            column = start_of(ids[0], ids[1], *chunk)
            taken = lax.dynamic_slice(held, (0, 0, column), (2, rows, depth))
            term = exact_dot(taken[0], values) + exact_dot(taken[1], turned_columns(values))
            total = term if total is None else total + term
        return (total, total.T) if turned else total
    before = [] if total is None else [(total, VMEM)]
    shapes = [(rows, width), (width, rows)] if turned else [(rows, width)]
    outs = call(
        functools.partial(fold_kernel, start_of, chunks, total is not None, turned),
        [(ids, pltpu.SMEM), *((chunk, VMEM) for chunk in vectors), (held, VMEM), *before],
        [jax.ShapeDtypeStruct(shape, jnp.float32) for shape in shapes],
        [],
        2 * 4 * len(chunks) * rows * depth * 2 * BLOCK,
    )
    return outs if turned else outs[0]


def pull_kernel(begin, count, has_total, minus, start_of, pieces, ids, *refs):
    chunk_refs, (held, *rest) = refs[:count], refs[count:]
    outs, total = rest[has_total:-1], rest[-1]
    depth, columns = chunk_refs[0].shape[1], held.shape[2]
    lefts = []
    for chunk in chunk_refs:
        values = chunk[...]
        high, low = halves(values)
        turned_high, turned_low = halves(turned_rows(values))
        lefts.append(
            (
                jnp.concatenate([high, low], axis=0),
                jnp.concatenate([turned_high, turned_low], axis=0),
            )
        )
    left = [jnp.concatenate(side, axis=1) for side in zip(*lefts)]
    rows = slice(begin * depth, (begin + count) * depth)
    for at in range(0, columns, 256):
        here = slice(at, min(at + 256, columns))
        term = rest[0][:, here] if has_total else None
        for part in (0, 1):
            high, low = halves(held[part, rows, here])
            wide = dot32(left[part], high)
            thin = dot32(left[part][:BLOCK], low)
            both = wide[:BLOCK] + wide[BLOCK:] + thin
            term = both if term is None else term - both if minus else term + both
        total[:, here] = term
    if not pieces:
        outs[0][...] = total[...]
    for piece, out in zip(pieces, outs):
        place = pl.multiple_of(start_of(ids[0], *piece), out.shape[1])
        out[...] = total[:, pl.ds(place, out.shape[1])]


def pull(held, ids, vectors, begin, total, start_of=None, pieces=(), size=0, minus=False):
    columns, (width, depth) = held.shape[2], vectors[0].shape
    if not fast(columns, depth):
        values = jnp.concatenate(vectors, axis=1)
        held = held[:, begin * depth : (begin + len(vectors)) * depth]
        term = exact_dot(values, held[0]) + exact_dot(turned_rows(values), held[1])
        total = term if total is None else total - term if minus else total + term
        if not pieces:
            return total
        return [
            lax.dynamic_slice(total, (0, start_of(ids[0], *piece)), (width, size))
            for piece in pieces
        ]
    before = [] if total is None else [(total, VMEM)]
    shapes = [(width, size)] * len(pieces) if pieces else [(width, columns)]
    outs = call(
        functools.partial(
            pull_kernel, begin, len(vectors), total is not None, minus, start_of, pieces
        ),
        [(ids, pltpu.SMEM), *((chunk, VMEM) for chunk in vectors), (held, VMEM), *before],
        [jax.ShapeDtypeStruct(shape, jnp.float32) for shape in shapes],
        [VMEM((width, columns), jnp.float32)],
        2 * 3 * len(vectors) * depth * columns * 2 * BLOCK,
    )
    return outs if pieces else outs[0]


def spread_kernel(start_of, chunks, ids, vectors, held, *refs):
    outs = refs[-len(chunks) :]
    size = outs[0].shape[0]
    values = vectors[...]
    high, low = halves(values)
    turned_high, turned_low = halves(turned_rows(values))
    left = (
        jnp.concatenate([high, low], axis=0),
        jnp.concatenate([turned_high, turned_low], axis=0),
    )
    for chunk, out in zip(chunks, outs):
        here = pl.ds(pl.multiple_of(start_of(ids[0], ids[1], *chunk), size), size)
        term = None
        for part in (0, 1):
            high, low = halves(held[part, :, here])
            wide = dot32(left[part], high)
            thin = dot32(left[part][:BLOCK], low)
            both = wide[:BLOCK] + wide[BLOCK:] + thin
            term = both if term is None else term + both
        out[...] = term.T


def spread(held, ids, vectors, start_of, chunks, size):
    width, depth = vectors.shape
    if not fast(depth, size):
        whole = exact_dot(vectors, held[0]) + exact_dot(turned_rows(vectors), held[1])
        return [
            lax.dynamic_slice(whole, (0, start_of(ids[0], ids[1], *chunk)), (width, size)).T
            for chunk in chunks
        ]
    return call(
        functools.partial(spread_kernel, start_of, chunks),
        [(ids, pltpu.SMEM), (vectors, VMEM), (held, VMEM)],
        [jax.ShapeDtypeStruct((size, width), jnp.float32)] * len(chunks),
        [],
        2 * 3 * len(chunks) * depth * size * 2 * BLOCK,
    )


def add_kernel(indices, has_base, turned, *refs):
    outs = refs[-2:] if turned else refs[-1:]
    total = None
    for index, ref in zip(indices, refs[has_base:]):
        term = ref[...] if index is None else ref[index]
        total = term if total is None else total + term
    total = refs[0][...] - total if has_base else total
    outs[0][...] = total
    if turned:
        outs[1][...] = total.T


def add(terms, base=None, tokens=(), turned=False):
    arrays, indices = zip(*terms)
    shape = base.shape if base is not None else arrays[0].shape[-2:]
    if not fast(*shape):
        total = sum(array if index is None else array[index] for array, index in terms)
        total = total if base is None else base - total
        return (total, total.T) if turned else total
    bases = [] if base is None else [base]
    shapes = [shape, shape[::-1]] if turned else [shape]
    outs = call(
        functools.partial(add_kernel, indices, len(bases), turned),
        [*((array, VMEM) for array in (*bases, *arrays)), *((token, pl.ANY) for token in tokens)],
        [jax.ShapeDtypeStruct(extent, jnp.float32) for extent in shapes],
        room=2,
    )
    return outs if turned else outs[0]


def settle_kernel(ids, *refs):
    out = refs[-1]
    for leaf, chunk in enumerate(refs[:-1]):
        rows = chunk.shape[1]
        place = pl.multiple_of((ids[0] ^ leaf) * rows, rows)
        out[pl.ds(place, rows), :] = chunk[...].T


def settle(ids, chunks):
    width, rows = chunks[0].shape
    if not fast(width, rows):
        natural = jnp.take(jnp.stack(chunks), jnp.arange(len(chunks), dtype=jnp.int32) ^ ids[0], axis=0)
        return jnp.transpose(natural, (0, 2, 1)).reshape(-1, width)
    return call(
        settle_kernel,
        [(ids, pltpu.SMEM), *((chunk, VMEM) for chunk in chunks)],
        [jax.ShapeDtypeStruct((len(chunks) * rows, width), jnp.float32)],
    )[0]


def swap(value, leaf_bits, front_bits):
    groups, fronts = lax.axis_size("leaf"), lax.axis_size("front")
    pairs = [
        (leaf * fronts + front, (leaf ^ leaf_bits) * fronts + (front ^ front_bits))
        for leaf in range(groups)
        for front in range(fronts)
    ]
    return lax.ppermute(value, ("leaf", "front"), pairs)


def across(value):
    return swap(value, 0, 1)


def along(value, apart):
    return swap(value, 0, 2 * apart)


def sibling(value):
    return swap(value, 1, 0)


def opposite(value):
    return swap(value, 2, 0)


def spread_chain(own, errands=(), with_beside=True):
    held, apart = {0: own}, lax.axis_size("front") // 4
    errands, done, beside = list(errands), [], {}
    while apart:
        far = {place | apart: along(value, apart) for place, value in held.items()}
        ready = errands.pop(0)(own) if errands else []
        done.append(ready)
        if with_beside:
            place = apart if len(done) > 1 else 0
            beside[place] = across(held[place] if place in held else far[place])
            ready = [*ready, beside[place]]
        far[max(far)] = after(far[max(far)], ready)
        held.update(far)
        apart //= 2
    if with_beside:
        beside = {place: beside[place] if place in beside else across(held[place]) for place in held}
    return held, beside, done


def sum_chain(terms, errands=(), first=(), **last):
    terms, apart, errands, done = dict(terms), 1, list(errands), []
    ready = list(first)
    while apart < len(terms):
        top = max(place for place in range(apart, len(terms), 2 * apart))
        for place in reversed(range(apart, len(terms), 2 * apart)):
            summed = add(terms[place], tokens=ready if place == top else ())
            token = summed if place == top else token
            terms[place - apart] = [*terms[place - apart], (along(summed, apart), None)]
        ready = errands.pop(0)(token) if errands else []
        done.append(ready)
        apart *= 2
    return add(terms[0], tokens=ready, **last), done


def ways(place):
    return ((across, opposite), (1, 0), (0, 2)) if place % 2 else ((opposite, across), (0, 2), (1, 0))


def body(
    leaf_source,
    mid_source,
    root_source,
    leaf_inverse,
    leaf_coupling,
    mid_inverse,
    mid_coupling,
    root_inverse,
    leaf_blocks,
    mid_blocks,
):
    fronts = lax.axis_size("front")
    places = list(range(fronts // 2))
    downward = places[::-1]
    group, front = lax.axis_index("leaf"), lax.axis_index("front")
    ids = jnp.stack([group, front]).astype(jnp.int32)
    side = group % 2
    source_two, source_one = leaf_source[0], mid_source[0]
    inverse_two, coupling_two = leaf_inverse[0], leaf_coupling[0]
    inverse_one, coupling_one = mid_inverse[0], mid_coupling[0]
    rows_two = source_two.shape[0]
    half = source_one.shape[0]
    root_block = root_source.shape[0]
    quarter = root_block // lax.axis_size("leaf")
    root_rows = root_inverse.shape[1] // fronts

    def backwards(order):
        numbers = jnp.arange(order.shape[0], dtype=jnp.int32)
        hits = order[None, :] == numbers[:, None]
        return jnp.sum(jnp.where(hits, numbers[None, :], 0), axis=1, dtype=jnp.int32)

    child_two = backwards(leaf_blocks[0])
    child_one = backwards(lax.dynamic_index_in_dim(mid_blocks, group // 2, 0, keepdims=False))

    def two_start(group, front, leaf_bits, front_bits):
        return (front ^ front_bits) * rows_two

    def half_start(group, front, leaf_bits, front_bits):
        return (front ^ front_bits) * (2 * half) + ((group ^ leaf_bits) % 2) * half

    def one_start(group, front, leaf_bits, front_bits):
        return (front ^ front_bits) * half

    def quarter_start(group, front, leaf_bits, front_bits):
        return (front ^ front_bits) * root_block + (group ^ leaf_bits) * quarter

    def root_start(group, front, leaf_bits, front_bits):
        return (front ^ front_bits) * root_rows

    def whole_start(group, front):
        return 0

    def first_row(group):
        return 0

    def side_row(group, bits):
        return ((group ^ bits) % 2) * half

    def leaf_row(group, bits):
        return (group ^ bits) * quarter

    def pair(place, leaf_bits=0):
        return [(leaf_bits, 2 * place + 1), (leaf_bits, 2 * place)]

    def arrivals(place, groups=(0,)):
        return [(leaf_bits, 2 * place + other) for other in (0, 1) for leaf_bits in groups]

    def square(place):
        _, first, second = ways(place)
        return [
            (first[1] | second[1], 2 * place + (first[0] | second[0])),
            (first[1], 2 * place + first[0]),
            (second[1], 2 * place + second[0]),
            (0, 2 * place),
        ]

    def square_both(place):
        return [(bits ^ 1, other) for bits, other in square(place)] + square(place)

    def square_arrivals(place):
        return [(bits ^ other, at) for bits, at in square(place)[::-1] for other in (0, 1)]

    count = len(places)
    early, late = downward[: count // 2], downward[count // 2 :]
    near, far = places[: count // 2], places[count // 2 :]

    def chunks_of(which, chunks):
        return [chunk for place in which for chunk in chunks(place)]

    def leaf_inverse_rows(token):
        return fetch(inverse_two, ids, None, whole_start, [()], inverse_two.shape[1], token)

    def leaf_lift_rows(which, token):
        chunks = chunks_of(which, lambda place: pair(place, 1)) + chunks_of(which, pair)
        return fetch(coupling_two, ids, child_two, half_start, chunks, half, token)

    def mid_lift_rows(which, token):
        return fetch(inverse_one, ids, None, one_start, chunks_of(which, pair), half, token)

    def root_lift_rows(which, token):
        chunks = chunks_of(which, square_both)
        return fetch(coupling_one, ids, child_one, quarter_start, chunks, quarter, token)

    def root_rows_of(which, token):
        return fetch(root_inverse, ids, None, root_start, chunks_of(which, pair), root_rows, token)

    def root_pull_rows(which, token):
        chunks = chunks_of(which, square_arrivals)
        return fetch(coupling_one, ids, child_one, quarter_start, chunks, quarter, token)

    def mid_pull_rows(which, token):
        return fetch(inverse_one, ids, None, one_start, chunks_of(which, arrivals), half, token)

    def leaf_pull_rows(which, token):
        chunks = chunks_of(which, lambda place: arrivals(place, (0, 1)))
        return fetch(coupling_two, ids, child_two, half_start, chunks, half, token)

    chain, beside, ((rows_inverse,), (rows_early, rows_late), *_) = spread_chain(
        source_two,
        [
            lambda token: [leaf_inverse_rows(token)],
            lambda token: [leaf_lift_rows(early, token), leaf_lift_rows(late, token)],
        ],
    )
    coming = [vector for place in places for vector in (chain[place], beside[place])]
    coming_chunks = chunks_of(places, arrivals)
    total = None
    for first, end in ((0, fronts // 2), (fronts // 2, fronts - 1), (fronts - 1, fronts)):
        total = fold(
            rows_inverse, ids, coming[first:end], two_start, coming_chunks[first:end], total, end == fronts
        )
    solved_two, solved_two_turned = total

    def leaf_lift(held, which):
        size = 2 * len(which)
        theirs, mine = lift(held, ids, [solved_two], first_row, [()], half, 0, [size, size])
        theirs, terms = sibling(theirs), {}
        for at, place in enumerate(which):
            given = add([(mine, 2 * at), (theirs, 2 * at)])
            terms[place] = [(mine, 2 * at + 1), (theirs, 2 * at + 1), (across(given), None)]
        return terms, mine

    terms, _ = leaf_lift(rows_early, early)
    more, token = leaf_lift(rows_late, late)
    own_half, ((rows_one_early,), (rows_one_late,), *_) = sum_chain(
        {**terms, **more},
        [
            lambda token: [mid_lift_rows(early, token)],
            lambda token: [mid_lift_rows(late, token)],
        ],
        [token],
        base=source_one,
    )

    halves_one = [own_half, sibling(own_half)]

    def paired(which, parts):
        return {
            place: [(kept, 0 if kept.ndim > 2 else None), (across(given.reshape(given.shape[-2:])), None)]
            for place, given, kept in zip(which, parts[0::2], parts[1::2])
        }

    def mid_lift(held, which):
        ones = [1] * (2 * len(which))
        return lift(held, ids, halves_one, side_row, [(0,), (1,)], half, 0, ones)

    parts, more = mid_lift(rows_one_early, early), mid_lift(rows_one_late, late)
    (solved_one, solved_one_turned), ((rows_early,), (rows_late,), *_) = sum_chain(
        {**paired(early, parts), **paired(late, more)},
        [
            lambda token: [root_lift_rows(early, token)],
            lambda token: [root_lift_rows(late, token)],
        ],
        more[:1],
        turned=True,
    )

    def corner_terms(place, theirs, mine, tokens=()):
        (first_way, second_way), _, _ = ways(place)
        theirs = sibling(theirs)
        if place == places[-1]:
            corner = first_way(add([(mine, 0), (theirs, 0)]))
            first = (first_way(add([(mine, 1), (theirs, 1)])), None)
            inner = add([(mine, 2), (theirs, 2), (corner, None)], tokens=tokens)
        else:
            outer = first_way(mine[:2] + theirs[:2])
            first = (outer, 1)
            inner = add([(mine, 2), (theirs, 2), (outer, 0)])
        return [(mine, 3), (theirs, 3), first, (second_way(inner), None)]

    def root_lift(held, begin, which):
        fours = [4] * (2 * len(which))
        return lift(held, ids, [solved_one], first_row, [()], quarter, 8 * begin, fours)

    parts = [part for at in range(len(early)) for part in root_lift(rows_early, at, early[at : at + 1])]
    parts += root_lift(rows_late, 0, late)
    own_source = lax.dynamic_slice_in_dim(root_source, group * quarter, quarter, 0)
    own_quarter, ((rows_root_early,), (rows_root_late,), *_) = sum_chain(
        {
            place: corner_terms(place, theirs, mine, parts[-1:])
            for place, theirs, mine in zip(downward, parts[0::2], parts[1::2])
        },
        [
            lambda token: [root_rows_of(early, token)],
            lambda token: [root_rows_of(late, token)],
        ],
        base=own_source,
    )
    over_quarter = opposite(own_quarter)
    quarters = [own_quarter, over_quarter, sibling(own_quarter), sibling(over_quarter)]

    def root_apply(held, which):
        ones, parts = [1] * (2 * len(which)), [(0,), (2,), (1,), (3,)]
        return lift(held, ids, quarters, leaf_row, parts, root_rows, 0, ones, turned=True)

    parts, more = root_apply(rows_root_early, early), root_apply(rows_root_late, late)
    whole_root, (_, (rows_near,), *_) = sum_chain(
        {**paired(early, parts), **paired(late, more)},
        [lambda token: [], lambda token: [root_pull_rows(near, token)]],
        more[:1],
    )
    chain, beside, ((rows_far,), (rows_one_near,), *_) = spread_chain(
        whole_root,
        [
            lambda token: [root_pull_rows(far, token)],
            lambda token: [mid_pull_rows(near, token)],
        ],
    )
    late_vectors = [vector for place in late for vector in (beside[place], chain[place])]
    early_vectors = [vector for place in early for vector in (beside[place], chain[place])]
    total = pull(rows_root_late, ids, late_vectors, 0, None)
    total = pull(rows_root_early, ids, early_vectors[1:], 1, total)
    theirs_own, theirs_over, mine_own, mine_over = pull(
        rows_root_early, ids, early_vectors[:1], 0, total, leaf_row, [(1,), (3,), (0,), (2,)], quarter
    )
    rows_one_far = mid_pull_rows(far, mine_own)
    over = add([(mine_over, None), (sibling(theirs_over), None)])
    theirs_own = sibling(theirs_own)
    own_quarter = add(
        [(mine_own, None), (theirs_own, None), (opposite(over), None)], tokens=[rows_one_far]
    )

    chain, _, _ = spread_chain(own_quarter, with_beside=False)
    rest_one = solved_one_turned
    for place in places:
        (first_way, second_way), _, _ = ways(place)
        first, second = first_way(chain[place]), second_way(chain[place])
        mine = [chain[place], second, first, second_way(first)]
        vectors = [vector for chunk in mine for vector in (chunk, sibling(chunk))]
        if place == 0:
            at = 4 if ways(place)[1][1] else 2
            root_solution = settle(ids, vectors[:2] + vectors[at : at + 2])
        held, begin = (rows_near, 8 * place) if place in near else (rows_far, 8 * (place - len(near)))
        for first, end in ((0, 8),) if place < places[-1] else ((0, 4), (4, 8)):
            rest_one = pull(held, ids, vectors[first:end], begin + first, rest_one, minus=True)
    chain, beside, ((rows_near,), (rows_far, *_), *_) = spread_chain(
        rest_one,
        [
            lambda token: [leaf_pull_rows(near, token)],
            lambda token: [leaf_pull_rows(far, token), root_solution],
        ],
    )
    near_vectors = [vector for place in near for vector in (chain[place], beside[place])]
    far_vectors = [vector for place in far for vector in (chain[place], beside[place])]
    total = pull(rows_one_near, ids, near_vectors, 0, None)
    total = pull(rows_one_far, ids, far_vectors[:-1], 0, total)
    theirs, mine = pull(
        rows_one_far, ids, far_vectors[-1:], len(far_vectors) - 1, total, side_row, [(1,), (0,)], half
    )
    mid_columns, mid_solution = add([(mine, None), (sibling(theirs), None)], turned=True)

    chain, beside, ((rows_inverse,), *_) = spread_chain(
        mid_columns, [lambda token: [leaf_inverse_rows(token)]]
    )
    vectors = {}
    for place in places:
        mine = [chain[place], beside[place]]
        vectors[place] = [vector for chunk in mine for vector in (chunk, sibling(chunk))]
    near_vectors = [vector for place in near for vector in vectors[place]]
    far_vectors = [vector for place in far for vector in vectors[place]]
    rest_two = pull(rows_near, ids, near_vectors, 0, solved_two_turned, minus=True)
    rest_two = pull(rows_far, ids, far_vectors[:-2], 0, rest_two, minus=True)
    rest_two = pull(
        rows_far, ids, far_vectors[-2:], len(far_vectors) - 2, rest_two, minus=True
    )

    def leaf_spread(which):
        return spread(rows_inverse, ids, rest_two, two_start, chunks_of(which, pair), rows_two)

    parts, more = leaf_spread(early), leaf_spread(late)
    leaf_solution, _ = sum_chain({**paired(early, parts), **paired(late, more)}, (), more[:1])
    return (leaf_solution[None], mid_solution[None], root_solution)


def solution(mesh):
    placed = (
        P("leaf", "front", None),
        P("leaf", "front", None),
        P("front", None),
        P("leaf", None, "front", None),
        P("leaf", None, None, "front"),
        P("leaf", None, None, "front"),
        P("leaf", None, None, "front"),
        P(None, "leaf", "front"),
        P("leaf", None),
        P(),
    )
    return jax.shard_map(
        body,
        mesh=mesh,
        in_specs=placed,
        out_specs=(P("leaf", "front", None), P("leaf", "front", None), P("front", None)),
        check_vma=False,
    )
```

```python
import functools
import math

import jax
import jax.numpy as jnp
from jax import lax
from jax.experimental import pallas as pl
from jax.experimental.pallas import tpu as pltpu
from jax.sharding import PartitionSpec as P

BLOCK = 128
VMEM = pltpu.VMEM
exact_dot = functools.partial(jnp.dot, precision=lax.Precision.HIGHEST)


def halves(values):
    high = values.astype(jnp.bfloat16)
    low = (values - high.astype(jnp.float32)).astype(jnp.bfloat16)
    return high, low


def turned_columns(vectors):
    width = vectors.shape[1] // 2
    return jnp.concatenate([-vectors[:, width:], vectors[:, :width]], axis=1)


def turned_rows(vectors):
    width = vectors.shape[0] // 2
    return jnp.concatenate([-vectors[width:], vectors[:width]], axis=0)


def dot32(left, right):
    return jnp.dot(left, right, preferred_element_type=jnp.float32)


def fast(*extents):
    return all(extent % BLOCK == 0 for extent in extents)


def call(kernel, operands, outs, scratch=(), flops=0, room=10):
    arrays, spaces = zip(*operands)
    size = lambda a: math.prod(a.shape) * a.dtype.itemsize
    held = sum(size(a) for a, space in operands if space == VMEM) + sum(size(o) for o in outs)
    scratch_bytes = sum(size(s) for s in scratch if hasattr(s, "shape") and s.memory_space == VMEM)
    moved = held if any(space == VMEM for space in spaces) else 2 * held
    return pl.pallas_call(
        kernel,
        out_shape=outs,
        in_specs=[pl.BlockSpec(memory_space=space) for space in spaces],
        out_specs=[pl.BlockSpec(memory_space=VMEM)] * len(outs),
        scratch_shapes=scratch,
        compiler_params=pltpu.CompilerParams(
            vmem_limit_bytes=scratch_bytes + room * 1024 * 1024
        ),
        cost_estimate=pl.CostEstimate(flops=flops, bytes_accessed=moved, transcendentals=0),
    )(*arrays)


class Place:
    def __init__(self, ids, child):
        self.ids, self.child = ids, child

    def starts(self, start_of, chunks, rows):
        group, front = self.ids[0], self.ids[1]
        unit = rows if self.child is None else min(BLOCK, rows)
        for chunk in chunks:
            start = start_of(group, front, *chunk)
            for inner in range(0, rows, unit):
                row = start + inner
                if self.child is not None:
                    row = self.child[row // BLOCK] * BLOCK + row % BLOCK
                yield row


def orders_kernel(ids, leaf_blocks, mid_blocks, child_two, child_one):
    @pl.loop(0, leaf_blocks.shape[1])
    def _(index):
        child_two[leaf_blocks[0, index]] = index

    row = lax.shift_right_logical(ids[0], 1)

    @pl.loop(0, mid_blocks.shape[1])
    def _(index):
        child_one[mid_blocks[row, index]] = index


def orders(ids, leaf_blocks, mid_blocks):
    return pl.pallas_call(
        orders_kernel,
        out_shape=[
            jax.ShapeDtypeStruct((leaf_blocks.shape[1],), jnp.int32),
            jax.ShapeDtypeStruct((mid_blocks.shape[1],), jnp.int32),
        ],
        in_specs=[pl.BlockSpec(memory_space=pltpu.SMEM)] * 3,
        out_specs=[pl.BlockSpec(memory_space=pltpu.SMEM)] * 2,
        compiler_params=pltpu.CompilerParams(vmem_limit_bytes=1024 * 1024),
    )(ids, leaf_blocks, mid_blocks)


def fetch_kernel(start_of, chunks, rows, unit, with_child, ids, *refs):
    child = refs[0] if with_child else None
    matrix, out, sems = refs[-3:]
    copies = []
    for index, row in enumerate(Place(ids, child).starts(start_of, chunks, rows)):
        copy = pltpu.make_async_copy(
            matrix.at[:, pl.ds(pl.multiple_of(row, unit), unit), :],
            out.at[:, pl.ds(index * unit, unit), :],
            sems.at[index],
        )
        copy.start()
        copies.append(copy)
    for copy in copies:
        copy.wait()


def fetch(matrix, ids, child, start_of, chunks, rows, token):
    columns, count = matrix.shape[2], len(chunks) * rows
    unit = rows if child is None else min(BLOCK, rows)
    if not fast(rows, columns):
        starts = jnp.stack(list(Place(ids, child).starts(start_of, chunks, rows)))
        picked = (starts[:, None] + jnp.arange(unit, dtype=jnp.int32)).reshape(-1)
        return jnp.take(matrix, picked, axis=1)
    orders = [(ids, pltpu.SMEM)] + ([] if child is None else [(child, pltpu.SMEM)])
    pinned = pltpu.with_memory_space_constraint(matrix, pltpu.HBM)
    return call(
        functools.partial(fetch_kernel, start_of, chunks, rows, unit, child is not None),
        [*orders, (token, pl.ANY), (pinned, pl.ANY)],
        [jax.ShapeDtypeStruct((2, count, columns), jnp.float32)],
        [pltpu.SemaphoreType.DMA((count // unit,))],
        room=1,
    )[0]


def pass_kernel(*refs):
    del refs


def copy_kernel(*refs):
    refs[-1][...] = refs[-2][...]


def after(value, tokens, copied=False):
    if not tokens or not fast(*value.shape[-2:]):
        return value
    space = VMEM if copied else pl.ANY
    return pl.pallas_call(
        copy_kernel if copied else pass_kernel,
        out_shape=jax.ShapeDtypeStruct(value.shape, value.dtype),
        in_specs=[pl.BlockSpec(memory_space=pl.ANY)] * len(tokens)
        + [pl.BlockSpec(memory_space=space)],
        out_specs=pl.BlockSpec(memory_space=space),
        input_output_aliases={} if copied else {len(tokens): 0},
        compiler_params=pltpu.CompilerParams(vmem_limit_bytes=1024 * 1024),
        cost_estimate=pl.CostEstimate(flops=0, bytes_accessed=1024, transcendentals=0),
    )(*tokens, value)


def wide_of(real, imag):
    real_high, real_low = halves(real)
    imag_high, imag_low = halves(imag)
    return jnp.concatenate([real_high, imag_high, real_low, imag_low], axis=1)


def lift_kernel(start_of, parts, rows, begin, counts, turned, ids, *refs):
    chunk_refs, (held, *rest) = refs[: len(parts)], refs[len(parts) :]
    outs, (natural, weights) = rest[-2 - len(counts) : -2], rest[-2:]
    depth = natural.shape[0]
    step = chunk_refs[0].shape[0]
    for part, chunk in zip(parts, chunk_refs):
        place = pl.multiple_of(start_of(ids[0], *part), step)
        natural[pl.ds(place, step), :] = chunk[...]
    for half, values in enumerate((natural[...], turned_columns(natural[...]))):
        high, low = halves(values)
        both = jnp.concatenate([high, low], axis=1)
        weights[half * depth : (half + 1) * depth, :] = both
        weights[(half + 2) * depth : (half + 3) * depth, :] = both
    for out, count in zip(outs, counts):
        together = 1 if turned or count % 2 else 2
        for index in range(0, count, together):
            here = slice((begin + index) * rows, (begin + index + together) * rows)
            wide = dot32(wide_of(held[0, here], held[1, here]), weights[...])
            whole = wide[:, :BLOCK] + wide[:, BLOCK:]
            if turned:
                out[index] = whole.T
            else:
                out[index : index + together] = whole.reshape(together, rows, BLOCK)
        begin += count


def lift(held, ids, vectors, start_of, parts, rows, begin, counts, turned=False, tokens=()):
    depth, width = held.shape[2], vectors[0].shape[1]
    if not fast(rows, depth, vectors[0].shape[0]):
        whole = jnp.zeros((depth, width), jnp.float32)
        for part, chunk in zip(parts, vectors):
            whole = lax.dynamic_update_slice(whole, chunk, (start_of(ids[0], *part), 0))
        held = held[:, begin * rows : (begin + sum(counts)) * rows]
        result = exact_dot(held[0], whole) + exact_dot(held[1], turned_columns(whole))
        result = result.reshape(-1, rows, width)
        result = jnp.transpose(result, (0, 2, 1)) if turned else result
        ends = [sum(counts[: i + 1]) for i in range(len(counts))]
        return [result[end - count : end] for end, count in zip(ends, counts)]
    shape = (width, rows) if turned else (rows, width)
    return call(
        functools.partial(lift_kernel, start_of, parts, rows, begin, counts, turned),
        [
            (ids, pltpu.SMEM),
            *((chunk, VMEM) for chunk in vectors),
            (held, VMEM),
            *((token, pl.ANY) for token in tokens),
        ],
        [jax.ShapeDtypeStruct((count, *shape), jnp.float32) for count in counts],
        [VMEM((depth, BLOCK), jnp.float32), VMEM((4 * depth, 2 * BLOCK), jnp.bfloat16)],
        2 * 4 * sum(counts) * rows * depth * 2 * BLOCK,
    )


def fold_kernel(start_of, chunks, has_total, turned, ids, *refs):
    chunk_refs, (held, *rest) = refs[: len(chunks)], refs[len(chunks) :]
    outs = rest[-2:] if turned else rest[-1:]
    total = rest[0][...] if has_total else None
    depth = chunk_refs[0].shape[0]
    for chunk, chunk_ref in zip(chunks, chunk_refs):
        values = chunk_ref[...]
        high, low = halves(values)
        turned_high, turned_low = halves(turned_columns(values))
        both = jnp.concatenate(
            [
                jnp.concatenate([high, low], axis=1),
                jnp.concatenate([turned_high, turned_low], axis=1),
            ],
            axis=0,
        )
        here = pl.ds(pl.multiple_of(start_of(ids[0], ids[1], *chunk), depth), depth)
        tile = wide_of(held[0, :, here], held[1, :, here])
        wide = dot32(tile, jnp.concatenate([both, both], axis=0))
        term = wide[:, :BLOCK] + wide[:, BLOCK:]
        total = term if total is None else total + term
    outs[0][...] = total
    if turned:
        outs[1][...] = total.T


def fold(held, ids, vectors, start_of, chunks, total, turned=False):
    rows, (depth, width) = held.shape[1], vectors[0].shape
    if not fast(rows, depth):
        for chunk, values in zip(chunks, vectors):
            column = start_of(ids[0], ids[1], *chunk)
            taken = lax.dynamic_slice(held, (0, 0, column), (2, rows, depth))
            term = exact_dot(taken[0], values) + exact_dot(taken[1], turned_columns(values))
            total = term if total is None else total + term
        return (total, total.T) if turned else total
    before = [] if total is None else [(total, VMEM)]
    shapes = [(rows, width), (width, rows)] if turned else [(rows, width)]
    outs = call(
        functools.partial(fold_kernel, start_of, chunks, total is not None, turned),
        [(ids, pltpu.SMEM), *((chunk, VMEM) for chunk in vectors), (held, VMEM), *before],
        [jax.ShapeDtypeStruct(shape, jnp.float32) for shape in shapes],
        [],
        2 * 4 * len(chunks) * rows * depth * 2 * BLOCK,
    )
    return outs if turned else outs[0]


def pull_kernel(begin, picks, arrays, has_total, minus, start_of, pieces, ids, *refs):
    array_refs, (held, *rest) = refs[:arrays], refs[arrays:]
    outs, total = rest[has_total:-1], rest[-1]
    count, depth, columns = len(picks), array_refs[0].shape[-1], held.shape[2]
    chunk_refs = [
        array_refs[at] if index is None else array_refs[at].at[index] for at, index in picks
    ]
    lefts = []
    for chunk in chunk_refs:
        values = chunk[...]
        high, low = halves(values)
        turned_high, turned_low = halves(turned_rows(values))
        lefts.append(
            (
                jnp.concatenate([high, low], axis=0),
                jnp.concatenate([turned_high, turned_low], axis=0),
            )
        )
    left = [jnp.concatenate(side, axis=1) for side in zip(*lefts)]
    rows = slice(begin * depth, (begin + count) * depth)
    for at in range(0, columns, 256):
        here = slice(at, min(at + 256, columns))
        term = rest[0][:, here] if has_total else None
        for part in (0, 1):
            high, low = halves(held[part, rows, here])
            wide = dot32(left[part], high)
            thin = dot32(left[part][:BLOCK], low)
            both = wide[:BLOCK] + wide[BLOCK:] + thin
            term = both if term is None else term - both if minus else term + both
        total[:, here] = term
    if not pieces:
        outs[0][...] = total[...]
    for piece, out in zip(pieces, outs):
        place = pl.multiple_of(start_of(ids[0], *piece), out.shape[1])
        out[...] = total[:, pl.ds(place, out.shape[1])]


def pull(held, ids, vectors, begin, total, start_of=None, pieces=(), size=0, minus=False):
    vectors = [vector if isinstance(vector, tuple) else (vector, None) for vector in vectors]
    columns, (width, depth) = held.shape[2], vectors[0][0].shape[-2:]
    if not fast(columns, depth):
        values = jnp.concatenate(
            [array if index is None else array[index] for array, index in vectors], axis=1
        )
        held = held[:, begin * depth : (begin + len(vectors)) * depth]
        term = exact_dot(values, held[0]) + exact_dot(turned_rows(values), held[1])
        total = term if total is None else total - term if minus else total + term
        if not pieces:
            return total
        return [
            lax.dynamic_slice(total, (0, start_of(ids[0], *piece)), (width, size))
            for piece in pieces
        ]
    before = [] if total is None else [(total, VMEM)]
    shapes = [(width, size)] * len(pieces) if pieces else [(width, columns)]
    arrays = list({id(array): array for array, _ in vectors}.values())
    at = {id(array): place for place, array in enumerate(arrays)}
    picks = [(at[id(array)], index) for array, index in vectors]
    outs = call(
        functools.partial(
            pull_kernel, begin, picks, len(arrays), total is not None, minus, start_of, pieces
        ),
        [(ids, pltpu.SMEM), *((array, VMEM) for array in arrays), (held, VMEM), *before],
        [jax.ShapeDtypeStruct(shape, jnp.float32) for shape in shapes],
        [VMEM((width, columns), jnp.float32)],
        2 * 3 * len(vectors) * depth * columns * 2 * BLOCK,
    )
    return outs if pieces else outs[0]


def spread_kernel(start_of, chunks, ids, vectors, held, *refs):
    outs = refs[-len(chunks) :]
    size = outs[0].shape[0]
    values = vectors[...]
    high, low = halves(values)
    turned_high, turned_low = halves(turned_rows(values))
    left = (
        jnp.concatenate([high, low], axis=0),
        jnp.concatenate([turned_high, turned_low], axis=0),
    )
    for chunk, out in zip(chunks, outs):
        here = pl.ds(pl.multiple_of(start_of(ids[0], ids[1], *chunk), size), size)
        term = None
        for part in (0, 1):
            high, low = halves(held[part, :, here])
            wide = dot32(left[part], high)
            thin = dot32(left[part][:BLOCK], low)
            both = wide[:BLOCK] + wide[BLOCK:] + thin
            term = both if term is None else term + both
        out[...] = term.T


def spread(held, ids, vectors, start_of, chunks, size):
    width, depth = vectors.shape
    if not fast(depth, size):
        whole = exact_dot(vectors, held[0]) + exact_dot(turned_rows(vectors), held[1])
        return [
            lax.dynamic_slice(whole, (0, start_of(ids[0], ids[1], *chunk)), (width, size)).T
            for chunk in chunks
        ]
    return call(
        functools.partial(spread_kernel, start_of, chunks),
        [(ids, pltpu.SMEM), (vectors, VMEM), (held, VMEM)],
        [jax.ShapeDtypeStruct((size, width), jnp.float32)] * len(chunks),
        [],
        2 * 3 * len(chunks) * depth * size * 2 * BLOCK,
    )


def add_kernel(indices, base_start, turned, *refs):
    outs = refs[-2:] if turned else refs[-1:]
    ids, base, *arrays = refs if base_start is not None else (None, None, *refs)
    total = None
    for index, ref in zip(indices, arrays):
        term = ref[...] if index is None else ref[index]
        total = term if total is None else total + term
    if base_start is not None:
        rows = total.shape[0]
        start = pl.multiple_of(base_start(ids[0]), rows)
        total = base[pl.ds(start, rows), :] - total
    outs[0][...] = total
    if turned:
        outs[1][...] = total.T


def add(terms, base=None, tokens=(), turned=False):
    arrays, indices = zip(*terms)
    shape = arrays[0].shape[-2:]
    if isinstance(indices[0], slice):
        shape = (indices[0].stop, *shape)
    if not fast(*shape[-2:]):
        total = sum(array if index is None else array[index] for array, index in terms)
        if base is not None:
            total = lax.dynamic_slice(base[1], (base[2](base[0][0]), 0), shape) - total
        return (total, total.T) if turned else total
    bases = [] if base is None else [(base[0], pltpu.SMEM), (base[1], VMEM)]
    shapes = [shape, shape[::-1]] if turned else [shape]
    outs = call(
        functools.partial(add_kernel, indices, None if base is None else base[2], turned),
        [*bases, *((array, VMEM) for array in arrays), *((token, pl.ANY) for token in tokens)],
        [jax.ShapeDtypeStruct(extent, jnp.float32) for extent in shapes],
        room=2,
    )
    return outs if turned else outs[0]


def settle_kernel(indices, ids, *refs):
    out = refs[-1]
    for leaf, (index, chunk) in enumerate(zip(indices, refs[:-1])):
        rows = chunk.shape[-1]
        place = pl.multiple_of((ids[0] ^ leaf) * rows, rows)
        out[pl.ds(place, rows), :] = (chunk[...] if index is None else chunk[index]).T


def settle(ids, chunks):
    chunks = [chunk if isinstance(chunk, tuple) else (chunk, None) for chunk in chunks]
    width, rows = chunks[0][0].shape[-2:]
    if not fast(width, rows):
        chunks = [array if index is None else array[index] for array, index in chunks]
        natural = jnp.take(jnp.stack(chunks), jnp.arange(len(chunks), dtype=jnp.int32) ^ ids[0], axis=0)
        return jnp.transpose(natural, (0, 2, 1)).reshape(-1, width)
    return call(
        functools.partial(settle_kernel, [index for _, index in chunks]),
        [(ids, pltpu.SMEM), *((array, VMEM) for array, _ in chunks)],
        [jax.ShapeDtypeStruct((len(chunks) * rows, width), jnp.float32)],
    )[0]


def swap(value, leaf_bits, front_bits):
    groups, fronts = lax.axis_size("leaf"), lax.axis_size("front")
    pairs = [
        (leaf * fronts + front, (leaf ^ leaf_bits) * fronts + (front ^ front_bits))
        for leaf in range(groups)
        for front in range(fronts)
    ]
    return lax.ppermute(value, ("leaf", "front"), pairs)


def across(value):
    return swap(value, 0, 1)


def along(value, apart):
    return swap(value, 0, 2 * apart)


def sibling(value):
    return swap(value, 1, 0)


def opposite(value):
    return swap(value, 2, 0)


def spread_chain(own, errands=(), with_beside=True, first_ready=()):
    held, apart = {0: own}, lax.axis_size("front") // 4
    errands, done, beside = list(errands), [], {}
    while apart:
        far = {place | apart: along(value, apart) for place, value in held.items()}
        ready = list(errands.pop(0)(own)) if errands else []
        done.append(list(ready))
        if len(done) == 1:
            ready += first_ready
        if with_beside:
            place = apart if len(done) > 1 else 0
            beside[place] = across(held[place] if place in held else far[place])
            ready.append(beside[place])
        if len(done) == 1 and apart > 1:
            near = along(own, apart // 2)
            ready.append(near)
        far[max(far)] = after(far[max(far)], ready)
        if len(done) == 2:
            far[apart] = near
        held.update(far)
        apart //= 2
    if with_beside:
        beside = {place: beside[place] if place in beside else across(held[place]) for place in held}
    return held, beside, done


def sum_chain(pieces, errands=(), first=(), **last):
    terms, count, errands, done = {}, len(pieces), list(errands), []
    received = {}
    for place in sorted(pieces, reverse=True):
        kept, given = pieces[place]
        terms[place] = list(kept)
        if given is not None:
            ready = [received[count // 2 if place == 0 else count - 1]] if received else []
            received[place] = across(after(given, ready))
            terms[place].append((received[place], None))
    apart, ready = 1, list(first)
    while apart < count:
        top = max(place for place in range(apart, count, 2 * apart))
        for place in reversed(range(apart, count, 2 * apart)):
            summed = add(terms[place], tokens=ready if place == top else ())
            token = summed if place == top else token
            terms[place - apart] = [*terms[place - apart], (along(summed, apart), None)]
        ready = errands.pop(0)(token) if errands else []
        done.append(ready)
        apart *= 2
    return add(terms[0], tokens=ready, **last), done


def ways(place):
    return ((across, opposite), (1, 0), (0, 2)) if place % 2 else ((opposite, across), (0, 2), (1, 0))


def body(
    leaf_source,
    mid_source,
    root_source,
    leaf_inverse,
    leaf_coupling,
    mid_inverse,
    mid_coupling,
    root_inverse,
    leaf_blocks,
    mid_blocks,
):
    fronts = lax.axis_size("front")
    places = list(range(fronts // 2))
    downward = places[::-1]
    group, front = lax.axis_index("leaf"), lax.axis_index("front")
    ids = jnp.stack([group, front]).astype(jnp.int32)
    source_two, source_one = leaf_source[0], mid_source[0]
    inverse_two, coupling_two = leaf_inverse[0], leaf_coupling[0]
    inverse_one, coupling_one = mid_inverse[0], mid_coupling[0]
    rows_two = source_two.shape[0]
    half = source_one.shape[0]
    root_block = root_source.shape[0]
    quarter = root_block // lax.axis_size("leaf")
    root_rows = root_inverse.shape[1] // fronts

    child_two, child_one = orders(ids, leaf_blocks, mid_blocks)

    def two_start(group, front, leaf_bits, front_bits):
        return (front ^ front_bits) * rows_two

    def half_start(group, front, leaf_bits, front_bits):
        return (front ^ front_bits) * (2 * half) + ((group ^ leaf_bits) % 2) * half

    def one_start(group, front, leaf_bits, front_bits):
        return (front ^ front_bits) * half

    def quarter_start(group, front, leaf_bits, front_bits):
        return (front ^ front_bits) * root_block + (group ^ leaf_bits) * quarter

    def root_start(group, front, leaf_bits, front_bits):
        return (front ^ front_bits) * root_rows

    def whole_start(group, front):
        return 0

    def first_row(group):
        return 0

    def own_row(group):
        return group * quarter

    def side_row(group, bits):
        return ((group ^ bits) % 2) * half

    def leaf_row(group, bits):
        return (group ^ bits) * quarter

    def pair(place, leaf_bits=0):
        return [(leaf_bits, 2 * place + 1), (leaf_bits, 2 * place)]

    def arrivals(place, groups=(0,)):
        return [(leaf_bits, 2 * place + other) for other in (0, 1) for leaf_bits in groups]

    def square(place):
        _, first, second = ways(place)
        return [
            (first[1] | second[1], 2 * place + (first[0] | second[0])),
            (first[1], 2 * place + first[0]),
            (second[1], 2 * place + second[0]),
            (0, 2 * place),
        ]

    def square_both(place):
        return [(bits ^ 1, other) for bits, other in square(place)] + square(place)

    def square_arrivals(place):
        return [(bits ^ other, at) for bits, at in square(place)[::-1] for other in (0, 1)]

    count = len(places)
    early, late = downward[: count // 2], downward[count // 2 :]
    near, far = places[: count // 2], places[count // 2 :]

    def chunks_of(which, chunks):
        return [chunk for place in which for chunk in chunks(place)]

    def leaf_inverse_rows(token):
        return fetch(inverse_two, ids, None, whole_start, [()], inverse_two.shape[1], token)

    def leaf_lift_rows(which, token):
        chunks = chunks_of(which, lambda place: pair(place, 1)) + chunks_of(which, pair)
        return fetch(coupling_two, ids, child_two, half_start, chunks, half, token)

    def mid_lift_rows(which, token):
        return fetch(inverse_one, ids, None, one_start, chunks_of(which, pair), half, token)

    def root_lift_rows(which, token):
        chunks = chunks_of(which, square_both)
        return fetch(coupling_one, ids, child_one, quarter_start, chunks, quarter, token)

    def root_rows_of(which, token):
        return fetch(root_inverse, ids, None, root_start, chunks_of(which, pair), root_rows, token)

    def root_pull_rows(which, token):
        chunks = chunks_of(which, square_arrivals)
        return fetch(coupling_one, ids, child_one, quarter_start, chunks, quarter, token)

    def mid_pull_rows(which, token):
        return fetch(inverse_one, ids, None, one_start, chunks_of(which, arrivals), half, token)

    def leaf_pull_rows(which, token):
        chunks = chunks_of(which, lambda place: arrivals(place, (0, 1)))
        return fetch(coupling_two, ids, child_two, half_start, chunks, half, token)

    chain, beside, ((rows_inverse,), (rows_early, rows_late), *_) = spread_chain(
        source_two,
        [
            lambda token: [leaf_inverse_rows(token)],
            lambda token: [leaf_lift_rows(early, token), leaf_lift_rows(late, token)],
        ],
    )
    coming = [vector for place in places for vector in (chain[place], beside[place])]
    coming_chunks = chunks_of(places, arrivals)
    total = None
    for first, end in ((0, fronts // 2), (fronts // 2, fronts - 1), (fronts - 1, fronts)):
        total = fold(
            rows_inverse, ids, coming[first:end], two_start, coming_chunks[first:end], total, end == fronts
        )
    solved_two, solved_two_turned = total

    def leaf_lift(held, which):
        size = 2 * len(which)
        theirs, mine = lift(held, ids, [solved_two], first_row, [()], half, 0, [size, size])
        theirs, terms = sibling(theirs), {}
        for at, place in enumerate(which):
            given = add([(mine, 2 * at), (theirs, 2 * at)])
            terms[place] = [(mine, 2 * at + 1), (theirs, 2 * at + 1)], given
        return terms, mine

    terms, _ = leaf_lift(rows_early, early)
    more, token = leaf_lift(rows_late, late)
    own_half, ((rows_one_early,), (rows_one_late,), *_) = sum_chain(
        {**terms, **more},
        [
            lambda token: [mid_lift_rows(early, token)],
            lambda token: [mid_lift_rows(late, token)],
        ],
        [token],
        base=(ids, source_one, first_row),
    )

    halves_one = [own_half, sibling(own_half)]

    def paired(which, parts):
        return {
            place: ([(kept, 0 if kept.ndim > 2 else None)], given.reshape(given.shape[-2:]))
            for place, given, kept in zip(which, parts[0::2], parts[1::2])
        }

    def mid_lift(held, which):
        ones = [1] * (2 * len(which))
        return lift(held, ids, halves_one, side_row, [(0,), (1,)], half, 0, ones)

    parts, more = mid_lift(rows_one_early, early), mid_lift(rows_one_late, late)
    (solved_one, solved_one_turned), ((rows_early,), (rows_late,), *_) = sum_chain(
        {**paired(early, parts), **paired(late, more)},
        [
            lambda token: [root_lift_rows(early, token)],
            lambda token: [root_lift_rows(late, token)],
        ],
        more[:1],
        turned=True,
    )

    def root_lift(held, begin, which, tokens=()):
        fours = [4] * (2 * len(which))
        return lift(
            held, ids, [solved_one], first_row, [()], quarter, 8 * begin, fours, tokens=tokens
        )

    def corner_terms(place, theirs, mine):
        (first_way, second_way), _, _ = ways(place)
        outer = first_way(add([(mine, slice(0, 2)), (theirs, slice(0, 2))]))
        inner = second_way(add([(mine, 2), (theirs, 2), (outer, 0)]))
        return [(mine, 3), (theirs, 3), (outer, 1), (inner, None)], None

    top, *rest = early
    (first_way, second_way), _, _ = ways(top)
    theirs, mine = root_lift(rows_early, 0, [top])
    theirs = sibling(theirs)
    parts = [part for at, place in enumerate(rest) for part in root_lift(rows_early, at + 1, [place])]
    corner = add([(mine, 0), (theirs, 0)], tokens=parts[-1:])
    parts += root_lift(rows_late, 0, late, [corner])
    first = first_way(add([(mine, 1), (theirs, 1)]))
    inner = add([(mine, 2), (theirs, 2), (first_way(corner), None)], tokens=parts[-1:])
    corners = {top: ([(mine, 3), (theirs, 3), (first, None), (second_way(inner), None)], None)}
    for place, theirs, mine in zip(rest + late, parts[0::2], parts[1::2]):
        corners[place] = corner_terms(place, sibling(theirs), mine)
    own_quarter, ((rows_root_early,), (rows_root_late,), *_) = sum_chain(
        corners,
        [
            lambda token: [root_rows_of(early, token)],
            lambda token: [root_rows_of(late, token)],
        ],
        base=(ids, root_source, own_row),
    )
    over_quarter = opposite(own_quarter)
    quarters = [own_quarter, over_quarter, sibling(own_quarter), sibling(over_quarter)]

    def root_apply(held, which):
        ones, parts = [1] * (2 * len(which)), [(0,), (2,), (1,), (3,)]
        return lift(held, ids, quarters, leaf_row, parts, root_rows, 0, ones, turned=True)

    parts, more = root_apply(rows_root_early, early), root_apply(rows_root_late, late)
    whole_root, (_, (rows_near,), *_) = sum_chain(
        {**paired(early, parts), **paired(late, more)},
        [lambda token: [], lambda token: [root_pull_rows(near, token)]],
        more[:1],
    )
    chain, beside, ((rows_far,), (rows_one_near,), *_) = spread_chain(
        whole_root,
        [
            lambda token: [root_pull_rows(far, token)],
            lambda token: [mid_pull_rows(near, token)],
        ],
    )
    late_vectors = [vector for place in late for vector in (beside[place], chain[place])]
    early_vectors = [vector for place in early for vector in (beside[place], chain[place])]
    total = pull(rows_root_late, ids, late_vectors, 0, None)
    total = pull(rows_root_early, ids, early_vectors[1:], 1, total)
    theirs_own, theirs_over, mine_own, mine_over = pull(
        rows_root_early, ids, early_vectors[:1], 0, total, leaf_row, [(1,), (3,), (0,), (2,)], quarter
    )
    rows_one_far = mid_pull_rows(far, mine_own)
    over = add([(mine_over, None), (sibling(theirs_over), None)])
    theirs_own = sibling(theirs_own)
    own_quarter = add(
        [(mine_own, None), (theirs_own, None), (opposite(over), None)], tokens=[rows_one_far]
    )

    def corner_values(place, value, ready=()):
        (first_way, second_way), _, _ = ways(place)
        first, second = first_way(value), second_way(value)
        return [value, second, first, second_way(after(first, ready))]

    corners = {0: corner_values(0, own_quarter)}
    chain, _, _ = spread_chain(own_quarter, (), False, corners[0][1:3])
    for place in places[1:]:
        value = chain[place]
        if place == count // 2:
            value = after(value, corners[0][3:], copied=True)
        corners[place] = corner_values(place, value)
    rest_one = solved_one_turned
    for place in places:
        mine = corners[place]
        held, begin = (rows_near, 8 * place) if place in near else (rows_far, 8 * (place - len(near)))
        if place == places[-1]:
            theirs = sibling(jnp.stack(mine[:3]))
            theirs = [(theirs, 0), (theirs, 1), (theirs, 2), sibling(mine[3])]
        else:
            theirs = sibling(jnp.stack(mine))
            theirs = [(theirs, at) for at in range(4)]
        if place == 0:
            at = 2 if ways(place)[1][1] else 1
            root_solution = settle(ids, [mine[0], theirs[0], mine[at], theirs[at]])
        vectors = [vector for both in zip(mine, theirs) for vector in both]
        for first, end in ((0, 8),) if place < places[-1] else ((0, 6), (6, 8)):
            rest_one = pull(held, ids, vectors[first:end], begin + first, rest_one, minus=True)
    chain, beside, ((rows_near,), (rows_far, *_), *_) = spread_chain(
        rest_one,
        [
            lambda token: [leaf_pull_rows(near, token)],
            lambda token: [leaf_pull_rows(far, token), root_solution],
        ],
    )
    near_vectors = [vector for place in near for vector in (chain[place], beside[place])]
    far_vectors = [vector for place in far for vector in (chain[place], beside[place])]
    total = pull(rows_one_near, ids, near_vectors, 0, None)
    total = pull(rows_one_far, ids, far_vectors[:-1], 0, total)
    theirs, mine = pull(
        rows_one_far, ids, far_vectors[-1:], len(far_vectors) - 1, total, side_row, [(1,), (0,)], half
    )
    mid_columns, mid_solution = add([(mine, None), (sibling(theirs), None)], turned=True)

    chain, beside, ((rows_inverse,), *_) = spread_chain(
        mid_columns, [lambda token: [leaf_inverse_rows(token)]]
    )
    def with_theirs(values):
        theirs = sibling(jnp.stack(values)) if len(values) > 1 else sibling(values[0])
        theirs = [(theirs, at) for at in range(len(values))] if len(values) > 1 else [theirs]
        return [vector for both in zip(values, theirs) for vector in both]

    near_values = [value for place in near for value in (chain[place], beside[place])]
    far_values = [value for place in far for value in (chain[place], beside[place])]
    rest_two = pull(rows_near, ids, with_theirs(near_values), 0, solved_two_turned, minus=True)
    rest_two = pull(rows_far, ids, with_theirs(far_values[:-1]), 0, rest_two, minus=True)
    rest_two = pull(
        rows_far, ids, with_theirs(far_values[-1:]), 2 * len(far_values) - 2, rest_two, minus=True
    )

    def leaf_spread(which):
        return spread(rows_inverse, ids, rest_two, two_start, chunks_of(which, pair), rows_two)

    parts, more = leaf_spread(early), leaf_spread(late)
    leaf_solution, _ = sum_chain({**paired(early, parts), **paired(late, more)}, (), more[:1])
    return (leaf_solution[None], mid_solution[None], root_solution)


def solution(mesh):
    placed = (
        P("leaf", "front", None),
        P("leaf", "front", None),
        P("front", None),
        P("leaf", None, "front", None),
        P("leaf", None, None, "front"),
        P("leaf", None, None, "front"),
        P("leaf", None, None, "front"),
        P(None, "leaf", "front"),
        P("leaf", None),
        P(),
    )
    return jax.shard_map(
        body,
        mesh=mesh,
        in_specs=placed,
        out_specs=(P("leaf", "front", None), P("leaf", "front", None), P("front", None)),
        check_vma=False,
    )
```

```python
import functools
import math

import jax
import jax.numpy as jnp
from jax import lax
from jax.experimental import pallas as pl
from jax.experimental.pallas import tpu as pltpu
from jax.sharding import PartitionSpec as P

BLOCK = 128
VMEM = pltpu.VMEM
exact_dot = functools.partial(jnp.dot, precision=lax.Precision.HIGHEST)


def halves(values):
    high = values.astype(jnp.bfloat16)
    low = (values - high.astype(jnp.float32)).astype(jnp.bfloat16)
    return high, low


def turned_columns(vectors):
    width = vectors.shape[1] // 2
    return jnp.concatenate([-vectors[:, width:], vectors[:, :width]], axis=1)


def turned_rows(vectors):
    width = vectors.shape[0] // 2
    return jnp.concatenate([-vectors[width:], vectors[:width]], axis=0)


def dot32(left, right):
    return jnp.dot(left, right, preferred_element_type=jnp.float32)


def fast(*extents):
    return all(extent % BLOCK == 0 for extent in extents)


def call(kernel, operands, outs, scratch=(), flops=0, room=10, hides=True):
    arrays, spaces = zip(*operands)
    size = lambda a: math.prod(a.shape) * a.dtype.itemsize
    held = sum(size(a) for a, space in operands if space == VMEM) + sum(size(o) for o in outs)
    scratch_bytes = sum(size(s) for s in scratch if hasattr(s, "shape") and s.memory_space == VMEM)
    moved = held if any(space == VMEM for space in spaces) else 2 * held
    flops, moved = (flops, moved) if hides else (1024, 1024)
    return pl.pallas_call(
        kernel,
        out_shape=outs,
        in_specs=[pl.BlockSpec(memory_space=space) for space in spaces],
        out_specs=[pl.BlockSpec(memory_space=VMEM)] * len(outs),
        scratch_shapes=scratch,
        compiler_params=pltpu.CompilerParams(
            vmem_limit_bytes=scratch_bytes + room * 1024 * 1024
        ),
        cost_estimate=pl.CostEstimate(flops=flops, bytes_accessed=moved, transcendentals=0),
    )(*arrays)


class Place:
    def __init__(self, ids, child):
        self.ids, self.child = ids, child

    def starts(self, start_of, chunks, rows):
        group, front = self.ids[0], self.ids[1]
        unit = rows if self.child is None else min(BLOCK, rows)
        for chunk in chunks:
            start = start_of(group, front, *chunk)
            for inner in range(0, rows, unit):
                row = start + inner
                if self.child is not None:
                    row = self.child[row // BLOCK] * BLOCK + row % BLOCK
                yield row


def orders_kernel(ids, leaf_blocks, mid_blocks, child_two, child_one):
    for index in range(leaf_blocks.shape[1]):
        child_two[leaf_blocks[0, index]] = index
    row = lax.shift_right_logical(ids[0], 1)
    for index in range(mid_blocks.shape[1]):
        child_one[mid_blocks[row, index]] = index


def orders(ids, leaf_blocks, mid_blocks):
    return pl.pallas_call(
        orders_kernel,
        out_shape=[
            jax.ShapeDtypeStruct((leaf_blocks.shape[1],), jnp.int32),
            jax.ShapeDtypeStruct((mid_blocks.shape[1],), jnp.int32),
        ],
        in_specs=[pl.BlockSpec(memory_space=pltpu.SMEM)] * 3,
        out_specs=[pl.BlockSpec(memory_space=pltpu.SMEM)] * 2,
        compiler_params=pltpu.CompilerParams(vmem_limit_bytes=1024 * 1024),
    )(ids, leaf_blocks, mid_blocks)


def fetch_kernel(start_of, chunks, rows, unit, with_child, ids, *refs):
    child = refs[0] if with_child else None
    matrix, out, sems = refs[-3:]
    copies = []
    for index, row in enumerate(Place(ids, child).starts(start_of, chunks, rows)):
        copy = pltpu.make_async_copy(
            matrix.at[:, pl.ds(pl.multiple_of(row, unit), unit), :],
            out.at[:, pl.ds(index * unit, unit), :],
            sems.at[index],
        )
        copy.start()
        copies.append(copy)
    for copy in copies:
        copy.wait()


def fetch(matrix, ids, child, start_of, chunks, rows, token):
    columns, count = matrix.shape[2], len(chunks) * rows
    unit = rows if child is None else min(BLOCK, rows)
    if not fast(rows, columns):
        starts = jnp.stack(list(Place(ids, child).starts(start_of, chunks, rows)))
        picked = (starts[:, None] + jnp.arange(unit, dtype=jnp.int32)).reshape(-1)
        return jnp.take(matrix, picked, axis=1)
    orders = [(ids, pltpu.SMEM)] + ([] if child is None else [(child, pltpu.SMEM)])
    pinned = pltpu.with_memory_space_constraint(matrix, pltpu.HBM)
    return call(
        functools.partial(fetch_kernel, start_of, chunks, rows, unit, child is not None),
        [*orders, (token, pl.ANY), (pinned, pl.ANY)],
        [jax.ShapeDtypeStruct((2, count, columns), jnp.float32)],
        [pltpu.SemaphoreType.DMA((count // unit,))],
        room=1,
    )[0]


def pass_kernel(*refs):
    del refs


def copy_kernel(*refs):
    refs[-1][...] = refs[-2][...]


def after(value, tokens, copied=False):
    if not tokens or not fast(*value.shape[-2:]):
        return value
    space = VMEM if copied else pl.ANY
    return pl.pallas_call(
        copy_kernel if copied else pass_kernel,
        out_shape=jax.ShapeDtypeStruct(value.shape, value.dtype),
        in_specs=[pl.BlockSpec(memory_space=pl.ANY)] * len(tokens)
        + [pl.BlockSpec(memory_space=space)],
        out_specs=pl.BlockSpec(memory_space=space),
        input_output_aliases={} if copied else {len(tokens): 0},
        compiler_params=pltpu.CompilerParams(vmem_limit_bytes=1024 * 1024),
        cost_estimate=pl.CostEstimate(flops=0, bytes_accessed=1024, transcendentals=0),
    )(*tokens, value)


def wide_of(real, imag):
    real_high, real_low = halves(real)
    imag_high, imag_low = halves(imag)
    return jnp.concatenate([real_high, imag_high, real_low, imag_low], axis=1)


def lift_kernel(start_of, parts, rows, begin, counts, turned, ids, *refs):
    chunk_refs, (held, *rest) = refs[: len(parts)], refs[len(parts) :]
    outs, (natural, weights) = rest[-2 - len(counts) : -2], rest[-2:]
    depth = natural.shape[0]
    step = chunk_refs[0].shape[0]
    for part, chunk in zip(parts, chunk_refs):
        place = pl.multiple_of(start_of(ids[0], *part), step)
        natural[pl.ds(place, step), :] = chunk[...]
    for half, values in enumerate((natural[...], turned_columns(natural[...]))):
        high, low = halves(values)
        both = jnp.concatenate([high, low], axis=1)
        weights[half * depth : (half + 1) * depth, :] = both
        weights[(half + 2) * depth : (half + 3) * depth, :] = both
    for out, count in zip(outs, counts):
        together = 1 if turned or count % 2 else 2
        for index in range(0, count, together):
            here = slice((begin + index) * rows, (begin + index + together) * rows)
            wide = dot32(wide_of(held[0, here], held[1, here]), weights[...])
            whole = wide[:, :BLOCK] + wide[:, BLOCK:]
            if turned:
                out[index] = whole.T
            else:
                out[index : index + together] = whole.reshape(together, rows, BLOCK)
        begin += count


def lift(held, ids, vectors, start_of, parts, rows, begin, counts, turned=False, tokens=()):
    depth, width = held.shape[2], vectors[0].shape[1]
    if not fast(rows, depth, vectors[0].shape[0]):
        whole = jnp.zeros((depth, width), jnp.float32)
        for part, chunk in zip(parts, vectors):
            whole = lax.dynamic_update_slice(whole, chunk, (start_of(ids[0], *part), 0))
        held = held[:, begin * rows : (begin + sum(counts)) * rows]
        result = exact_dot(held[0], whole) + exact_dot(held[1], turned_columns(whole))
        result = result.reshape(-1, rows, width)
        result = jnp.transpose(result, (0, 2, 1)) if turned else result
        ends = [sum(counts[: i + 1]) for i in range(len(counts))]
        return [result[end - count : end] for end, count in zip(ends, counts)]
    shape = (width, rows) if turned else (rows, width)
    return call(
        functools.partial(lift_kernel, start_of, parts, rows, begin, counts, turned),
        [
            (ids, pltpu.SMEM),
            *((chunk, VMEM) for chunk in vectors),
            (held, VMEM),
            *((token, pl.ANY) for token in tokens),
        ],
        [jax.ShapeDtypeStruct((count, *shape), jnp.float32) for count in counts],
        [VMEM((depth, BLOCK), jnp.float32), VMEM((4 * depth, 2 * BLOCK), jnp.bfloat16)],
        2 * 4 * sum(counts) * rows * depth * 2 * BLOCK,
    )


def fold_kernel(start_of, chunks, has_total, turned, ids, *refs):
    chunk_refs, (held, *rest) = refs[: len(chunks)], refs[len(chunks) :]
    outs = rest[-2:] if turned else rest[-1:]
    total = rest[0][...] if has_total else None
    depth = chunk_refs[0].shape[0]
    for chunk, chunk_ref in zip(chunks, chunk_refs):
        values = chunk_ref[...]
        high, low = halves(values)
        turned_high, turned_low = halves(turned_columns(values))
        both = jnp.concatenate(
            [
                jnp.concatenate([high, low], axis=1),
                jnp.concatenate([turned_high, turned_low], axis=1),
            ],
            axis=0,
        )
        here = pl.ds(pl.multiple_of(start_of(ids[0], ids[1], *chunk), depth), depth)
        tile = wide_of(held[0, :, here], held[1, :, here])
        wide = dot32(tile, jnp.concatenate([both, both], axis=0))
        term = wide[:, :BLOCK] + wide[:, BLOCK:]
        total = term if total is None else total + term
    outs[0][...] = total
    if turned:
        outs[1][...] = total.T


def fold(held, ids, vectors, start_of, chunks, total, turned=False):
    rows, (depth, width) = held.shape[1], vectors[0].shape
    if not fast(rows, depth):
        for chunk, values in zip(chunks, vectors):
            column = start_of(ids[0], ids[1], *chunk)
            taken = lax.dynamic_slice(held, (0, 0, column), (2, rows, depth))
            term = exact_dot(taken[0], values) + exact_dot(taken[1], turned_columns(values))
            total = term if total is None else total + term
        return (total, total.T) if turned else total
    before = [] if total is None else [(total, VMEM)]
    shapes = [(rows, width), (width, rows)] if turned else [(rows, width)]
    outs = call(
        functools.partial(fold_kernel, start_of, chunks, total is not None, turned),
        [(ids, pltpu.SMEM), *((chunk, VMEM) for chunk in vectors), (held, VMEM), *before],
        [jax.ShapeDtypeStruct(shape, jnp.float32) for shape in shapes],
        [],
        2 * 4 * len(chunks) * rows * depth * 2 * BLOCK,
    )
    return outs if turned else outs[0]


def pull_kernel(begin, picks, arrays, has_total, minus, start_of, pieces, ids, *refs):
    array_refs, (held, *rest) = refs[:arrays], refs[arrays:]
    outs, total = rest[has_total:-1], rest[-1]
    count, depth, columns = len(picks), array_refs[0].shape[-1], held.shape[2]
    chunk_refs = [
        array_refs[at] if index is None else array_refs[at].at[index] for at, index in picks
    ]
    lefts = []
    for chunk in chunk_refs:
        values = chunk[...]
        high, low = halves(values)
        turned_high, turned_low = halves(turned_rows(values))
        lefts.append(
            (
                jnp.concatenate([high, low], axis=0),
                jnp.concatenate([turned_high, turned_low], axis=0),
            )
        )
    left = [jnp.concatenate(side, axis=1) for side in zip(*lefts)]
    rows = slice(begin * depth, (begin + count) * depth)
    for at in range(0, columns, 256):
        here = slice(at, min(at + 256, columns))
        term = rest[0][:, here] if has_total else None
        for part in (0, 1):
            high, low = halves(held[part, rows, here])
            wide = dot32(left[part], high)
            thin = dot32(left[part][:BLOCK], low)
            both = wide[:BLOCK] + wide[BLOCK:] + thin
            term = both if term is None else term - both if minus else term + both
        total[:, here] = term
    if not pieces:
        outs[0][...] = total[...]
    for piece, out in zip(pieces, outs):
        place = pl.multiple_of(start_of(ids[0], *piece), out.shape[1])
        out[...] = total[:, pl.ds(place, out.shape[1])]


def pull(
    held, ids, vectors, begin, total, start_of=None, pieces=(), size=0, minus=False, hides=True
):
    vectors = [vector if isinstance(vector, tuple) else (vector, None) for vector in vectors]
    columns, (width, depth) = held.shape[2], vectors[0][0].shape[-2:]
    if not fast(columns, depth):
        values = jnp.concatenate(
            [array if index is None else array[index] for array, index in vectors], axis=1
        )
        held = held[:, begin * depth : (begin + len(vectors)) * depth]
        term = exact_dot(values, held[0]) + exact_dot(turned_rows(values), held[1])
        total = term if total is None else total - term if minus else total + term
        if not pieces:
            return total
        return [
            lax.dynamic_slice(total, (0, start_of(ids[0], *piece)), (width, size))
            for piece in pieces
        ]
    before = [] if total is None else [(total, VMEM)]
    shapes = [(width, size)] * len(pieces) if pieces else [(width, columns)]
    arrays = list({id(array): array for array, _ in vectors}.values())
    at = {id(array): place for place, array in enumerate(arrays)}
    picks = [(at[id(array)], index) for array, index in vectors]
    outs = call(
        functools.partial(
            pull_kernel, begin, picks, len(arrays), total is not None, minus, start_of, pieces
        ),
        [(ids, pltpu.SMEM), *((array, VMEM) for array in arrays), (held, VMEM), *before],
        [jax.ShapeDtypeStruct(shape, jnp.float32) for shape in shapes],
        [VMEM((width, columns), jnp.float32)],
        2 * 3 * len(vectors) * depth * columns * 2 * BLOCK,
        hides=hides,
    )
    return outs if pieces else outs[0]


def spread_kernel(start_of, chunks, ids, vectors, held, *refs):
    outs = refs[-len(chunks) :]
    size = outs[0].shape[0]
    values = vectors[...]
    high, low = halves(values)
    turned_high, turned_low = halves(turned_rows(values))
    left = (
        jnp.concatenate([high, low], axis=0),
        jnp.concatenate([turned_high, turned_low], axis=0),
    )
    for chunk, out in zip(chunks, outs):
        here = pl.ds(pl.multiple_of(start_of(ids[0], ids[1], *chunk), size), size)
        term = None
        for part in (0, 1):
            high, low = halves(held[part, :, here])
            wide = dot32(left[part], high)
            thin = dot32(left[part][:BLOCK], low)
            both = wide[:BLOCK] + wide[BLOCK:] + thin
            term = both if term is None else term + both
        out[...] = term.T


def spread(held, ids, vectors, start_of, chunks, size):
    width, depth = vectors.shape
    if not fast(depth, size):
        whole = exact_dot(vectors, held[0]) + exact_dot(turned_rows(vectors), held[1])
        return [
            lax.dynamic_slice(whole, (0, start_of(ids[0], ids[1], *chunk)), (width, size)).T
            for chunk in chunks
        ]
    return call(
        functools.partial(spread_kernel, start_of, chunks),
        [(ids, pltpu.SMEM), (vectors, VMEM), (held, VMEM)],
        [jax.ShapeDtypeStruct((size, width), jnp.float32)] * len(chunks),
        [],
        2 * 3 * len(chunks) * depth * size * 2 * BLOCK,
    )


def add_kernel(indices, base_start, turned, *refs):
    outs = refs[-2:] if turned else refs[-1:]
    ids, base, *arrays = refs if base_start is not None else (None, None, *refs)
    total = None
    for index, ref in zip(indices, arrays):
        term = ref[...] if index is None else ref[index]
        total = term if total is None else total + term
    if base_start is not None:
        rows = total.shape[0]
        start = pl.multiple_of(base_start(ids[0]), rows)
        total = base[pl.ds(start, rows), :] - total
    outs[0][...] = total
    if turned:
        outs[1][...] = total.T


def add(terms, base=None, tokens=(), turned=False):
    arrays, indices = zip(*terms)
    shape = arrays[0].shape[-2:]
    if isinstance(indices[0], slice):
        shape = (indices[0].stop, *shape)
    if not fast(*shape[-2:]):
        total = sum(array if index is None else array[index] for array, index in terms)
        if base is not None:
            total = lax.dynamic_slice(base[1], (base[2](base[0][0]), 0), shape) - total
        return (total, total.T) if turned else total
    bases = [] if base is None else [(base[0], pltpu.SMEM), (base[1], VMEM)]
    shapes = [shape, shape[::-1]] if turned else [shape]
    outs = call(
        functools.partial(add_kernel, indices, None if base is None else base[2], turned),
        [*bases, *((array, VMEM) for array in arrays), *((token, pl.ANY) for token in tokens)],
        [jax.ShapeDtypeStruct(extent, jnp.float32) for extent in shapes],
        room=2,
    )
    return outs if turned else outs[0]


def settle_kernel(indices, ids, *refs):
    out = refs[-1]
    for leaf, (index, chunk) in enumerate(zip(indices, refs[:-1])):
        rows = chunk.shape[-1]
        place = pl.multiple_of((ids[0] ^ leaf) * rows, rows)
        out[pl.ds(place, rows), :] = (chunk[...] if index is None else chunk[index]).T


def settle(ids, chunks):
    chunks = [chunk if isinstance(chunk, tuple) else (chunk, None) for chunk in chunks]
    width, rows = chunks[0][0].shape[-2:]
    if not fast(width, rows):
        chunks = [array if index is None else array[index] for array, index in chunks]
        natural = jnp.take(jnp.stack(chunks), jnp.arange(len(chunks), dtype=jnp.int32) ^ ids[0], axis=0)
        return jnp.transpose(natural, (0, 2, 1)).reshape(-1, width)
    return call(
        functools.partial(settle_kernel, [index for _, index in chunks]),
        [(ids, pltpu.SMEM), *((array, VMEM) for array, _ in chunks)],
        [jax.ShapeDtypeStruct((len(chunks) * rows, width), jnp.float32)],
    )[0]


def swap(value, leaf_bits, front_bits):
    groups, fronts = lax.axis_size("leaf"), lax.axis_size("front")
    pairs = [
        (leaf * fronts + front, (leaf ^ leaf_bits) * fronts + (front ^ front_bits))
        for leaf in range(groups)
        for front in range(fronts)
    ]
    return lax.ppermute(value, ("leaf", "front"), pairs)


def across(value):
    return swap(value, 0, 1)


def along(value, apart):
    return swap(value, 0, 2 * apart)


def sibling(value):
    return swap(value, 1, 0)


def opposite(value):
    return swap(value, 2, 0)


def spread_chain(own, errands=(), with_beside=True, first_ready=()):
    held, apart = {0: own}, lax.axis_size("front") // 4
    errands, done, beside = list(errands), [], {}
    while apart:
        far = {place | apart: along(value, apart) for place, value in held.items()}
        ready = list(errands.pop(0)(own)) if errands else []
        done.append(list(ready))
        if len(done) == 1:
            ready += first_ready
        if with_beside:
            place = apart if len(done) > 1 else 0
            beside[place] = across(held[place] if place in held else far[place])
            ready.append(beside[place])
        if len(done) == 1 and apart > 1:
            near = along(own, apart // 2)
            ready.append(near)
        far[max(far)] = after(far[max(far)], ready)
        if len(done) == 2:
            far[apart] = near
        held.update(far)
        apart //= 2
    if with_beside:
        beside = {place: beside[place] if place in beside else across(held[place]) for place in held}
    return held, beside, done


def sum_chain(pieces, errands=(), first=(), **last):
    count, errands, done = len(pieces), list(errands), []
    terms = {
        place: kept if given is None else [*kept, (across(given), None)]
        for place, (kept, given) in pieces.items()
    }
    apart, ready = 1, list(first)
    while apart < count:
        top = max(place for place in range(apart, count, 2 * apart))
        for place in reversed(range(apart, count, 2 * apart)):
            summed = add(terms[place], tokens=ready if place == top else ())
            token = summed if place == top else token
            terms[place - apart] = [*terms[place - apart], (along(summed, apart), None)]
        ready = errands.pop(0)(token) if errands else []
        done.append(ready)
        apart *= 2
    return add(terms[0], tokens=ready, **last), done


def ways(place):
    return ((across, opposite), (1, 0), (0, 2)) if place % 2 else ((opposite, across), (0, 2), (1, 0))


def body(
    leaf_source,
    mid_source,
    root_source,
    leaf_inverse,
    leaf_coupling,
    mid_inverse,
    mid_coupling,
    root_inverse,
    leaf_blocks,
    mid_blocks,
):
    fronts = lax.axis_size("front")
    places = list(range(fronts // 2))
    downward = places[::-1]
    group, front = lax.axis_index("leaf"), lax.axis_index("front")
    ids = jnp.stack([group, front]).astype(jnp.int32)
    source_two, source_one = leaf_source[0], mid_source[0]
    inverse_two, coupling_two = leaf_inverse[0], leaf_coupling[0]
    inverse_one, coupling_one = mid_inverse[0], mid_coupling[0]
    rows_two = source_two.shape[0]
    half = source_one.shape[0]
    root_block = root_source.shape[0]
    quarter = root_block // lax.axis_size("leaf")
    root_rows = root_inverse.shape[1] // fronts

    child_two, child_one = orders(ids, leaf_blocks, mid_blocks)

    def two_start(group, front, leaf_bits, front_bits):
        return (front ^ front_bits) * rows_two

    def half_start(group, front, leaf_bits, front_bits):
        return (front ^ front_bits) * (2 * half) + ((group ^ leaf_bits) % 2) * half

    def one_start(group, front, leaf_bits, front_bits):
        return (front ^ front_bits) * half

    def quarter_start(group, front, leaf_bits, front_bits):
        return (front ^ front_bits) * root_block + (group ^ leaf_bits) * quarter

    def root_start(group, front, leaf_bits, front_bits):
        return (front ^ front_bits) * root_rows

    def whole_start(group, front):
        return 0

    def first_row(group):
        return 0

    def own_row(group):
        return group * quarter

    def side_row(group, bits):
        return ((group ^ bits) % 2) * half

    def leaf_row(group, bits):
        return (group ^ bits) * quarter

    def pair(place, leaf_bits=0):
        return [(leaf_bits, 2 * place + 1), (leaf_bits, 2 * place)]

    def arrivals(place, groups=(0,)):
        return [(leaf_bits, 2 * place + other) for other in (0, 1) for leaf_bits in groups]

    def square(place):
        _, first, second = ways(place)
        return [
            (first[1] | second[1], 2 * place + (first[0] | second[0])),
            (first[1], 2 * place + first[0]),
            (second[1], 2 * place + second[0]),
            (0, 2 * place),
        ]

    def square_both(place):
        return [(bits ^ 1, other) for bits, other in square(place)] + square(place)

    def square_arrivals(place):
        return [(bits ^ other, at) for bits, at in square(place)[::-1] for other in (0, 1)]

    count = len(places)
    early, late = downward[: count // 2], downward[count // 2 :]
    near, far = places[: count // 2], places[count // 2 :]

    def chunks_of(which, chunks):
        return [chunk for place in which for chunk in chunks(place)]

    def leaf_inverse_rows(token):
        return fetch(inverse_two, ids, None, whole_start, [()], inverse_two.shape[1], token)

    def leaf_lift_rows(which, token):
        chunks = chunks_of(which, lambda place: pair(place, 1)) + chunks_of(which, pair)
        return fetch(coupling_two, ids, child_two, half_start, chunks, half, token)

    def mid_lift_rows(which, token):
        return fetch(inverse_one, ids, None, one_start, chunks_of(which, pair), half, token)

    def root_lift_rows(which, token):
        chunks = chunks_of(which, square_both)
        return fetch(coupling_one, ids, child_one, quarter_start, chunks, quarter, token)

    def root_rows_of(which, token):
        return fetch(root_inverse, ids, None, root_start, chunks_of(which, pair), root_rows, token)

    def root_pull_rows(which, token):
        chunks = chunks_of(which, square_arrivals)
        return fetch(coupling_one, ids, child_one, quarter_start, chunks, quarter, token)

    def mid_pull_rows(which, token):
        return fetch(inverse_one, ids, None, one_start, chunks_of(which, arrivals), half, token)

    def leaf_pull_rows(which, token):
        chunks = chunks_of(which, lambda place: arrivals(place, (0, 1)))
        return fetch(coupling_two, ids, child_two, half_start, chunks, half, token)

    chain, beside, ((rows_inverse,), (rows_early,), *_) = spread_chain(
        source_two,
        [
            lambda token: [leaf_inverse_rows(token)],
            lambda token: [leaf_lift_rows(early, token)],
        ],
    )
    rows_late = leaf_lift_rows(late, rows_early)
    coming = [vector for place in places for vector in (chain[place], beside[place])]
    coming_chunks = chunks_of(places, arrivals)
    total = None
    for first, end in ((0, fronts // 2), (fronts // 2, fronts - 1), (fronts - 1, fronts)):
        last = end == fronts
        if last:
            coming[-1] = after(coming[-1], [rows_late])
        total = fold(
            rows_inverse, ids, coming[first:end], two_start, coming_chunks[first:end], total, last
        )
    solved_two, solved_two_turned = total

    def leaf_lift(held, which):
        size = 2 * len(which)
        theirs, mine = lift(held, ids, [solved_two], first_row, [()], half, 0, [size, size])
        theirs, terms = sibling(theirs), {}
        for at, place in enumerate(which):
            given = add([(mine, 2 * at), (theirs, 2 * at)])
            terms[place] = [(mine, 2 * at + 1), (theirs, 2 * at + 1)], given
        return terms, mine

    terms, _ = leaf_lift(rows_early, early)
    more, token = leaf_lift(rows_late, late)
    own_half, ((rows_one_early,), (rows_one_late,), *_) = sum_chain(
        {**terms, **more},
        [
            lambda token: [mid_lift_rows(early, token)],
            lambda token: [mid_lift_rows(late, token)],
        ],
        [token],
        base=(ids, source_one, first_row),
    )

    halves_one = [own_half, sibling(own_half)]

    def paired(which, parts):
        return {
            place: ([(kept, 0 if kept.ndim > 2 else None)], given.reshape(given.shape[-2:]))
            for place, given, kept in zip(which, parts[0::2], parts[1::2])
        }

    def mid_lift(held, which):
        ones = [1] * (2 * len(which))
        return lift(held, ids, halves_one, side_row, [(0,), (1,)], half, 0, ones)

    parts, more = mid_lift(rows_one_early, early), mid_lift(rows_one_late, late)
    (solved_one, solved_one_turned), ((rows_early,), (rows_late,), *_) = sum_chain(
        {**paired(early, parts), **paired(late, more)},
        [
            lambda token: [root_lift_rows(early, token)],
            lambda token: [root_lift_rows(late, token)],
        ],
        more[:1],
        turned=True,
    )

    def root_lift(held, begin, which, tokens=()):
        fours = [4] * (2 * len(which))
        return lift(
            held, ids, [solved_one], first_row, [()], quarter, 8 * begin, fours, tokens=tokens
        )

    def corner_terms(place, theirs, mine):
        (first_way, second_way), _, _ = ways(place)
        outer = first_way(add([(mine, slice(0, 2)), (theirs, slice(0, 2))]))
        inner = second_way(add([(mine, 2), (theirs, 2), (outer, 0)]))
        return [(mine, 3), (theirs, 3), (outer, 1), (inner, None)], None

    top, *rest = early
    (first_way, second_way), _, _ = ways(top)
    theirs, mine = root_lift(rows_early, 0, [top])
    theirs = sibling(theirs)
    parts = [part for at, place in enumerate(rest) for part in root_lift(rows_early, at + 1, [place])]
    corner = add([(mine, 0), (theirs, 0)], tokens=parts[-1:])
    corner = first_way(corner)
    parts += root_lift(rows_late, 0, late, [corner])
    first = first_way(add([(mine, 1), (theirs, 1)]))
    inner = add([(mine, 2), (theirs, 2), (corner, None)])
    corners = {top: ([(mine, 3), (theirs, 3), (first, None), (second_way(inner), None)], None)}
    for place, theirs, mine in zip(rest + late, parts[0::2], parts[1::2]):
        corners[place] = corner_terms(place, sibling(theirs), mine)
    own_quarter, ((rows_root_early,), (rows_root_late,), *_) = sum_chain(
        corners,
        [
            lambda token: [root_rows_of(early, token)],
            lambda token: [root_rows_of(late, token)],
        ],
        base=(ids, root_source, own_row),
    )
    over_quarter = opposite(own_quarter)
    quarters = [own_quarter, over_quarter, sibling(own_quarter), sibling(over_quarter)]

    def root_apply(held, which):
        ones, parts = [1] * (2 * len(which)), [(0,), (2,), (1,), (3,)]
        return lift(held, ids, quarters, leaf_row, parts, root_rows, 0, ones, turned=True)

    parts, more = root_apply(rows_root_early, early), root_apply(rows_root_late, late)
    whole_root, (_, (rows_near,), *_) = sum_chain(
        {**paired(early, parts), **paired(late, more)},
        [lambda token: [], lambda token: [root_pull_rows(near, token)]],
        more[:1],
    )
    chain, beside, ((rows_far,), (rows_one_near,), *_) = spread_chain(
        whole_root,
        [
            lambda token: [root_pull_rows(far, token)],
            lambda token: [mid_pull_rows(near, token)],
        ],
    )
    late_vectors = [vector for place in late for vector in (beside[place], chain[place])]
    early_vectors = [vector for place in early for vector in (beside[place], chain[place])]
    total = pull(rows_root_late, ids, late_vectors, 0, None)
    total = pull(rows_root_early, ids, early_vectors[1:], 1, total)
    theirs_own, theirs_over, mine_own, mine_over = pull(
        rows_root_early, ids, early_vectors[:1], 0, total, leaf_row, [(1,), (3,), (0,), (2,)], quarter
    )
    rows_one_far = mid_pull_rows(far, mine_own)
    over = add([(mine_over, None), (sibling(theirs_over), None)])
    theirs_own = sibling(theirs_own)
    own_quarter = add(
        [(mine_own, None), (theirs_own, None), (opposite(over), None)], tokens=[rows_one_far]
    )

    def corner_values(place, value, ready=()):
        (first_way, second_way), _, _ = ways(place)
        first, second = first_way(value), second_way(value)
        return [value, second, first, second_way(after(first, ready))]

    corners = {0: corner_values(0, own_quarter)}
    chain, _, _ = spread_chain(own_quarter, (), False, corners[0][1:3])
    for place in places[1:-1]:
        value = chain[place]
        if place == count // 2:
            value = after(value, corners[0][3:], copied=True)
        corners[place] = corner_values(place, value)
    def with_theirs(values):
        theirs = sibling(jnp.stack(values)) if len(values) > 1 else sibling(values[0])
        theirs = [(theirs, at) for at in range(len(values))] if len(values) > 1 else [theirs]
        return [vector for both in zip(values, theirs) for vector in both]

    def pull_one(place, vectors, first, total):
        held, begin = (rows_near, 8 * place) if place in near else (rows_far, 8 * (place - len(near)))
        return pull(held, ids, vectors, begin + first, total, minus=True, hides=False)

    rest_one = solved_one_turned
    for place in places[:-1]:
        vectors = with_theirs(corners[place])
        if place == 0:
            at = 4 if ways(place)[1][1] else 2
            root_solution = settle(ids, [*vectors[:2], *vectors[at : at + 2]])
        rest_one = pull_one(place, vectors, 0, rest_one)
        if place == near[-1]:
            corners[places[-1]] = corner_values(places[-1], chain[places[-1]])
    rest_one = pull_one(places[-1], with_theirs(corners[places[-1]][:3]), 0, rest_one)
    corner = after(corners[places[-1]][3], [rest_one])
    rest_one = pull_one(places[-1], with_theirs([corner]), 6, rest_one)
    chain, beside, ((rows_near,), (rows_far, *_), *_) = spread_chain(
        rest_one,
        [
            lambda token: [leaf_pull_rows(near, token)],
            lambda token: [leaf_pull_rows(far, token), root_solution],
        ],
    )
    near_vectors = [vector for place in near for vector in (chain[place], beside[place])]
    far_vectors = [vector for place in far for vector in (chain[place], beside[place])]
    total = pull(rows_one_near, ids, near_vectors, 0, None)
    total = pull(rows_one_far, ids, far_vectors[:-1], 0, total)
    theirs, mine = pull(
        rows_one_far, ids, far_vectors[-1:], len(far_vectors) - 1, total, side_row, [(1,), (0,)], half
    )
    mid_columns, mid_solution = add([(mine, None), (sibling(theirs), None)], turned=True)

    chain, beside, ((rows_inverse,), *_) = spread_chain(
        mid_columns, [lambda token: [leaf_inverse_rows(token)]]
    )
    near_values = [value for place in near for value in (chain[place], beside[place])]
    far_values = [value for place in far for value in (chain[place], beside[place])]
    rest_two = pull(rows_near, ids, with_theirs(near_values), 0, solved_two_turned, minus=True)
    rest_two = pull(rows_far, ids, with_theirs(far_values[:-1]), 0, rest_two, minus=True)
    vectors = with_theirs([after(far_values[-1], [rest_two])])
    rest_two = pull(rows_far, ids, vectors, 2 * len(far_values) - 2, rest_two, minus=True)

    def leaf_spread(which):
        return spread(rows_inverse, ids, rest_two, two_start, chunks_of(which, pair), rows_two)

    parts, more = leaf_spread(early), leaf_spread(late)
    leaf_solution, _ = sum_chain({**paired(early, parts), **paired(late, more)}, (), more[:1])
    return (leaf_solution[None], mid_solution[None], root_solution)


def solution(mesh):
    placed = (
        P("leaf", "front", None),
        P("leaf", "front", None),
        P("front", None),
        P("leaf", None, "front", None),
        P("leaf", None, None, "front"),
        P("leaf", None, None, "front"),
        P("leaf", None, None, "front"),
        P(None, "leaf", "front"),
        P("leaf", None),
        P(),
    )
    return jax.shard_map(
        body,
        mesh=mesh,
        in_specs=placed,
        out_specs=(P("leaf", "front", None), P("leaf", "front", None), P("front", None)),
        check_vma=False,
    )
```

```python
import functools
import math

import jax
import jax.numpy as jnp
from jax import lax
from jax.experimental import pallas as pl
from jax.experimental.pallas import tpu as pltpu
from jax.sharding import PartitionSpec as P

BLOCK = 128
VMEM = pltpu.VMEM
exact_dot = functools.partial(jnp.dot, precision=lax.Precision.HIGHEST)


def halves(values):
    high = values.astype(jnp.bfloat16)
    low = (values - high.astype(jnp.float32)).astype(jnp.bfloat16)
    return high, low


def turned_columns(vectors):
    width = vectors.shape[1] // 2
    return jnp.concatenate([-vectors[:, width:], vectors[:, :width]], axis=1)


def turned_rows(vectors):
    width = vectors.shape[0] // 2
    return jnp.concatenate([-vectors[width:], vectors[:width]], axis=0)


def dot32(left, right):
    return jnp.dot(left, right, preferred_element_type=jnp.float32)


def fast(*extents):
    return all(extent % BLOCK == 0 for extent in extents)


def call(kernel, operands, outs, scratch=(), flops=0, room=10, hides=True):
    arrays, spaces = zip(*operands)
    size = lambda a: math.prod(a.shape) * a.dtype.itemsize
    held = sum(size(a) for a, space in operands if space == VMEM) + sum(size(o) for o in outs)
    scratch_bytes = sum(size(s) for s in scratch if hasattr(s, "shape") and s.memory_space == VMEM)
    moved = held if any(space == VMEM for space in spaces) else 2 * held
    flops, moved = (flops, moved) if hides else (1024, 1024)
    return pl.pallas_call(
        kernel,
        out_shape=outs,
        in_specs=[pl.BlockSpec(memory_space=space) for space in spaces],
        out_specs=[pl.BlockSpec(memory_space=VMEM)] * len(outs),
        scratch_shapes=scratch,
        compiler_params=pltpu.CompilerParams(
            vmem_limit_bytes=scratch_bytes + room * 1024 * 1024
        ),
        cost_estimate=pl.CostEstimate(flops=flops, bytes_accessed=moved, transcendentals=0),
    )(*arrays)


class Place:
    def __init__(self, ids, child):
        self.ids, self.child = ids, child

    def starts(self, start_of, chunks, rows):
        group, front = self.ids[0], self.ids[1]
        unit = rows if self.child is None else min(BLOCK, rows)
        for chunk in chunks:
            start = start_of(group, front, *chunk)
            for inner in range(0, rows, unit):
                row = start + inner
                if self.child is not None:
                    row = self.child[row // BLOCK] * BLOCK + row % BLOCK
                yield row


def orders_kernel(ids, leaf_blocks, mid_blocks, child_two, child_one):
    for index in range(leaf_blocks.shape[1]):
        child_two[leaf_blocks[0, index]] = index
    row = lax.shift_right_logical(ids[0], 1)
    for index in range(mid_blocks.shape[1]):
        child_one[mid_blocks[row, index]] = index


def orders(ids, leaf_blocks, mid_blocks):
    return pl.pallas_call(
        orders_kernel,
        out_shape=[
            jax.ShapeDtypeStruct((leaf_blocks.shape[1],), jnp.int32),
            jax.ShapeDtypeStruct((mid_blocks.shape[1],), jnp.int32),
        ],
        in_specs=[pl.BlockSpec(memory_space=pltpu.SMEM)] * 3,
        out_specs=[pl.BlockSpec(memory_space=pltpu.SMEM)] * 2,
        compiler_params=pltpu.CompilerParams(vmem_limit_bytes=1024 * 1024),
    )(ids, leaf_blocks, mid_blocks)


def fetch_kernel(start_of, chunks, rows, unit, with_child, ids, *refs):
    child = refs[0] if with_child else None
    matrix, out, sems = refs[-3:]
    copies = []
    for index, row in enumerate(Place(ids, child).starts(start_of, chunks, rows)):
        copy = pltpu.make_async_copy(
            matrix.at[:, pl.ds(pl.multiple_of(row, unit), unit), :],
            out.at[:, pl.ds(index * unit, unit), :],
            sems.at[index],
        )
        copy.start()
        copies.append(copy)
    for copy in copies:
        copy.wait()


def fetch(matrix, ids, child, start_of, chunks, rows, token):
    columns, count = matrix.shape[2], len(chunks) * rows
    unit = rows if child is None else min(BLOCK, rows)
    if not fast(rows, columns):
        starts = jnp.stack(list(Place(ids, child).starts(start_of, chunks, rows)))
        picked = (starts[:, None] + jnp.arange(unit, dtype=jnp.int32)).reshape(-1)
        return jnp.take(matrix, picked, axis=1)
    orders = [(ids, pltpu.SMEM)] + ([] if child is None else [(child, pltpu.SMEM)])
    pinned = pltpu.with_memory_space_constraint(matrix, pltpu.HBM)
    return call(
        functools.partial(fetch_kernel, start_of, chunks, rows, unit, child is not None),
        [*orders, (token, pl.ANY), (pinned, pl.ANY)],
        [jax.ShapeDtypeStruct((2, count, columns), jnp.float32)],
        [pltpu.SemaphoreType.DMA((count // unit,))],
        room=1,
    )[0]


def pass_kernel(*refs):
    del refs


def copy_kernel(*refs):
    refs[-1][...] = refs[-2][...]


def after(value, tokens, copied=False):
    if not tokens or not fast(*value.shape[-2:]):
        return value
    space = VMEM if copied else pl.ANY
    return pl.pallas_call(
        copy_kernel if copied else pass_kernel,
        out_shape=jax.ShapeDtypeStruct(value.shape, value.dtype),
        in_specs=[pl.BlockSpec(memory_space=pl.ANY)] * len(tokens)
        + [pl.BlockSpec(memory_space=space)],
        out_specs=pl.BlockSpec(memory_space=space),
        input_output_aliases={} if copied else {len(tokens): 0},
        compiler_params=pltpu.CompilerParams(vmem_limit_bytes=1024 * 1024),
        cost_estimate=pl.CostEstimate(flops=0, bytes_accessed=1024, transcendentals=0),
    )(*tokens, value)


def wide_of(real, imag):
    real_high, real_low = halves(real)
    imag_high, imag_low = halves(imag)
    return jnp.concatenate([real_high, imag_high, real_low, imag_low], axis=1)


def lift_kernel(start_of, parts, rows, begin, counts, turned, ids, *refs):
    chunk_refs, (held, *rest) = refs[: len(parts)], refs[len(parts) :]
    outs, (natural, weights) = rest[-2 - len(counts) : -2], rest[-2:]
    depth = natural.shape[0]
    step = chunk_refs[0].shape[0]
    for part, chunk in zip(parts, chunk_refs):
        place = pl.multiple_of(start_of(ids[0], *part), step)
        natural[pl.ds(place, step), :] = chunk[...]
    for half, values in enumerate((natural[...], turned_columns(natural[...]))):
        high, low = halves(values)
        both = jnp.concatenate([high, low], axis=1)
        weights[half * depth : (half + 1) * depth, :] = both
        weights[(half + 2) * depth : (half + 3) * depth, :] = both
    for out, count in zip(outs, counts):
        together = 1 if turned or count % 2 else 2
        for index in range(0, count, together):
            here = slice((begin + index) * rows, (begin + index + together) * rows)
            wide = dot32(wide_of(held[0, here], held[1, here]), weights[...])
            whole = wide[:, :BLOCK] + wide[:, BLOCK:]
            if turned:
                out[index] = whole.T
            else:
                out[index : index + together] = whole.reshape(together, rows, BLOCK)
        begin += count


def lift(held, ids, vectors, start_of, parts, rows, begin, counts, turned=False, tokens=()):
    depth, width = held.shape[2], vectors[0].shape[1]
    if not fast(rows, depth, vectors[0].shape[0]):
        whole = jnp.zeros((depth, width), jnp.float32)
        for part, chunk in zip(parts, vectors):
            whole = lax.dynamic_update_slice(whole, chunk, (start_of(ids[0], *part), 0))
        held = held[:, begin * rows : (begin + sum(counts)) * rows]
        result = exact_dot(held[0], whole) + exact_dot(held[1], turned_columns(whole))
        result = result.reshape(-1, rows, width)
        result = jnp.transpose(result, (0, 2, 1)) if turned else result
        ends = [sum(counts[: i + 1]) for i in range(len(counts))]
        return [result[end - count : end] for end, count in zip(ends, counts)]
    shape = (width, rows) if turned else (rows, width)
    return call(
        functools.partial(lift_kernel, start_of, parts, rows, begin, counts, turned),
        [
            (ids, pltpu.SMEM),
            *((chunk, VMEM) for chunk in vectors),
            (held, VMEM),
            *((token, pl.ANY) for token in tokens),
        ],
        [jax.ShapeDtypeStruct((count, *shape), jnp.float32) for count in counts],
        [VMEM((depth, BLOCK), jnp.float32), VMEM((4 * depth, 2 * BLOCK), jnp.bfloat16)],
        2 * 4 * sum(counts) * rows * depth * 2 * BLOCK,
    )


def fold_kernel(start_of, chunks, has_total, turned, ids, *refs):
    chunk_refs, (held, *rest) = refs[: len(chunks)], refs[len(chunks) :]
    outs = rest[-2:] if turned else rest[-1:]
    total = rest[0][...] if has_total else None
    depth = chunk_refs[0].shape[0]
    for chunk, chunk_ref in zip(chunks, chunk_refs):
        values = chunk_ref[...]
        high, low = halves(values)
        turned_high, turned_low = halves(turned_columns(values))
        both = jnp.concatenate(
            [
                jnp.concatenate([high, low], axis=1),
                jnp.concatenate([turned_high, turned_low], axis=1),
            ],
            axis=0,
        )
        here = pl.ds(pl.multiple_of(start_of(ids[0], ids[1], *chunk), depth), depth)
        tile = wide_of(held[0, :, here], held[1, :, here])
        wide = dot32(tile, jnp.concatenate([both, both], axis=0))
        term = wide[:, :BLOCK] + wide[:, BLOCK:]
        total = term if total is None else total + term
    outs[0][...] = total
    if turned:
        outs[1][...] = total.T


def fold(held, ids, vectors, start_of, chunks, total, turned=False):
    rows, (depth, width) = held.shape[1], vectors[0].shape
    if not fast(rows, depth):
        for chunk, values in zip(chunks, vectors):
            column = start_of(ids[0], ids[1], *chunk)
            taken = lax.dynamic_slice(held, (0, 0, column), (2, rows, depth))
            term = exact_dot(taken[0], values) + exact_dot(taken[1], turned_columns(values))
            total = term if total is None else total + term
        return (total, total.T) if turned else total
    before = [] if total is None else [(total, VMEM)]
    shapes = [(rows, width), (width, rows)] if turned else [(rows, width)]
    outs = call(
        functools.partial(fold_kernel, start_of, chunks, total is not None, turned),
        [(ids, pltpu.SMEM), *((chunk, VMEM) for chunk in vectors), (held, VMEM), *before],
        [jax.ShapeDtypeStruct(shape, jnp.float32) for shape in shapes],
        [],
        2 * 4 * len(chunks) * rows * depth * 2 * BLOCK,
    )
    return outs if turned else outs[0]


def pull_kernel(begin, picks, arrays, has_total, minus, start_of, pieces, ids, *refs):
    array_refs, (held, *rest) = refs[:arrays], refs[arrays:]
    outs, total = rest[has_total:-1], rest[-1]
    count, depth, columns = len(picks), array_refs[0].shape[-1], held.shape[2]
    chunk_refs = [
        array_refs[at] if index is None else array_refs[at].at[index] for at, index in picks
    ]
    lefts = []
    for chunk in chunk_refs:
        values = chunk[...]
        high, low = halves(values)
        turned_high, turned_low = halves(turned_rows(values))
        lefts.append(
            (
                jnp.concatenate([high, low], axis=0),
                jnp.concatenate([turned_high, turned_low], axis=0),
            )
        )
    left = [jnp.concatenate(side, axis=1) for side in zip(*lefts)]
    rows = slice(begin * depth, (begin + count) * depth)
    for at in range(0, columns, 256):
        here = slice(at, min(at + 256, columns))
        term = rest[0][:, here] if has_total else None
        for part in (0, 1):
            high, low = halves(held[part, rows, here])
            wide = dot32(left[part], high)
            thin = dot32(left[part][:BLOCK], low)
            both = wide[:BLOCK] + wide[BLOCK:] + thin
            term = both if term is None else term - both if minus else term + both
        total[:, here] = term
    if not pieces:
        outs[0][...] = total[...]
    for piece, out in zip(pieces, outs):
        place = pl.multiple_of(start_of(ids[0], *piece), out.shape[1])
        out[...] = total[:, pl.ds(place, out.shape[1])]


def pull(
    held, ids, vectors, begin, total, start_of=None, pieces=(), size=0, minus=False, hides=True
):
    vectors = [vector if isinstance(vector, tuple) else (vector, None) for vector in vectors]
    columns, (width, depth) = held.shape[2], vectors[0][0].shape[-2:]
    if not fast(columns, depth):
        values = jnp.concatenate(
            [array if index is None else array[index] for array, index in vectors], axis=1
        )
        held = held[:, begin * depth : (begin + len(vectors)) * depth]
        term = exact_dot(values, held[0]) + exact_dot(turned_rows(values), held[1])
        total = term if total is None else total - term if minus else total + term
        if not pieces:
            return total
        return [
            lax.dynamic_slice(total, (0, start_of(ids[0], *piece)), (width, size))
            for piece in pieces
        ]
    before = [] if total is None else [(total, VMEM)]
    shapes = [(width, size)] * len(pieces) if pieces else [(width, columns)]
    arrays = list({id(array): array for array, _ in vectors}.values())
    at = {id(array): place for place, array in enumerate(arrays)}
    picks = [(at[id(array)], index) for array, index in vectors]
    outs = call(
        functools.partial(
            pull_kernel, begin, picks, len(arrays), total is not None, minus, start_of, pieces
        ),
        [(ids, pltpu.SMEM), *((array, VMEM) for array in arrays), (held, VMEM), *before],
        [jax.ShapeDtypeStruct(shape, jnp.float32) for shape in shapes],
        [VMEM((width, columns), jnp.float32)],
        2 * 3 * len(vectors) * depth * columns * 2 * BLOCK,
        hides=hides,
    )
    return outs if pieces else outs[0]


def spread_kernel(start_of, chunks, ids, vectors, held, *refs):
    outs = refs[-len(chunks) :]
    size = outs[0].shape[0]
    values = vectors[...]
    high, low = halves(values)
    turned_high, turned_low = halves(turned_rows(values))
    left = (
        jnp.concatenate([high, low], axis=0),
        jnp.concatenate([turned_high, turned_low], axis=0),
    )
    for chunk, out in zip(chunks, outs):
        here = pl.ds(pl.multiple_of(start_of(ids[0], ids[1], *chunk), size), size)
        term = None
        for part in (0, 1):
            high, low = halves(held[part, :, here])
            wide = dot32(left[part], high)
            thin = dot32(left[part][:BLOCK], low)
            both = wide[:BLOCK] + wide[BLOCK:] + thin
            term = both if term is None else term + both
        out[...] = term.T


def spread(held, ids, vectors, start_of, chunks, size):
    width, depth = vectors.shape
    if not fast(depth, size):
        whole = exact_dot(vectors, held[0]) + exact_dot(turned_rows(vectors), held[1])
        return [
            lax.dynamic_slice(whole, (0, start_of(ids[0], ids[1], *chunk)), (width, size)).T
            for chunk in chunks
        ]
    return call(
        functools.partial(spread_kernel, start_of, chunks),
        [(ids, pltpu.SMEM), (vectors, VMEM), (held, VMEM)],
        [jax.ShapeDtypeStruct((size, width), jnp.float32)] * len(chunks),
        [],
        2 * 3 * len(chunks) * depth * size * 2 * BLOCK,
    )


def add_kernel(indices, base_start, turned, *refs):
    outs = refs[-2:] if turned else refs[-1:]
    ids, base, *arrays = refs if base_start is not None else (None, None, *refs)
    total = None
    for index, ref in zip(indices, arrays):
        term = ref[...] if index is None else ref[index]
        total = term if total is None else total + term
    if base_start is not None:
        rows = total.shape[0]
        start = pl.multiple_of(base_start(ids[0]), rows)
        total = base[pl.ds(start, rows), :] - total
    outs[0][...] = total
    if turned:
        outs[1][...] = total.T


def add(terms, base=None, tokens=(), turned=False):
    arrays, indices = zip(*terms)
    shape = arrays[0].shape[-2:]
    if isinstance(indices[0], slice):
        shape = (indices[0].stop, *shape)
    if not fast(*shape[-2:]):
        total = sum(array if index is None else array[index] for array, index in terms)
        if base is not None:
            total = lax.dynamic_slice(base[1], (base[2](base[0][0]), 0), shape) - total
        return (total, total.T) if turned else total
    bases = [] if base is None else [(base[0], pltpu.SMEM), (base[1], VMEM)]
    shapes = [shape, shape[::-1]] if turned else [shape]
    outs = call(
        functools.partial(add_kernel, indices, None if base is None else base[2], turned),
        [*bases, *((array, VMEM) for array in arrays), *((token, pl.ANY) for token in tokens)],
        [jax.ShapeDtypeStruct(extent, jnp.float32) for extent in shapes],
        room=2,
    )
    return outs if turned else outs[0]


def settle_kernel(indices, ids, *refs):
    out = refs[-1]
    for leaf, (index, chunk) in enumerate(zip(indices, refs[:-1])):
        rows = chunk.shape[-1]
        place = pl.multiple_of((ids[0] ^ leaf) * rows, rows)
        out[pl.ds(place, rows), :] = (chunk[...] if index is None else chunk[index]).T


def settle(ids, chunks):
    chunks = [chunk if isinstance(chunk, tuple) else (chunk, None) for chunk in chunks]
    width, rows = chunks[0][0].shape[-2:]
    if not fast(width, rows):
        chunks = [array if index is None else array[index] for array, index in chunks]
        natural = jnp.take(jnp.stack(chunks), jnp.arange(len(chunks), dtype=jnp.int32) ^ ids[0], axis=0)
        return jnp.transpose(natural, (0, 2, 1)).reshape(-1, width)
    return call(
        functools.partial(settle_kernel, [index for _, index in chunks]),
        [(ids, pltpu.SMEM), *((array, VMEM) for array, _ in chunks)],
        [jax.ShapeDtypeStruct((len(chunks) * rows, width), jnp.float32)],
    )[0]


def swap(value, leaf_bits, front_bits):
    groups, fronts = lax.axis_size("leaf"), lax.axis_size("front")
    pairs = [
        (leaf * fronts + front, (leaf ^ leaf_bits) * fronts + (front ^ front_bits))
        for leaf in range(groups)
        for front in range(fronts)
    ]
    return lax.ppermute(value, ("leaf", "front"), pairs)


def across(value):
    return swap(value, 0, 1)


def along(value, apart):
    return swap(value, 0, 2 * apart)


def sibling(value):
    return swap(value, 1, 0)


def opposite(value):
    return swap(value, 2, 0)


def spread_chain(own, errands=(), with_beside=True, first_ready=()):
    held, apart = {0: own}, lax.axis_size("front") // 4
    errands, done, beside = list(errands), [], {}
    while apart:
        far = {place | apart: along(value, apart) for place, value in held.items()}
        ready = list(errands.pop(0)(own)) if errands else []
        done.append(list(ready))
        if len(done) == 1:
            ready += first_ready
        if with_beside:
            place = apart if len(done) > 1 else 0
            beside[place] = across(held[place] if place in held else far[place])
            ready.append(beside[place])
        if len(done) == 1 and apart > 1:
            near = along(own, apart // 2)
            ready.append(near)
        far[max(far)] = after(far[max(far)], ready)
        if len(done) == 2:
            far[apart] = near
        held.update(far)
        apart //= 2
    if with_beside:
        beside = {place: beside[place] if place in beside else across(held[place]) for place in held}
    return held, beside, done


def sum_chain(pieces, errands=(), first=(), sent=None, **last):
    count, errands, done = len(pieces), list(errands), []
    terms = {
        place: kept if given is None else [*kept, (across(given), None)]
        for place, (kept, given) in pieces.items()
    }
    apart, ready = 1, list(first)
    while apart < count:
        top = max(place for place in range(apart, count, 2 * apart))
        for place in reversed(range(apart, count, 2 * apart)):
            if sent is not None and place == count - 1:
                summed, received = sent
            else:
                summed = add(terms[place], tokens=ready if place == top else ())
                received = along(summed, apart)
            token = summed if place == top else token
            terms[place - apart] = [*terms[place - apart], (received, None)]
        ready = errands.pop(0)(token) if errands else []
        done.append(ready)
        apart *= 2
    return add(terms[0], tokens=ready, **last), done


def ways(place):
    return ((across, opposite), (1, 0), (0, 2)) if place % 2 else ((opposite, across), (0, 2), (1, 0))


def body(
    leaf_source,
    mid_source,
    root_source,
    leaf_inverse,
    leaf_coupling,
    mid_inverse,
    mid_coupling,
    root_inverse,
    leaf_blocks,
    mid_blocks,
):
    fronts = lax.axis_size("front")
    places = list(range(fronts // 2))
    downward = places[::-1]
    group, front = lax.axis_index("leaf"), lax.axis_index("front")
    ids = jnp.stack([group, front]).astype(jnp.int32)
    source_two, source_one = leaf_source[0], mid_source[0]
    inverse_two, coupling_two = leaf_inverse[0], leaf_coupling[0]
    inverse_one, coupling_one = mid_inverse[0], mid_coupling[0]
    rows_two = source_two.shape[0]
    half = source_one.shape[0]
    root_block = root_source.shape[0]
    quarter = root_block // lax.axis_size("leaf")
    root_rows = root_inverse.shape[1] // fronts

    child_two, child_one = orders(ids, leaf_blocks, mid_blocks)

    def two_start(group, front, leaf_bits, front_bits):
        return (front ^ front_bits) * rows_two

    def half_start(group, front, leaf_bits, front_bits):
        return (front ^ front_bits) * (2 * half) + ((group ^ leaf_bits) % 2) * half

    def one_start(group, front, leaf_bits, front_bits):
        return (front ^ front_bits) * half

    def quarter_start(group, front, leaf_bits, front_bits):
        return (front ^ front_bits) * root_block + (group ^ leaf_bits) * quarter

    def root_start(group, front, leaf_bits, front_bits):
        return (front ^ front_bits) * root_rows

    def whole_start(group, front):
        return 0

    def first_row(group):
        return 0

    def own_row(group):
        return group * quarter

    def side_row(group, bits):
        return ((group ^ bits) % 2) * half

    def leaf_row(group, bits):
        return (group ^ bits) * quarter

    def pair(place, leaf_bits=0):
        return [(leaf_bits, 2 * place + 1), (leaf_bits, 2 * place)]

    def arrivals(place, groups=(0,)):
        return [(leaf_bits, 2 * place + other) for other in (0, 1) for leaf_bits in groups]

    def square(place):
        _, first, second = ways(place)
        return [
            (first[1] | second[1], 2 * place + (first[0] | second[0])),
            (first[1], 2 * place + first[0]),
            (second[1], 2 * place + second[0]),
            (0, 2 * place),
        ]

    def square_both(place):
        return [(bits ^ 1, other) for bits, other in square(place)] + square(place)

    def square_arrivals(place):
        return [(bits ^ other, at) for bits, at in square(place)[::-1] for other in (0, 1)]

    count = len(places)
    early, late = downward[: count // 2], downward[count // 2 :]
    near, far = places[: count // 2], places[count // 2 :]

    def chunks_of(which, chunks):
        return [chunk for place in which for chunk in chunks(place)]

    def leaf_inverse_rows(token):
        return fetch(inverse_two, ids, None, whole_start, [()], inverse_two.shape[1], token)

    def leaf_lift_rows(which, token):
        chunks = chunks_of(which, lambda place: pair(place, 1)) + chunks_of(which, pair)
        return fetch(coupling_two, ids, child_two, half_start, chunks, half, token)

    def mid_lift_rows(which, token):
        return fetch(inverse_one, ids, None, one_start, chunks_of(which, pair), half, token)

    def root_lift_rows(which, token):
        chunks = chunks_of(which, square_both)
        return fetch(coupling_one, ids, child_one, quarter_start, chunks, quarter, token)

    def root_rows_of(which, token):
        return fetch(root_inverse, ids, None, root_start, chunks_of(which, pair), root_rows, token)

    def root_pull_rows(which, token):
        chunks = chunks_of(which, square_arrivals)
        return fetch(coupling_one, ids, child_one, quarter_start, chunks, quarter, token)

    def mid_pull_rows(which, token):
        return fetch(inverse_one, ids, None, one_start, chunks_of(which, arrivals), half, token)

    def leaf_pull_rows(which, token):
        chunks = chunks_of(which, lambda place: arrivals(place, (0, 1)))
        return fetch(coupling_two, ids, child_two, half_start, chunks, half, token)

    chain, beside, ((rows_inverse,), (rows_early,), *_) = spread_chain(
        source_two,
        [
            lambda token: [leaf_inverse_rows(token)],
            lambda token: [leaf_lift_rows(early, token)],
        ],
    )
    rows_late = leaf_lift_rows(late, rows_early)
    coming = [vector for place in places for vector in (chain[place], beside[place])]
    coming_chunks = chunks_of(places, arrivals)
    total = None
    for first, end in ((0, fronts // 2), (fronts // 2, fronts - 1), (fronts - 1, fronts)):
        last = end == fronts
        if last:
            coming[-1] = after(coming[-1], [rows_late])
        total = fold(
            rows_inverse, ids, coming[first:end], two_start, coming_chunks[first:end], total, last
        )
    solved_two, solved_two_turned = total

    def leaf_lift(held, which):
        size = 2 * len(which)
        theirs, mine = lift(held, ids, [solved_two], first_row, [()], half, 0, [size, size])
        theirs, terms = sibling(theirs), {}
        for at, place in enumerate(which):
            given = add([(mine, 2 * at), (theirs, 2 * at)])
            terms[place] = [(mine, 2 * at + 1), (theirs, 2 * at + 1)], given
        return terms, mine

    terms, _ = leaf_lift(rows_early, early)
    more, token = leaf_lift(rows_late, late)
    rows_one_early = mid_lift_rows(early, token)
    own_half, (_, (rows_one_late,), *_) = sum_chain(
        {**terms, **more},
        [lambda token: [], lambda token: [mid_lift_rows(late, token)]],
        [rows_one_early],
        base=(ids, source_one, first_row),
    )

    halves_one = [own_half, sibling(own_half)]

    def paired(which, parts):
        return {
            place: ([(kept, 0 if kept.ndim > 2 else None)], given.reshape(given.shape[-2:]))
            for place, given, kept in zip(which, parts[0::2], parts[1::2])
        }

    def mid_lift(held, which):
        ones = [1] * (2 * len(which))
        return lift(held, ids, halves_one, side_row, [(0,), (1,)], half, 0, ones)

    parts, more = mid_lift(rows_one_early, early), mid_lift(rows_one_late, late)
    (solved_one, solved_one_turned), (_, (rows_early,), *_) = sum_chain(
        {**paired(early, parts), **paired(late, more)},
        [lambda token: [], lambda token: [root_lift_rows(early, token)]],
        more[:1],
        turned=True,
    )

    def root_lift(held, begin, which, tokens=()):
        fours = [4] * (2 * len(which))
        return lift(
            held,
            ids,
            [solved_one],
            first_row,
            [()],
            quarter,
            8 * begin,
            fours,
            tokens=tokens,
        )

    def corner_terms(place, theirs, mine, tokens=()):
        (first_way, second_way), _, _ = ways(place)
        outer = add([(mine, slice(0, 2)), (theirs, slice(0, 2))], tokens=tokens)
        outer = first_way(outer)
        inner = second_way(add([(mine, 2), (theirs, 2), (outer, 0)]))
        return ([(mine, 3), (theirs, 3), (outer, 1), (inner, None)], None), outer

    top, *rest = early
    (first_way, second_way), _, _ = ways(top)
    theirs, mine = root_lift(rows_early, 0, [top])
    theirs = sibling(theirs)
    parts = [part for at, place in enumerate(rest) for part in root_lift(rows_early, at + 1, [place])]
    corner = add([(mine, 0), (theirs, 0)], tokens=parts[-1:])
    rows_late = root_lift_rows(late, corner)
    first = first_way(add([(mine, 1), (theirs, 1)]))
    inner = add([(mine, 2), (theirs, 2), (first_way(corner), None)], tokens=[rows_late])
    parts += root_lift(rows_late, 0, late, [inner])
    sent, inner = inner, second_way(inner)
    last = inner
    summed = add([(mine, 3), (theirs, 3), (first, None), (inner, None)])
    carried = along(summed, 1)
    corners = {top: ((), None)}
    ready = [inner, first]
    for place, theirs, mine in zip(rest + late, parts[0::2], parts[1::2]):
        theirs = sibling(theirs if place in rest else after(theirs, ready))
        corners[place], outer = corner_terms(place, theirs, mine, [sent] if place in rest else ())
        last = outer if place in rest else last
        ready = [last, carried] if place == 1 else ready
    own_quarter, ((rows_root_early,), (rows_root_late,), *_) = sum_chain(
        corners,
        [
            lambda token: [root_rows_of(early, token)],
            lambda token: [root_rows_of(late, token)],
        ],
        sent=(summed, carried),
        base=(ids, root_source, own_row),
    )
    over_quarter = opposite(own_quarter)
    quarters = [own_quarter, over_quarter, sibling(own_quarter), sibling(over_quarter)]

    def root_apply(held, which):
        ones, parts = [1] * (2 * len(which)), [(0,), (2,), (1,), (3,)]
        return lift(held, ids, quarters, leaf_row, parts, root_rows, 0, ones, turned=True)

    parts, more = root_apply(rows_root_early, early), root_apply(rows_root_late, late)
    whole_root, (_, (rows_near,), *_) = sum_chain(
        {**paired(early, parts), **paired(late, more)},
        [lambda token: [], lambda token: [root_pull_rows(near, token)]],
        more[:1],
    )
    chain, beside, ((rows_far,), (rows_one_near,), *_) = spread_chain(
        whole_root,
        [
            lambda token: [root_pull_rows(far, token)],
            lambda token: [mid_pull_rows(near, token)],
        ],
    )
    late_vectors = [vector for place in late for vector in (beside[place], chain[place])]
    early_vectors = [vector for place in early for vector in (beside[place], chain[place])]
    total = pull(rows_root_late, ids, late_vectors, 0, None)
    total = pull(rows_root_early, ids, early_vectors[1:], 1, total)
    theirs_own, theirs_over, mine_own, mine_over = pull(
        rows_root_early, ids, early_vectors[:1], 0, total, leaf_row, [(1,), (3,), (0,), (2,)], quarter
    )
    rows_one_far = mid_pull_rows(far, mine_own)
    over = add([(mine_over, None), (sibling(theirs_over), None)])
    theirs_own = sibling(theirs_own)
    own_quarter = add(
        [(mine_own, None), (theirs_own, None), (opposite(over), None)], tokens=[rows_one_far]
    )

    def corner_values(place, value, ready=()):
        (first_way, second_way), _, _ = ways(place)
        first, second = first_way(value), second_way(value)
        return [value, second, first, second_way(after(first, ready))]

    corners = {0: corner_values(0, own_quarter)}
    chain, _, _ = spread_chain(own_quarter, (), False, corners[0][1:3])
    for place in places[1:-1]:
        value = chain[place]
        if place == count // 2:
            value = after(value, [chain[places[-1]]], copied=True)
        corners[place] = corner_values(place, value)
    def with_theirs(values):
        theirs = sibling(jnp.stack(values)) if len(values) > 1 else sibling(values[0])
        theirs = [(theirs, at) for at in range(len(values))] if len(values) > 1 else [theirs]
        return [vector for both in zip(values, theirs) for vector in both]

    def pull_one(place, vectors, first, total):
        held, begin = (rows_near, 8 * place) if place in near else (rows_far, 8 * (place - len(near)))
        return pull(held, ids, vectors, begin + first, total, minus=True, hides=False)

    rest_one = solved_one_turned
    for place in places[:-1]:
        vectors = with_theirs(corners[place])
        if place == 0:
            at = 4 if ways(place)[1][1] else 2
            root_solution = settle(ids, [*vectors[:2], *vectors[at : at + 2]])
        rest_one = pull_one(place, vectors, 0, rest_one)
        if place == 0:
            value = after(chain[places[-1]], corners[1][1:3])
            corners[places[-1]] = corner_values(places[-1], value)
    rest_one = pull_one(places[-1], with_theirs(corners[places[-1]][:3]), 0, rest_one)
    corner = after(corners[places[-1]][3], [rest_one])
    rest_one = pull_one(places[-1], with_theirs([corner]), 6, rest_one)
    chain, beside, ((rows_near,), (rows_far,), *_) = spread_chain(
        rest_one,
        [
            lambda token: [leaf_pull_rows(near, token)],
            lambda token: [leaf_pull_rows(far, token)],
        ],
    )
    near_vectors = [vector for place in near for vector in (chain[place], beside[place])]
    far_vectors = [vector for place in far for vector in (chain[place], beside[place])]
    total = pull(rows_one_near, ids, near_vectors, 0, None)
    total = pull(rows_one_far, ids, far_vectors[:-1], 0, total)
    theirs, mine = pull(
        rows_one_far, ids, far_vectors[-1:], len(far_vectors) - 1, total, side_row, [(1,), (0,)], half
    )
    mid_columns, mid_solution = add([(mine, None), (sibling(theirs), None)], turned=True)

    chain, beside, ((rows_inverse,), *_) = spread_chain(
        mid_columns, [lambda token: [leaf_inverse_rows(token)], lambda token: [root_solution]]
    )
    near_values = [value for place in near for value in (chain[place], beside[place])]
    far_values = [value for place in far for value in (chain[place], beside[place])]
    rest_two = pull(rows_near, ids, with_theirs(near_values), 0, solved_two_turned, minus=True)
    rest_two = pull(rows_far, ids, with_theirs(far_values[:-1]), 0, rest_two, minus=True)
    vectors = with_theirs([after(far_values[-1], [rest_two])])
    rest_two = pull(rows_far, ids, vectors, 2 * len(far_values) - 2, rest_two, minus=True)

    def leaf_spread(which):
        return spread(rows_inverse, ids, rest_two, two_start, chunks_of(which, pair), rows_two)

    parts, more = leaf_spread(early), leaf_spread(late)
    leaf_solution, _ = sum_chain({**paired(early, parts), **paired(late, more)}, (), more[:1])
    return (leaf_solution[None], mid_solution[None], root_solution)


def solution(mesh):
    placed = (
        P("leaf", "front", None),
        P("leaf", "front", None),
        P("front", None),
        P("leaf", None, "front", None),
        P("leaf", None, None, "front"),
        P("leaf", None, None, "front"),
        P("leaf", None, None, "front"),
        P(None, "leaf", "front"),
        P("leaf", None),
        P(),
    )
    return jax.shard_map(
        body,
        mesh=mesh,
        in_specs=placed,
        out_specs=(P("leaf", "front", None), P("leaf", "front", None), P("front", None)),
        check_vma=False,
    )
```

```python
import functools
import math

import jax
import jax.numpy as jnp
from jax import lax
from jax.experimental import pallas as pl
from jax.experimental.pallas import tpu as pltpu
from jax.sharding import PartitionSpec as P

BLOCK = 128
VMEM = pltpu.VMEM
exact_dot = functools.partial(jnp.dot, precision=lax.Precision.HIGHEST)


def halves(values):
    high = values.astype(jnp.bfloat16)
    low = (values - high.astype(jnp.float32)).astype(jnp.bfloat16)
    return high, low


def turned_columns(vectors):
    width = vectors.shape[1] // 2
    return jnp.concatenate([-vectors[:, width:], vectors[:, :width]], axis=1)


def turned_rows(vectors):
    width = vectors.shape[0] // 2
    return jnp.concatenate([-vectors[width:], vectors[:width]], axis=0)


def dot32(left, right):
    return jnp.dot(left, right, preferred_element_type=jnp.float32)


def fast(*extents):
    return all(extent % BLOCK == 0 for extent in extents)


def call(kernel, operands, outs, scratch=(), flops=0, room=10, hides=True):
    arrays, spaces = zip(*operands)
    size = lambda a: math.prod(a.shape) * a.dtype.itemsize
    held = sum(size(a) for a, space in operands if space == VMEM) + sum(size(o) for o in outs)
    scratch_bytes = sum(size(s) for s in scratch if hasattr(s, "shape") and s.memory_space == VMEM)
    moved = held if any(space == VMEM for space in spaces) else 2 * held
    flops, moved = (flops, moved) if hides else (1024, 1024)
    return pl.pallas_call(
        kernel,
        out_shape=outs,
        in_specs=[pl.BlockSpec(memory_space=space) for space in spaces],
        out_specs=[pl.BlockSpec(memory_space=VMEM)] * len(outs),
        scratch_shapes=scratch,
        compiler_params=pltpu.CompilerParams(
            vmem_limit_bytes=scratch_bytes + room * 1024 * 1024
        ),
        cost_estimate=pl.CostEstimate(flops=flops, bytes_accessed=moved, transcendentals=0),
    )(*arrays)


class Place:
    def __init__(self, ids, child):
        self.ids, self.child = ids, child

    def starts(self, start_of, chunks, rows):
        group, front = self.ids[0], self.ids[1]
        unit = rows if self.child is None else min(BLOCK, rows)
        for chunk in chunks:
            start = start_of(group, front, *chunk)
            for inner in range(0, rows, unit):
                row = start + inner
                if self.child is not None:
                    row = self.child[row // BLOCK] * BLOCK + row % BLOCK
                yield row


def orders_kernel(ids, leaf_blocks, mid_blocks, child_two, child_one):
    for index in range(leaf_blocks.shape[1]):
        child_two[leaf_blocks[0, index]] = index
    row = lax.shift_right_logical(ids[0], 1)
    for index in range(mid_blocks.shape[1]):
        child_one[mid_blocks[row, index]] = index


def orders(ids, leaf_blocks, mid_blocks):
    return pl.pallas_call(
        orders_kernel,
        out_shape=[
            jax.ShapeDtypeStruct((leaf_blocks.shape[1],), jnp.int32),
            jax.ShapeDtypeStruct((mid_blocks.shape[1],), jnp.int32),
        ],
        in_specs=[pl.BlockSpec(memory_space=pltpu.SMEM)] * 3,
        out_specs=[pl.BlockSpec(memory_space=pltpu.SMEM)] * 2,
        compiler_params=pltpu.CompilerParams(vmem_limit_bytes=1024 * 1024),
    )(ids, leaf_blocks, mid_blocks)


def fetch_kernel(start_of, chunks, rows, unit, with_child, ids, *refs):
    child = refs[0] if with_child else None
    matrix, out, sems = refs[-3:]
    copies = []
    for index, row in enumerate(Place(ids, child).starts(start_of, chunks, rows)):
        copy = pltpu.make_async_copy(
            matrix.at[:, pl.ds(pl.multiple_of(row, unit), unit), :],
            out.at[:, pl.ds(index * unit, unit), :],
            sems.at[index],
        )
        copy.start()
        copies.append(copy)
    for copy in copies:
        copy.wait()


def fetch(matrix, ids, child, start_of, chunks, rows, token):
    columns, count = matrix.shape[2], len(chunks) * rows
    unit = rows if child is None else min(BLOCK, rows)
    if not fast(rows, columns):
        starts = jnp.stack(list(Place(ids, child).starts(start_of, chunks, rows)))
        picked = (starts[:, None] + jnp.arange(unit, dtype=jnp.int32)).reshape(-1)
        return jnp.take(matrix, picked, axis=1)
    orders = [(ids, pltpu.SMEM)] + ([] if child is None else [(child, pltpu.SMEM)])
    pinned = pltpu.with_memory_space_constraint(matrix, pltpu.HBM)
    return call(
        functools.partial(fetch_kernel, start_of, chunks, rows, unit, child is not None),
        [*orders, (token, pl.ANY), (pinned, pl.ANY)],
        [jax.ShapeDtypeStruct((2, count, columns), jnp.float32)],
        [pltpu.SemaphoreType.DMA((count // unit,))],
        room=1,
    )[0]


def pass_kernel(*refs):
    del refs


def copy_kernel(*refs):
    refs[-1][...] = refs[-2][...]


def after(value, tokens, copied=False):
    if not tokens or not fast(*value.shape[-2:]):
        return value
    space = VMEM if copied else pl.ANY
    return pl.pallas_call(
        copy_kernel if copied else pass_kernel,
        out_shape=jax.ShapeDtypeStruct(value.shape, value.dtype),
        in_specs=[pl.BlockSpec(memory_space=pl.ANY)] * len(tokens)
        + [pl.BlockSpec(memory_space=space)],
        out_specs=pl.BlockSpec(memory_space=space),
        input_output_aliases={} if copied else {len(tokens): 0},
        compiler_params=pltpu.CompilerParams(vmem_limit_bytes=1024 * 1024),
        cost_estimate=pl.CostEstimate(flops=0, bytes_accessed=1024, transcendentals=0),
    )(*tokens, value)


def wide_of(real, imag):
    real_high, real_low = halves(real)
    imag_high, imag_low = halves(imag)
    return jnp.concatenate([real_high, imag_high, real_low, imag_low], axis=1)


def lift_kernel(start_of, parts, rows, begin, counts, turned, ids, *refs):
    chunk_refs, (held, *rest) = refs[: len(parts)], refs[len(parts) :]
    outs, (natural, weights) = rest[-2 - len(counts) : -2], rest[-2:]
    depth = natural.shape[0]
    step = chunk_refs[0].shape[0]
    for part, chunk in zip(parts, chunk_refs):
        place = pl.multiple_of(start_of(ids[0], *part), step)
        natural[pl.ds(place, step), :] = chunk[...]
    for half, values in enumerate((natural[...], turned_columns(natural[...]))):
        high, low = halves(values)
        both = jnp.concatenate([high, low], axis=1)
        weights[half * depth : (half + 1) * depth, :] = both
        weights[(half + 2) * depth : (half + 3) * depth, :] = both
    for out, count in zip(outs, counts):
        together = 1 if turned or count % 2 else 2
        for index in range(0, count, together):
            here = slice((begin + index) * rows, (begin + index + together) * rows)
            wide = dot32(wide_of(held[0, here], held[1, here]), weights[...])
            whole = wide[:, :BLOCK] + wide[:, BLOCK:]
            if turned:
                out[index] = whole.T
            else:
                out[index : index + together] = whole.reshape(together, rows, BLOCK)
        begin += count


def lift(held, ids, vectors, start_of, parts, rows, begin, counts, turned=False, tokens=()):
    depth, width = held.shape[2], vectors[0].shape[1]
    if not fast(rows, depth, vectors[0].shape[0]):
        whole = jnp.zeros((depth, width), jnp.float32)
        for part, chunk in zip(parts, vectors):
            whole = lax.dynamic_update_slice(whole, chunk, (start_of(ids[0], *part), 0))
        held = held[:, begin * rows : (begin + sum(counts)) * rows]
        result = exact_dot(held[0], whole) + exact_dot(held[1], turned_columns(whole))
        result = result.reshape(-1, rows, width)
        result = jnp.transpose(result, (0, 2, 1)) if turned else result
        ends = [sum(counts[: i + 1]) for i in range(len(counts))]
        return [result[end - count : end] for end, count in zip(ends, counts)]
    shape = (width, rows) if turned else (rows, width)
    return call(
        functools.partial(lift_kernel, start_of, parts, rows, begin, counts, turned),
        [
            (ids, pltpu.SMEM),
            *((chunk, VMEM) for chunk in vectors),
            (held, VMEM),
            *((token, pl.ANY) for token in tokens),
        ],
        [jax.ShapeDtypeStruct((count, *shape), jnp.float32) for count in counts],
        [VMEM((depth, BLOCK), jnp.float32), VMEM((4 * depth, 2 * BLOCK), jnp.bfloat16)],
        2 * 4 * sum(counts) * rows * depth * 2 * BLOCK,
    )


def fold_kernel(start_of, chunks, has_total, turned, ids, *refs):
    chunk_refs, (held, *rest) = refs[: len(chunks)], refs[len(chunks) :]
    outs = rest[-2:] if turned else rest[-1:]
    total = rest[0][...] if has_total else None
    depth = chunk_refs[0].shape[0]
    for chunk, chunk_ref in zip(chunks, chunk_refs):
        values = chunk_ref[...]
        high, low = halves(values)
        turned_high, turned_low = halves(turned_columns(values))
        both = jnp.concatenate(
            [
                jnp.concatenate([high, low], axis=1),
                jnp.concatenate([turned_high, turned_low], axis=1),
            ],
            axis=0,
        )
        here = pl.ds(pl.multiple_of(start_of(ids[0], ids[1], *chunk), depth), depth)
        tile = wide_of(held[0, :, here], held[1, :, here])
        wide = dot32(tile, jnp.concatenate([both, both], axis=0))
        term = wide[:, :BLOCK] + wide[:, BLOCK:]
        total = term if total is None else total + term
    outs[0][...] = total
    if turned:
        outs[1][...] = total.T


def fold(held, ids, vectors, start_of, chunks, total, turned=False):
    rows, (depth, width) = held.shape[1], vectors[0].shape
    if not fast(rows, depth):
        for chunk, values in zip(chunks, vectors):
            column = start_of(ids[0], ids[1], *chunk)
            taken = lax.dynamic_slice(held, (0, 0, column), (2, rows, depth))
            term = exact_dot(taken[0], values) + exact_dot(taken[1], turned_columns(values))
            total = term if total is None else total + term
        return (total, total.T) if turned else total
    before = [] if total is None else [(total, VMEM)]
    shapes = [(rows, width), (width, rows)] if turned else [(rows, width)]
    outs = call(
        functools.partial(fold_kernel, start_of, chunks, total is not None, turned),
        [(ids, pltpu.SMEM), *((chunk, VMEM) for chunk in vectors), (held, VMEM), *before],
        [jax.ShapeDtypeStruct(shape, jnp.float32) for shape in shapes],
        [],
        2 * 4 * len(chunks) * rows * depth * 2 * BLOCK,
    )
    return outs if turned else outs[0]


def pull_kernel(begin, picks, arrays, has_total, minus, start_of, pieces, ids, *refs):
    array_refs, (held, *rest) = refs[:arrays], refs[arrays:]
    outs, total = rest[has_total:-1], rest[-1]
    count, depth, columns = len(picks), array_refs[0].shape[-1], held.shape[2]
    chunk_refs = [
        array_refs[at] if index is None else array_refs[at].at[index] for at, index in picks
    ]
    lefts = []
    for chunk in chunk_refs:
        values = chunk[...]
        high, low = halves(values)
        turned_high, turned_low = halves(turned_rows(values))
        lefts.append(
            (
                jnp.concatenate([high, low], axis=0),
                jnp.concatenate([turned_high, turned_low], axis=0),
            )
        )
    left = [jnp.concatenate(side, axis=1) for side in zip(*lefts)]
    rows = slice(begin * depth, (begin + count) * depth)
    for at in range(0, columns, 256):
        here = slice(at, min(at + 256, columns))
        term = rest[0][:, here] if has_total else None
        for part in (0, 1):
            high, low = halves(held[part, rows, here])
            wide = dot32(left[part], high)
            thin = dot32(left[part][:BLOCK], low)
            both = wide[:BLOCK] + wide[BLOCK:] + thin
            term = both if term is None else term - both if minus else term + both
        total[:, here] = term
    if not pieces:
        outs[0][...] = total[...]
    for piece, out in zip(pieces, outs):
        place = pl.multiple_of(start_of(ids[0], *piece), out.shape[1])
        out[...] = total[:, pl.ds(place, out.shape[1])]


def pull(
    held, ids, vectors, begin, total, start_of=None, pieces=(), size=0, minus=False, hides=True
):
    vectors = [vector if isinstance(vector, tuple) else (vector, None) for vector in vectors]
    columns, (width, depth) = held.shape[2], vectors[0][0].shape[-2:]
    if not fast(columns, depth):
        values = jnp.concatenate(
            [array if index is None else array[index] for array, index in vectors], axis=1
        )
        held = held[:, begin * depth : (begin + len(vectors)) * depth]
        term = exact_dot(values, held[0]) + exact_dot(turned_rows(values), held[1])
        total = term if total is None else total - term if minus else total + term
        if not pieces:
            return total
        return [
            lax.dynamic_slice(total, (0, start_of(ids[0], *piece)), (width, size))
            for piece in pieces
        ]
    before = [] if total is None else [(total, VMEM)]
    shapes = [(width, size)] * len(pieces) if pieces else [(width, columns)]
    arrays = list({id(array): array for array, _ in vectors}.values())
    at = {id(array): place for place, array in enumerate(arrays)}
    picks = [(at[id(array)], index) for array, index in vectors]
    outs = call(
        functools.partial(
            pull_kernel, begin, picks, len(arrays), total is not None, minus, start_of, pieces
        ),
        [(ids, pltpu.SMEM), *((array, VMEM) for array in arrays), (held, VMEM), *before],
        [jax.ShapeDtypeStruct(shape, jnp.float32) for shape in shapes],
        [VMEM((width, columns), jnp.float32)],
        2 * 3 * len(vectors) * depth * columns * 2 * BLOCK,
        hides=hides,
    )
    return outs if pieces else outs[0]


def spread_kernel(start_of, chunks, ids, vectors, held, *refs):
    outs = refs[-len(chunks) :]
    size = outs[0].shape[0]
    values = vectors[...]
    high, low = halves(values)
    turned_high, turned_low = halves(turned_rows(values))
    left = (
        jnp.concatenate([high, low], axis=0),
        jnp.concatenate([turned_high, turned_low], axis=0),
    )
    for chunk, out in zip(chunks, outs):
        here = pl.ds(pl.multiple_of(start_of(ids[0], ids[1], *chunk), size), size)
        term = None
        for part in (0, 1):
            high, low = halves(held[part, :, here])
            wide = dot32(left[part], high)
            thin = dot32(left[part][:BLOCK], low)
            both = wide[:BLOCK] + wide[BLOCK:] + thin
            term = both if term is None else term + both
        out[...] = term.T


def spread(held, ids, vectors, start_of, chunks, size):
    width, depth = vectors.shape
    if not fast(depth, size):
        whole = exact_dot(vectors, held[0]) + exact_dot(turned_rows(vectors), held[1])
        return [
            lax.dynamic_slice(whole, (0, start_of(ids[0], ids[1], *chunk)), (width, size)).T
            for chunk in chunks
        ]
    return call(
        functools.partial(spread_kernel, start_of, chunks),
        [(ids, pltpu.SMEM), (vectors, VMEM), (held, VMEM)],
        [jax.ShapeDtypeStruct((size, width), jnp.float32)] * len(chunks),
        [],
        2 * 3 * len(chunks) * depth * size * 2 * BLOCK,
    )


def add_kernel(indices, base_start, turned, *refs):
    outs = refs[-2:] if turned else refs[-1:]
    ids, base, *arrays = refs if base_start is not None else (None, None, *refs)
    total = None
    for index, ref in zip(indices, arrays):
        term = ref[...] if index is None else ref[index]
        total = term if total is None else total + term
    if base_start is not None:
        rows = total.shape[0]
        start = pl.multiple_of(base_start(ids[0]), rows)
        total = base[pl.ds(start, rows), :] - total
    outs[0][...] = total
    if turned:
        outs[1][...] = total.T


def add(terms, base=None, tokens=(), turned=False):
    arrays, indices = zip(*terms)
    shape = arrays[0].shape[-2:]
    if isinstance(indices[0], slice):
        shape = (indices[0].stop, *shape)
    if not fast(*shape[-2:]):
        total = sum(array if index is None else array[index] for array, index in terms)
        if base is not None:
            total = lax.dynamic_slice(base[1], (base[2](base[0][0]), 0), shape) - total
        return (total, total.T) if turned else total
    bases = [] if base is None else [(base[0], pltpu.SMEM), (base[1], VMEM)]
    shapes = [shape, shape[::-1]] if turned else [shape]
    outs = call(
        functools.partial(add_kernel, indices, None if base is None else base[2], turned),
        [*bases, *((array, VMEM) for array in arrays), *((token, pl.ANY) for token in tokens)],
        [jax.ShapeDtypeStruct(extent, jnp.float32) for extent in shapes],
        room=2,
    )
    return outs if turned else outs[0]


def settle_kernel(indices, ids, *refs):
    out = refs[-1]
    for leaf, (index, chunk) in enumerate(zip(indices, refs[:-1])):
        rows = chunk.shape[-1]
        place = pl.multiple_of((ids[0] ^ leaf) * rows, rows)
        out[pl.ds(place, rows), :] = (chunk[...] if index is None else chunk[index]).T


def settle(ids, chunks):
    chunks = [chunk if isinstance(chunk, tuple) else (chunk, None) for chunk in chunks]
    width, rows = chunks[0][0].shape[-2:]
    if not fast(width, rows):
        chunks = [array if index is None else array[index] for array, index in chunks]
        natural = jnp.take(jnp.stack(chunks), jnp.arange(len(chunks), dtype=jnp.int32) ^ ids[0], axis=0)
        return jnp.transpose(natural, (0, 2, 1)).reshape(-1, width)
    return call(
        functools.partial(settle_kernel, [index for _, index in chunks]),
        [(ids, pltpu.SMEM), *((array, VMEM) for array, _ in chunks)],
        [jax.ShapeDtypeStruct((len(chunks) * rows, width), jnp.float32)],
    )[0]


def swap(value, leaf_bits, front_bits):
    groups, fronts = lax.axis_size("leaf"), lax.axis_size("front")
    pairs = [
        (leaf * fronts + front, (leaf ^ leaf_bits) * fronts + (front ^ front_bits))
        for leaf in range(groups)
        for front in range(fronts)
    ]
    return lax.ppermute(value, ("leaf", "front"), pairs)


def across(value):
    return swap(value, 0, 1)


def along(value, apart):
    return swap(value, 0, 2 * apart)


def sibling(value):
    return swap(value, 1, 0)


def opposite(value):
    return swap(value, 2, 0)


def spread_chain(own, errands=(), with_beside=True, first_ready=()):
    held, apart = {0: own}, lax.axis_size("front") // 4
    errands, done, beside = list(errands), [], {}
    while apart:
        far = {place | apart: along(value, apart) for place, value in held.items()}
        if done:
            far[apart] = near if len(done) == 1 else far[apart]
        ready = list(errands.pop(0)(own)) if errands else []
        done.append(list(ready))
        if len(done) == 1:
            ready += first_ready
        if with_beside:
            place = apart if len(done) > 1 else 0
            beside[place] = across(held[place] if place in held else far[place])
            ready.append(beside[place])
        far[max(far)] = after(far[max(far)], ready)
        if len(done) == 1 and apart > 1:
            near = along(own, apart // 2)
            near = after(near, [far[max(far)]]) if with_beside else near
        held.update(far)
        apart //= 2
    if with_beside:
        beside = {place: beside[place] if place in beside else across(held[place]) for place in held}
    return held, beside, done


def sum_chain(pieces, errands=(), first=(), **last):
    count, errands, done = len(pieces), list(errands), []
    terms = {
        place: kept if given is None else [*kept, (across(given), None)]
        for place, (kept, given) in pieces.items()
    }
    apart, ready = 1, list(first)
    while apart < count:
        top = max(place for place in range(apart, count, 2 * apart))
        for place in reversed(range(apart, count, 2 * apart)):
            summed = add(terms[place], tokens=ready)
            if place == top:
                ready = errands.pop(0)(summed) if errands else []
                done.append(ready)
            terms[place - apart] = [*terms[place - apart], (along(summed, apart), None)]
        apart *= 2
    return add(terms[0], tokens=ready, **last), done


def ways(place):
    return ((across, opposite), (1, 0), (0, 2)) if place % 2 else ((opposite, across), (0, 2), (1, 0))


def body(
    leaf_source,
    mid_source,
    root_source,
    leaf_inverse,
    leaf_coupling,
    mid_inverse,
    mid_coupling,
    root_inverse,
    leaf_blocks,
    mid_blocks,
):
    fronts = lax.axis_size("front")
    places = list(range(fronts // 2))
    downward = places[::-1]
    group, front = lax.axis_index("leaf"), lax.axis_index("front")
    ids = jnp.stack([group, front]).astype(jnp.int32)
    source_two, source_one = leaf_source[0], mid_source[0]
    inverse_two, coupling_two = leaf_inverse[0], leaf_coupling[0]
    inverse_one, coupling_one = mid_inverse[0], mid_coupling[0]
    rows_two = source_two.shape[0]
    half = source_one.shape[0]
    root_block = root_source.shape[0]
    quarter = root_block // lax.axis_size("leaf")
    root_rows = root_inverse.shape[1] // fronts

    child_two, child_one = orders(ids, leaf_blocks, mid_blocks)

    def two_start(group, front, leaf_bits, front_bits):
        return (front ^ front_bits) * rows_two

    def half_start(group, front, leaf_bits, front_bits):
        return (front ^ front_bits) * (2 * half) + ((group ^ leaf_bits) % 2) * half

    def one_start(group, front, leaf_bits, front_bits):
        return (front ^ front_bits) * half

    def quarter_start(group, front, leaf_bits, front_bits):
        return (front ^ front_bits) * root_block + (group ^ leaf_bits) * quarter

    def root_start(group, front, leaf_bits, front_bits):
        return (front ^ front_bits) * root_rows

    def whole_start(group, front):
        return 0

    def first_row(group):
        return 0

    def own_row(group):
        return group * quarter

    def side_row(group, bits):
        return ((group ^ bits) % 2) * half

    def leaf_row(group, bits):
        return (group ^ bits) * quarter

    def pair(place, leaf_bits=0):
        return [(leaf_bits, 2 * place + 1), (leaf_bits, 2 * place)]

    def arrivals(place, groups=(0,)):
        return [(leaf_bits, 2 * place + other) for other in (0, 1) for leaf_bits in groups]

    def square(place):
        _, first, second = ways(place)
        return [
            (first[1] | second[1], 2 * place + (first[0] | second[0])),
            (first[1], 2 * place + first[0]),
            (second[1], 2 * place + second[0]),
            (0, 2 * place),
        ]

    def square_both(place):
        return [(bits ^ 1, other) for bits, other in square(place)] + square(place)

    def square_arrivals(place):
        return [(bits ^ other, at) for bits, at in square(place)[::-1] for other in (0, 1)]

    count = len(places)
    early, late = downward[: count // 2], downward[count // 2 :]
    near, far = places[: count // 2], places[count // 2 :]

    def chunks_of(which, chunks):
        return [chunk for place in which for chunk in chunks(place)]

    def leaf_inverse_rows(token):
        return fetch(inverse_two, ids, None, whole_start, [()], inverse_two.shape[1], token)

    def leaf_lift_rows(which, token):
        chunks = chunks_of(which, lambda place: pair(place, 1)) + chunks_of(which, pair)
        return fetch(coupling_two, ids, child_two, half_start, chunks, half, token)

    def mid_lift_rows(which, token):
        return fetch(inverse_one, ids, None, one_start, chunks_of(which, pair), half, token)

    def root_lift_rows(which, token):
        chunks = chunks_of(which, square_both)
        return fetch(coupling_one, ids, child_one, quarter_start, chunks, quarter, token)

    def root_rows_of(which, token):
        return fetch(root_inverse, ids, None, root_start, chunks_of(which, pair), root_rows, token)

    def root_pull_rows(which, token):
        chunks = chunks_of(which, square_arrivals)
        return fetch(coupling_one, ids, child_one, quarter_start, chunks, quarter, token)

    def mid_pull_rows(which, token):
        return fetch(inverse_one, ids, None, one_start, chunks_of(which, arrivals), half, token)

    def leaf_pull_rows(which, token):
        chunks = chunks_of(which, lambda place: arrivals(place, (0, 1)))
        return fetch(coupling_two, ids, child_two, half_start, chunks, half, token)

    chain, beside, ((rows_inverse,), (rows_early,), *_) = spread_chain(
        source_two,
        [
            lambda token: [leaf_inverse_rows(token)],
            lambda token: [leaf_lift_rows(early, token)],
        ],
    )
    rows_late = leaf_lift_rows(late, rows_early)
    coming = [vector for place in places for vector in (chain[place], beside[place])]
    coming_chunks = chunks_of(places, arrivals)
    total = None
    for first, end in ((0, fronts // 2), (fronts // 2, fronts - 1), (fronts - 1, fronts)):
        last = end == fronts
        if last:
            coming[-1] = after(coming[-1], [rows_late])
        total = fold(
            rows_inverse, ids, coming[first:end], two_start, coming_chunks[first:end], total, last
        )
    solved_two, solved_two_turned = total

    def leaf_lift(held, which):
        size = 2 * len(which)
        theirs, mine = lift(held, ids, [solved_two], first_row, [()], half, 0, [size, size])
        theirs, terms = sibling(theirs), {}
        for at, place in enumerate(which):
            given = add([(mine, 2 * at), (theirs, 2 * at)])
            terms[place] = [(mine, 2 * at + 1), (theirs, 2 * at + 1)], given
        return terms, mine

    terms, _ = leaf_lift(rows_early, early)
    more, token = leaf_lift(rows_late, late)
    rows_one_early = mid_lift_rows(early, token)
    own_half, (_, (rows_one_late,), *_) = sum_chain(
        {**terms, **more},
        [lambda token: [], lambda token: [mid_lift_rows(late, token)]],
        [rows_one_early],
        base=(ids, source_one, first_row),
    )

    halves_one = [own_half, sibling(own_half)]

    def paired(which, parts):
        return {
            place: ([(kept, 0 if kept.ndim > 2 else None)], given.reshape(given.shape[-2:]))
            for place, given, kept in zip(which, parts[0::2], parts[1::2])
        }

    def mid_lift(held, which):
        ones = [1] * (2 * len(which))
        return lift(held, ids, halves_one, side_row, [(0,), (1,)], half, 0, ones)

    parts, more = mid_lift(rows_one_early, early), mid_lift(rows_one_late, late)
    (solved_one, solved_one_turned), ((rows_early,), (rows_late,), *_) = sum_chain(
        {**paired(early, parts), **paired(late, more)},
        [
            lambda token: [root_lift_rows(early, token)],
            lambda token: [root_lift_rows(late, token)],
        ],
        more[:1],
        turned=True,
    )

    def root_lift(held, begin, which, tokens=()):
        fours = [4] * (2 * len(which))
        return lift(
            held,
            ids,
            [solved_one],
            first_row,
            [()],
            quarter,
            8 * begin,
            fours,
            tokens=tokens,
        )

    def corner_terms(place, theirs, mine):
        (first_way, second_way), _, _ = ways(place)
        outer = first_way(add([(mine, slice(0, 2)), (theirs, slice(0, 2))]))
        inner = second_way(add([(mine, 2), (theirs, 2), (outer, 0)]))
        return [(mine, 3), (theirs, 3), (outer, 1), (inner, None)], None

    top, *rest = early
    (first_way, second_way), _, _ = ways(top)
    theirs, mine = root_lift(rows_early, 0, [top])
    theirs = sibling(theirs)
    parts = [part for at, place in enumerate(rest) for part in root_lift(rows_early, at + 1, [place])]
    corner = add([(mine, 0), (theirs, 0)], tokens=parts[-1:])
    parts += root_lift(rows_late, 0, late, [corner])
    first = first_way(add([(mine, 1), (theirs, 1)]))
    inner = add([(mine, 2), (theirs, 2), (first_way(corner), None)], tokens=parts[-1:])
    corners = {top: ([(mine, 3), (theirs, 3), (first, None), (second_way(inner), None)], None)}
    for place, theirs, mine in zip(rest + late, parts[0::2], parts[1::2]):
        corners[place] = corner_terms(place, sibling(theirs), mine)
    own_quarter, ((rows_root_early,), (rows_root_late,), *_) = sum_chain(
        corners,
        [
            lambda token: [root_rows_of(early, token)],
            lambda token: [root_rows_of(late, token)],
        ],
        base=(ids, root_source, own_row),
    )
    over_quarter = opposite(own_quarter)
    quarters = [own_quarter, over_quarter, sibling(own_quarter), sibling(over_quarter)]

    def root_apply(held, which):
        ones, parts = [1] * (2 * len(which)), [(0,), (2,), (1,), (3,)]
        return lift(held, ids, quarters, leaf_row, parts, root_rows, 0, ones, turned=True)

    parts, more = root_apply(rows_root_early, early), root_apply(rows_root_late, late)
    whole_root, (_, (rows_near,), *_) = sum_chain(
        {**paired(early, parts), **paired(late, more)},
        [lambda token: [], lambda token: [root_pull_rows(near, token)]],
        more[:1],
    )
    chain, beside, ((rows_far,), (rows_one_near,), *_) = spread_chain(
        whole_root,
        [
            lambda token: [root_pull_rows(far, token)],
            lambda token: [mid_pull_rows(near, token)],
        ],
    )
    late_vectors = [vector for place in late for vector in (beside[place], chain[place])]
    early_vectors = [vector for place in early for vector in (beside[place], chain[place])]
    total = pull(rows_root_late, ids, late_vectors, 0, None)
    total = pull(rows_root_early, ids, early_vectors[1:], 1, total)
    theirs_own, theirs_over, mine_own, mine_over = pull(
        rows_root_early, ids, early_vectors[:1], 0, total, leaf_row, [(1,), (3,), (0,), (2,)], quarter
    )
    rows_one_far = mid_pull_rows(far, mine_own)
    over = add([(mine_over, None), (sibling(theirs_over), None)])
    theirs_own = sibling(theirs_own)
    own_quarter = add(
        [(mine_own, None), (theirs_own, None), (opposite(over), None)], tokens=[rows_one_far]
    )

    def corner_values(place, value, ready=()):
        (first_way, second_way), _, _ = ways(place)
        first, second = first_way(value), second_way(value)
        return [value, second, first, second_way(after(first, ready))]

    corners = {0: corner_values(0, own_quarter)}
    chain, _, _ = spread_chain(own_quarter, (), False, corners[0][1:3])
    for place in places[1:-1]:
        value = chain[place]
        if place == count // 2:
            value = after(value, corners[0][3:], copied=True)
        corners[place] = corner_values(place, value)
    def with_theirs(values):
        theirs = sibling(jnp.stack(values)) if len(values) > 1 else sibling(values[0])
        theirs = [(theirs, at) for at in range(len(values))] if len(values) > 1 else [theirs]
        return [vector for both in zip(values, theirs) for vector in both]

    def pull_one(place, vectors, first, total):
        held, begin = (rows_near, 8 * place) if place in near else (rows_far, 8 * (place - len(near)))
        return pull(held, ids, vectors, begin + first, total, minus=True, hides=False)

    rest_one = solved_one_turned
    for place in places[:-1]:
        vectors = with_theirs(corners[place])
        if place == 0:
            at = 4 if ways(place)[1][1] else 2
            root_solution = settle(ids, [*vectors[:2], *vectors[at : at + 2]])
        rest_one = pull_one(place, vectors, 0, rest_one)
        if place == near[-1]:
            corners[places[-1]] = corner_values(places[-1], chain[places[-1]])
    rest_one = pull_one(places[-1], with_theirs(corners[places[-1]][:3]), 0, rest_one)
    corner = after(corners[places[-1]][3], [rest_one])
    rest_one = pull_one(places[-1], with_theirs([corner]), 6, rest_one)
    chain, beside, ((rows_near,), (rows_far,), *_) = spread_chain(
        rest_one,
        [
            lambda token: [leaf_pull_rows(near, token)],
            lambda token: [leaf_pull_rows(far, token)],
        ],
    )
    near_vectors = [vector for place in near for vector in (chain[place], beside[place])]
    far_vectors = [vector for place in far for vector in (chain[place], beside[place])]
    total = pull(rows_one_near, ids, near_vectors, 0, None)
    total = pull(rows_one_far, ids, far_vectors[:-1], 0, total)
    theirs, mine = pull(
        rows_one_far, ids, far_vectors[-1:], len(far_vectors) - 1, total, side_row, [(1,), (0,)], half
    )
    mid_columns, mid_solution = add([(mine, None), (sibling(theirs), None)], turned=True)

    chain, beside, ((rows_inverse,), *_) = spread_chain(
        mid_columns, [lambda token: [leaf_inverse_rows(token)]]
    )
    near_values = [value for place in near for value in (chain[place], beside[place])]
    far_values = [value for place in far for value in (chain[place], beside[place])]
    rest_two = pull(rows_near, ids, with_theirs(near_values), 0, solved_two_turned, minus=True)
    rest_two = pull(rows_far, ids, with_theirs(far_values[:-1]), 0, rest_two, minus=True)
    vectors = with_theirs([after(far_values[-1], [rest_two])])
    rest_two = pull(rows_far, ids, vectors, 2 * len(far_values) - 2, rest_two, minus=True)

    def leaf_spread(which):
        return spread(rows_inverse, ids, rest_two, two_start, chunks_of(which, pair), rows_two)

    parts, more = leaf_spread(early), leaf_spread(late)
    leaf_solution, _ = sum_chain(
        {**paired(early, parts), **paired(late, more)},
        [lambda token: [], lambda token: [root_solution]],
        more[:1],
    )
    return (leaf_solution[None], mid_solution[None], root_solution)


def solution(mesh):
    placed = (
        P("leaf", "front", None),
        P("leaf", "front", None),
        P("front", None),
        P("leaf", None, "front", None),
        P("leaf", None, None, "front"),
        P("leaf", None, None, "front"),
        P("leaf", None, None, "front"),
        P(None, "leaf", "front"),
        P("leaf", None),
        P(),
    )
    return jax.shard_map(
        body,
        mesh=mesh,
        in_specs=placed,
        out_specs=(P("leaf", "front", None), P("leaf", "front", None), P("front", None)),
        check_vma=False,
    )
```

```python
import functools
import math

import jax
import jax.numpy as jnp
from jax import lax
from jax.experimental import pallas as pl
from jax.experimental.pallas import tpu as pltpu
from jax.sharding import PartitionSpec as P

BLOCK = 128
VMEM = pltpu.VMEM
exact_dot = functools.partial(jnp.dot, precision=lax.Precision.HIGHEST)


def halves(values):
    high = values.astype(jnp.bfloat16)
    low = (values - high.astype(jnp.float32)).astype(jnp.bfloat16)
    return high, low


def turned_columns(vectors):
    width = vectors.shape[1] // 2
    return jnp.concatenate([-vectors[:, width:], vectors[:, :width]], axis=1)


def turned_rows(vectors):
    width = vectors.shape[0] // 2
    return jnp.concatenate([-vectors[width:], vectors[:width]], axis=0)


def dot32(left, right):
    return jnp.dot(left, right, preferred_element_type=jnp.float32)


def fast(*extents):
    return all(extent % BLOCK == 0 for extent in extents)


def call(kernel, operands, outs, scratch=(), flops=0, room=10, hides=True):
    arrays, spaces = zip(*operands)
    size = lambda a: math.prod(a.shape) * a.dtype.itemsize
    held = sum(size(a) for a, space in operands if space == VMEM) + sum(size(o) for o in outs)
    scratch_bytes = sum(size(s) for s in scratch if hasattr(s, "shape") and s.memory_space == VMEM)
    moved = held if any(space == VMEM for space in spaces) else 2 * held
    flops, moved = (flops, moved) if hides else (1024, 1024)
    return pl.pallas_call(
        kernel,
        out_shape=outs,
        in_specs=[pl.BlockSpec(memory_space=space) for space in spaces],
        out_specs=[pl.BlockSpec(memory_space=VMEM)] * len(outs),
        scratch_shapes=scratch,
        compiler_params=pltpu.CompilerParams(
            vmem_limit_bytes=scratch_bytes + room * 1024 * 1024
        ),
        cost_estimate=pl.CostEstimate(flops=flops, bytes_accessed=moved, transcendentals=0),
    )(*arrays)


class Place:
    def __init__(self, ids, child):
        self.ids, self.child = ids, child

    def starts(self, start_of, chunks, rows):
        group, front = self.ids[0], self.ids[1]
        unit = rows if self.child is None else min(BLOCK, rows)
        for chunk in chunks:
            start = start_of(group, front, *chunk)
            for inner in range(0, rows, unit):
                row = start + inner
                if self.child is not None:
                    row = self.child[row // BLOCK] * BLOCK + row % BLOCK
                yield row


def orders_kernel(ids, leaf_blocks, mid_blocks, child_two, child_one):
    for index in range(leaf_blocks.shape[1]):
        child_two[leaf_blocks[0, index]] = index
    row = lax.shift_right_logical(ids[0], 1)
    for index in range(mid_blocks.shape[1]):
        child_one[mid_blocks[row, index]] = index


def orders(ids, leaf_blocks, mid_blocks):
    return pl.pallas_call(
        orders_kernel,
        out_shape=[
            jax.ShapeDtypeStruct((leaf_blocks.shape[1],), jnp.int32),
            jax.ShapeDtypeStruct((mid_blocks.shape[1],), jnp.int32),
        ],
        in_specs=[pl.BlockSpec(memory_space=pltpu.SMEM)] * 3,
        out_specs=[pl.BlockSpec(memory_space=pltpu.SMEM)] * 2,
        compiler_params=pltpu.CompilerParams(vmem_limit_bytes=1024 * 1024),
    )(ids, leaf_blocks, mid_blocks)


def fetch_kernel(start_of, chunks, rows, unit, with_child, ids, *refs):
    child = refs[0] if with_child else None
    matrix, out, sems = refs[-3:]
    copies = []
    for index, row in enumerate(Place(ids, child).starts(start_of, chunks, rows)):
        copy = pltpu.make_async_copy(
            matrix.at[:, pl.ds(pl.multiple_of(row, unit), unit), :],
            out.at[:, pl.ds(index * unit, unit), :],
            sems.at[index],
        )
        copy.start()
        copies.append(copy)
    for copy in copies:
        copy.wait()


def fetch(matrix, ids, child, start_of, chunks, rows, token):
    columns, count = matrix.shape[2], len(chunks) * rows
    unit = rows if child is None else min(BLOCK, rows)
    if not fast(rows, columns):
        starts = jnp.stack(list(Place(ids, child).starts(start_of, chunks, rows)))
        picked = (starts[:, None] + jnp.arange(unit, dtype=jnp.int32)).reshape(-1)
        return jnp.take(matrix, picked, axis=1)
    orders = [(ids, pltpu.SMEM)] + ([] if child is None else [(child, pltpu.SMEM)])
    pinned = pltpu.with_memory_space_constraint(matrix, pltpu.HBM)
    return call(
        functools.partial(fetch_kernel, start_of, chunks, rows, unit, child is not None),
        [*orders, (token, pl.ANY), (pinned, pl.ANY)],
        [jax.ShapeDtypeStruct((2, count, columns), jnp.float32)],
        [pltpu.SemaphoreType.DMA((count // unit,))],
        room=1,
    )[0]


def pass_kernel(*refs):
    del refs


def copy_kernel(*refs):
    refs[-1][...] = refs[-2][...]


def after(value, tokens, copied=False):
    if not tokens or not fast(*value.shape[-2:]):
        return value
    space = VMEM if copied else pl.ANY
    return pl.pallas_call(
        copy_kernel if copied else pass_kernel,
        out_shape=jax.ShapeDtypeStruct(value.shape, value.dtype),
        in_specs=[pl.BlockSpec(memory_space=pl.ANY)] * len(tokens)
        + [pl.BlockSpec(memory_space=space)],
        out_specs=pl.BlockSpec(memory_space=space),
        input_output_aliases={} if copied else {len(tokens): 0},
        compiler_params=pltpu.CompilerParams(vmem_limit_bytes=1024 * 1024),
        cost_estimate=pl.CostEstimate(flops=0, bytes_accessed=1024, transcendentals=0),
    )(*tokens, value)


def wide_of(real, imag):
    real_high, real_low = halves(real)
    imag_high, imag_low = halves(imag)
    return jnp.concatenate([real_high, imag_high, real_low, imag_low], axis=1)


def lift_kernel(start_of, parts, rows, begin, counts, turned, ids, *refs):
    chunk_refs, (held, *rest) = refs[: len(parts)], refs[len(parts) :]
    outs, (natural, weights) = rest[-2 - len(counts) : -2], rest[-2:]
    depth = natural.shape[0]
    step = chunk_refs[0].shape[0]
    for part, chunk in zip(parts, chunk_refs):
        place = pl.multiple_of(start_of(ids[0], *part), step)
        natural[pl.ds(place, step), :] = chunk[...]
    for half, values in enumerate((natural[...], turned_columns(natural[...]))):
        high, low = halves(values)
        both = jnp.concatenate([high, low], axis=1)
        weights[half * depth : (half + 1) * depth, :] = both
        weights[(half + 2) * depth : (half + 3) * depth, :] = both
    for out, count in zip(outs, counts):
        together = 1 if turned or count % 2 else 2
        for index in range(0, count, together):
            here = slice((begin + index) * rows, (begin + index + together) * rows)
            wide = dot32(wide_of(held[0, here], held[1, here]), weights[...])
            whole = wide[:, :BLOCK] + wide[:, BLOCK:]
            if turned:
                out[index] = whole.T
            else:
                out[index : index + together] = whole.reshape(together, rows, BLOCK)
        begin += count


def lift(held, ids, vectors, start_of, parts, rows, begin, counts, turned=False, tokens=()):
    depth, width = held.shape[2], vectors[0].shape[1]
    if not fast(rows, depth, vectors[0].shape[0]):
        whole = jnp.zeros((depth, width), jnp.float32)
        for part, chunk in zip(parts, vectors):
            whole = lax.dynamic_update_slice(whole, chunk, (start_of(ids[0], *part), 0))
        held = held[:, begin * rows : (begin + sum(counts)) * rows]
        result = exact_dot(held[0], whole) + exact_dot(held[1], turned_columns(whole))
        result = result.reshape(-1, rows, width)
        result = jnp.transpose(result, (0, 2, 1)) if turned else result
        ends = [sum(counts[: i + 1]) for i in range(len(counts))]
        return [result[end - count : end] for end, count in zip(ends, counts)]
    shape = (width, rows) if turned else (rows, width)
    return call(
        functools.partial(lift_kernel, start_of, parts, rows, begin, counts, turned),
        [
            (ids, pltpu.SMEM),
            *((chunk, VMEM) for chunk in vectors),
            (held, VMEM),
            *((token, pl.ANY) for token in tokens),
        ],
        [jax.ShapeDtypeStruct((count, *shape), jnp.float32) for count in counts],
        [VMEM((depth, BLOCK), jnp.float32), VMEM((4 * depth, 2 * BLOCK), jnp.bfloat16)],
        2 * 4 * sum(counts) * rows * depth * 2 * BLOCK,
    )


def fold_kernel(start_of, chunks, has_total, turned, ids, *refs):
    chunk_refs, (held, *rest) = refs[: len(chunks)], refs[len(chunks) :]
    outs = rest[-2:] if turned else rest[-1:]
    total = rest[0][...] if has_total else None
    depth = chunk_refs[0].shape[0]
    for chunk, chunk_ref in zip(chunks, chunk_refs):
        values = chunk_ref[...]
        high, low = halves(values)
        turned_high, turned_low = halves(turned_columns(values))
        both = jnp.concatenate(
            [
                jnp.concatenate([high, low], axis=1),
                jnp.concatenate([turned_high, turned_low], axis=1),
            ],
            axis=0,
        )
        here = pl.ds(pl.multiple_of(start_of(ids[0], ids[1], *chunk), depth), depth)
        tile = wide_of(held[0, :, here], held[1, :, here])
        wide = dot32(tile, jnp.concatenate([both, both], axis=0))
        term = wide[:, :BLOCK] + wide[:, BLOCK:]
        total = term if total is None else total + term
    outs[0][...] = total
    if turned:
        outs[1][...] = total.T


def fold(held, ids, vectors, start_of, chunks, total, turned=False):
    rows, (depth, width) = held.shape[1], vectors[0].shape
    if not fast(rows, depth):
        for chunk, values in zip(chunks, vectors):
            column = start_of(ids[0], ids[1], *chunk)
            taken = lax.dynamic_slice(held, (0, 0, column), (2, rows, depth))
            term = exact_dot(taken[0], values) + exact_dot(taken[1], turned_columns(values))
            total = term if total is None else total + term
        return (total, total.T) if turned else total
    before = [] if total is None else [(total, VMEM)]
    shapes = [(rows, width), (width, rows)] if turned else [(rows, width)]
    outs = call(
        functools.partial(fold_kernel, start_of, chunks, total is not None, turned),
        [(ids, pltpu.SMEM), *((chunk, VMEM) for chunk in vectors), (held, VMEM), *before],
        [jax.ShapeDtypeStruct(shape, jnp.float32) for shape in shapes],
        [],
        2 * 4 * len(chunks) * rows * depth * 2 * BLOCK,
    )
    return outs if turned else outs[0]


def pull_kernel(begin, picks, arrays, has_total, minus, start_of, pieces, ids, *refs):
    array_refs, (held, *rest) = refs[:arrays], refs[arrays:]
    outs, total = rest[has_total:-1], rest[-1]
    count, depth, columns = len(picks), array_refs[0].shape[-1], held.shape[2]
    chunk_refs = [
        array_refs[at] if index is None else array_refs[at].at[index] for at, index in picks
    ]
    lefts = []
    for chunk in chunk_refs:
        values = chunk[...]
        high, low = halves(values)
        turned_high, turned_low = halves(turned_rows(values))
        lefts.append(
            (
                jnp.concatenate([high, low], axis=0),
                jnp.concatenate([turned_high, turned_low], axis=0),
            )
        )
    left = [jnp.concatenate(side, axis=1) for side in zip(*lefts)]
    rows = slice(begin * depth, (begin + count) * depth)
    for at in range(0, columns, 256):
        here = slice(at, min(at + 256, columns))
        term = rest[0][:, here] if has_total else None
        for part in (0, 1):
            high, low = halves(held[part, rows, here])
            wide = dot32(left[part], high)
            thin = dot32(left[part][:BLOCK], low)
            both = wide[:BLOCK] + wide[BLOCK:] + thin
            term = both if term is None else term - both if minus else term + both
        total[:, here] = term
    if not pieces:
        outs[0][...] = total[...]
    for piece, out in zip(pieces, outs):
        place = pl.multiple_of(start_of(ids[0], *piece), out.shape[1])
        out[...] = total[:, pl.ds(place, out.shape[1])]


def pull(
    held, ids, vectors, begin, total, start_of=None, pieces=(), size=0, minus=False, hides=True
):
    vectors = [vector if isinstance(vector, tuple) else (vector, None) for vector in vectors]
    columns, (width, depth) = held.shape[2], vectors[0][0].shape[-2:]
    if not fast(columns, depth):
        values = jnp.concatenate(
            [array if index is None else array[index] for array, index in vectors], axis=1
        )
        held = held[:, begin * depth : (begin + len(vectors)) * depth]
        term = exact_dot(values, held[0]) + exact_dot(turned_rows(values), held[1])
        total = term if total is None else total - term if minus else total + term
        if not pieces:
            return total
        return [
            lax.dynamic_slice(total, (0, start_of(ids[0], *piece)), (width, size))
            for piece in pieces
        ]
    before = [] if total is None else [(total, VMEM)]
    shapes = [(width, size)] * len(pieces) if pieces else [(width, columns)]
    arrays = list({id(array): array for array, _ in vectors}.values())
    at = {id(array): place for place, array in enumerate(arrays)}
    picks = [(at[id(array)], index) for array, index in vectors]
    outs = call(
        functools.partial(
            pull_kernel, begin, picks, len(arrays), total is not None, minus, start_of, pieces
        ),
        [(ids, pltpu.SMEM), *((array, VMEM) for array in arrays), (held, VMEM), *before],
        [jax.ShapeDtypeStruct(shape, jnp.float32) for shape in shapes],
        [VMEM((width, columns), jnp.float32)],
        2 * 3 * len(vectors) * depth * columns * 2 * BLOCK,
        hides=hides,
    )
    return outs if pieces else outs[0]


def spread_kernel(start_of, chunks, ids, vectors, held, *refs):
    outs = refs[-len(chunks) :]
    size = outs[0].shape[0]
    values = vectors[...]
    high, low = halves(values)
    turned_high, turned_low = halves(turned_rows(values))
    left = (
        jnp.concatenate([high, low], axis=0),
        jnp.concatenate([turned_high, turned_low], axis=0),
    )
    for chunk, out in zip(chunks, outs):
        here = pl.ds(pl.multiple_of(start_of(ids[0], ids[1], *chunk), size), size)
        term = None
        for part in (0, 1):
            high, low = halves(held[part, :, here])
            wide = dot32(left[part], high)
            thin = dot32(left[part][:BLOCK], low)
            both = wide[:BLOCK] + wide[BLOCK:] + thin
            term = both if term is None else term + both
        out[...] = term.T


def spread(held, ids, vectors, start_of, chunks, size):
    width, depth = vectors.shape
    if not fast(depth, size):
        whole = exact_dot(vectors, held[0]) + exact_dot(turned_rows(vectors), held[1])
        return [
            lax.dynamic_slice(whole, (0, start_of(ids[0], ids[1], *chunk)), (width, size)).T
            for chunk in chunks
        ]
    return call(
        functools.partial(spread_kernel, start_of, chunks),
        [(ids, pltpu.SMEM), (vectors, VMEM), (held, VMEM)],
        [jax.ShapeDtypeStruct((size, width), jnp.float32)] * len(chunks),
        [],
        2 * 3 * len(chunks) * depth * size * 2 * BLOCK,
    )


def add_kernel(indices, base_start, turned, *refs):
    outs = refs[-2:] if turned else refs[-1:]
    ids, base, *arrays = refs if base_start is not None else (None, None, *refs)
    total = None
    for index, ref in zip(indices, arrays):
        term = ref[...] if index is None else ref[index]
        total = term if total is None else total + term
    if base_start is not None:
        rows = total.shape[0]
        start = pl.multiple_of(base_start(ids[0]), rows)
        total = base[pl.ds(start, rows), :] - total
    outs[0][...] = total
    if turned:
        outs[1][...] = total.T


def add(terms, base=None, tokens=(), turned=False):
    arrays, indices = zip(*terms)
    shape = arrays[0].shape[-2:]
    if isinstance(indices[0], slice):
        shape = (indices[0].stop, *shape)
    if not fast(*shape[-2:]):
        total = sum(array if index is None else array[index] for array, index in terms)
        if base is not None:
            total = lax.dynamic_slice(base[1], (base[2](base[0][0]), 0), shape) - total
        return (total, total.T) if turned else total
    bases = [] if base is None else [(base[0], pltpu.SMEM), (base[1], VMEM)]
    shapes = [shape, shape[::-1]] if turned else [shape]
    outs = call(
        functools.partial(add_kernel, indices, None if base is None else base[2], turned),
        [*bases, *((array, VMEM) for array in arrays), *((token, pl.ANY) for token in tokens)],
        [jax.ShapeDtypeStruct(extent, jnp.float32) for extent in shapes],
        room=2,
    )
    return outs if turned else outs[0]


def settle_kernel(indices, ids, *refs):
    out = refs[-1]
    for leaf, (index, chunk) in enumerate(zip(indices, refs[:-1])):
        rows = chunk.shape[-1]
        place = pl.multiple_of((ids[0] ^ leaf) * rows, rows)
        out[pl.ds(place, rows), :] = (chunk[...] if index is None else chunk[index]).T


def settle(ids, chunks):
    chunks = [chunk if isinstance(chunk, tuple) else (chunk, None) for chunk in chunks]
    width, rows = chunks[0][0].shape[-2:]
    if not fast(width, rows):
        chunks = [array if index is None else array[index] for array, index in chunks]
        natural = jnp.take(jnp.stack(chunks), jnp.arange(len(chunks), dtype=jnp.int32) ^ ids[0], axis=0)
        return jnp.transpose(natural, (0, 2, 1)).reshape(-1, width)
    return call(
        functools.partial(settle_kernel, [index for _, index in chunks]),
        [(ids, pltpu.SMEM), *((array, VMEM) for array, _ in chunks)],
        [jax.ShapeDtypeStruct((len(chunks) * rows, width), jnp.float32)],
    )[0]


def swap(value, leaf_bits, front_bits):
    groups, fronts = lax.axis_size("leaf"), lax.axis_size("front")
    pairs = [
        (leaf * fronts + front, (leaf ^ leaf_bits) * fronts + (front ^ front_bits))
        for leaf in range(groups)
        for front in range(fronts)
    ]
    return lax.ppermute(value, ("leaf", "front"), pairs)


def across(value):
    return swap(value, 0, 1)


def along(value, apart):
    return swap(value, 0, 2 * apart)


def sibling(value):
    return swap(value, 1, 0)


def opposite(value):
    return swap(value, 2, 0)


def spread_chain(own, errands=(), with_beside=True, first_ready=()):
    held, apart = {0: own}, lax.axis_size("front") // 4
    errands, done, beside = list(errands), [], {}
    while apart:
        far = {place | apart: along(value, apart) for place, value in held.items()}
        ready = list(errands.pop(0)(own)) if errands else []
        done.append(list(ready))
        if len(done) == 1:
            ready += first_ready
        if with_beside:
            place = apart if len(done) > 1 else 0
            beside[place] = across(held[place] if place in held else far[place])
            ready.append(beside[place])
        if len(done) == 1 and apart > 1:
            near = along(own, apart // 2)
            ready.append(near)
        far[max(far)] = after(far[max(far)], ready)
        if len(done) == 2:
            far[apart] = near
        held.update(far)
        apart //= 2
    if with_beside:
        beside = {place: beside[place] if place in beside else across(held[place]) for place in held}
    return held, beside, done


def sum_chain(pieces, errands=(), first=(), **last):
    count, errands, done = len(pieces), list(errands), []
    terms = {
        place: kept if given is None else [*kept, (across(given), None)]
        for place, (kept, given) in pieces.items()
    }
    apart, ready = 1, list(first)
    while apart < count:
        top = max(place for place in range(apart, count, 2 * apart))
        for place in reversed(range(apart, count, 2 * apart)):
            summed = add(terms[place], tokens=ready)
            if place == top:
                ready = errands.pop(0)(summed) if errands else []
                done.append(ready)
            terms[place - apart] = [*terms[place - apart], (along(summed, apart), None)]
        apart *= 2
    return add(terms[0], tokens=ready, **last), done


def ways(place):
    return ((across, opposite), (1, 0), (0, 2)) if place % 2 else ((opposite, across), (0, 2), (1, 0))


def body(
    leaf_source,
    mid_source,
    root_source,
    leaf_inverse,
    leaf_coupling,
    mid_inverse,
    mid_coupling,
    root_inverse,
    leaf_blocks,
    mid_blocks,
):
    fronts = lax.axis_size("front")
    places = list(range(fronts // 2))
    downward = places[::-1]
    group, front = lax.axis_index("leaf"), lax.axis_index("front")
    ids = jnp.stack([group, front]).astype(jnp.int32)
    source_two, source_one = leaf_source[0], mid_source[0]
    inverse_two, coupling_two = leaf_inverse[0], leaf_coupling[0]
    inverse_one, coupling_one = mid_inverse[0], mid_coupling[0]
    rows_two = source_two.shape[0]
    half = source_one.shape[0]
    root_block = root_source.shape[0]
    quarter = root_block // lax.axis_size("leaf")
    root_rows = root_inverse.shape[1] // fronts

    child_two, child_one = orders(ids, leaf_blocks, mid_blocks)

    def two_start(group, front, leaf_bits, front_bits):
        return (front ^ front_bits) * rows_two

    def half_start(group, front, leaf_bits, front_bits):
        return (front ^ front_bits) * (2 * half) + ((group ^ leaf_bits) % 2) * half

    def one_start(group, front, leaf_bits, front_bits):
        return (front ^ front_bits) * half

    def quarter_start(group, front, leaf_bits, front_bits):
        return (front ^ front_bits) * root_block + (group ^ leaf_bits) * quarter

    def root_start(group, front, leaf_bits, front_bits):
        return (front ^ front_bits) * root_rows

    def whole_start(group, front):
        return 0

    def first_row(group):
        return 0

    def own_row(group):
        return group * quarter

    def side_row(group, bits):
        return ((group ^ bits) % 2) * half

    def leaf_row(group, bits):
        return (group ^ bits) * quarter

    def pair(place, leaf_bits=0):
        return [(leaf_bits, 2 * place + 1), (leaf_bits, 2 * place)]

    def arrivals(place, groups=(0,)):
        return [(leaf_bits, 2 * place + other) for other in (0, 1) for leaf_bits in groups]

    def square(place):
        _, first, second = ways(place)
        return [
            (first[1] | second[1], 2 * place + (first[0] | second[0])),
            (first[1], 2 * place + first[0]),
            (second[1], 2 * place + second[0]),
            (0, 2 * place),
        ]

    def square_both(place):
        return [(bits ^ 1, other) for bits, other in square(place)] + square(place)

    def square_arrivals(place):
        return [(bits ^ other, at) for bits, at in square(place)[::-1] for other in (0, 1)]

    count = len(places)
    early, late = downward[: count // 2], downward[count // 2 :]
    near, far = places[: count // 2], places[count // 2 :]

    def chunks_of(which, chunks):
        return [chunk for place in which for chunk in chunks(place)]

    def leaf_inverse_rows(token):
        return fetch(inverse_two, ids, None, whole_start, [()], inverse_two.shape[1], token)

    def leaf_lift_rows(which, token):
        chunks = chunks_of(which, lambda place: pair(place, 1)) + chunks_of(which, pair)
        return fetch(coupling_two, ids, child_two, half_start, chunks, half, token)

    def mid_lift_rows(which, token):
        return fetch(inverse_one, ids, None, one_start, chunks_of(which, pair), half, token)

    def root_lift_rows(which, token):
        chunks = chunks_of(which, square_both)
        return fetch(coupling_one, ids, child_one, quarter_start, chunks, quarter, token)

    def root_rows_of(which, token):
        return fetch(root_inverse, ids, None, root_start, chunks_of(which, pair), root_rows, token)

    def root_pull_rows(which, token):
        chunks = chunks_of(which, square_arrivals)
        return fetch(coupling_one, ids, child_one, quarter_start, chunks, quarter, token)

    def mid_pull_rows(which, token):
        return fetch(inverse_one, ids, None, one_start, chunks_of(which, arrivals), half, token)

    def leaf_pull_rows(which, token):
        chunks = chunks_of(which, lambda place: arrivals(place, (0, 1)))
        return fetch(coupling_two, ids, child_two, half_start, chunks, half, token)

    chain, beside, ((rows_inverse,), (rows_early,), *_) = spread_chain(
        source_two,
        [
            lambda token: [leaf_inverse_rows(token)],
            lambda token: [leaf_lift_rows(early, token)],
        ],
    )
    rows_late = leaf_lift_rows(late, rows_early)
    coming = [vector for place in places for vector in (chain[place], beside[place])]
    coming_chunks = chunks_of(places, arrivals)
    total = None
    for first, end in ((0, fronts // 2), (fronts // 2, fronts - 1), (fronts - 1, fronts)):
        last = end == fronts
        if last:
            coming[-1] = after(coming[-1], [rows_late])
        total = fold(
            rows_inverse, ids, coming[first:end], two_start, coming_chunks[first:end], total, last
        )
    solved_two, solved_two_turned = total

    def leaf_lift(held, which):
        size = 2 * len(which)
        theirs, mine = lift(held, ids, [solved_two], first_row, [()], half, 0, [size, size])
        theirs, terms = sibling(theirs), {}
        for at, place in enumerate(which):
            given = add([(mine, 2 * at), (theirs, 2 * at)])
            terms[place] = [(mine, 2 * at + 1), (theirs, 2 * at + 1)], given
        return terms, mine

    terms, _ = leaf_lift(rows_early, early)
    more, token = leaf_lift(rows_late, late)
    rows_one_early = mid_lift_rows(early, token)
    own_half, (_, (rows_one_late,), *_) = sum_chain(
        {**terms, **more},
        [lambda token: [], lambda token: [mid_lift_rows(late, token)]],
        [rows_one_early],
        base=(ids, source_one, first_row),
    )

    halves_one = [own_half, sibling(own_half)]

    def paired(which, parts):
        return {
            place: ([(kept, 0 if kept.ndim > 2 else None)], given.reshape(given.shape[-2:]))
            for place, given, kept in zip(which, parts[0::2], parts[1::2])
        }

    def mid_lift(held, which):
        ones = [1] * (2 * len(which))
        return lift(held, ids, halves_one, side_row, [(0,), (1,)], half, 0, ones)

    parts, more = mid_lift(rows_one_early, early), mid_lift(rows_one_late, late)
    (solved_one, solved_one_turned), ((rows_early,), (rows_late,), *_) = sum_chain(
        {**paired(early, parts), **paired(late, more)},
        [
            lambda token: [root_lift_rows(early, token)],
            lambda token: [root_lift_rows(late, token)],
        ],
        more[:1],
        turned=True,
    )

    def root_lift(held, begin, which, tokens=()):
        fours = [4] * (2 * len(which))
        return lift(
            held,
            ids,
            [solved_one],
            first_row,
            [()],
            quarter,
            8 * begin,
            fours,
            tokens=tokens,
        )

    def corner_terms(place, theirs, mine):
        (first_way, second_way), _, _ = ways(place)
        outer = first_way(add([(mine, slice(0, 2)), (theirs, slice(0, 2))]))
        inner = second_way(add([(mine, 2), (theirs, 2), (outer, 0)]))
        return [(mine, 3), (theirs, 3), (outer, 1), (inner, None)], None

    top, *rest = early
    (first_way, second_way), _, _ = ways(top)
    theirs, mine = root_lift(rows_early, 0, [top])
    theirs = sibling(theirs)
    parts = [part for at, place in enumerate(rest) for part in root_lift(rows_early, at + 1, [place])]
    corner = add([(mine, 0), (theirs, 0)], tokens=parts[-1:])
    parts += root_lift(rows_late, 0, late, [corner])
    first = first_way(add([(mine, 1), (theirs, 1)]))
    inner = add([(mine, 2), (theirs, 2), (first_way(corner), None)], tokens=parts[-1:])
    corners = {top: ([(mine, 3), (theirs, 3), (first, None), (second_way(inner), None)], None)}
    for place, theirs, mine in zip(rest + late, parts[0::2], parts[1::2]):
        corners[place] = corner_terms(place, sibling(theirs), mine)
    own_quarter, ((rows_root_early,), (rows_root_late,), *_) = sum_chain(
        corners,
        [
            lambda token: [root_rows_of(early, token)],
            lambda token: [root_rows_of(late, token)],
        ],
        base=(ids, root_source, own_row),
    )
    over_quarter = opposite(own_quarter)
    quarters = [own_quarter, over_quarter, sibling(own_quarter), sibling(over_quarter)]

    def root_apply(held, which):
        ones, parts = [1] * (2 * len(which)), [(0,), (2,), (1,), (3,)]
        return lift(held, ids, quarters, leaf_row, parts, root_rows, 0, ones, turned=True)

    parts, more = root_apply(rows_root_early, early), root_apply(rows_root_late, late)
    whole_root, (_, (rows_near,), *_) = sum_chain(
        {**paired(early, parts), **paired(late, more)},
        [lambda token: [], lambda token: [root_pull_rows(near, token)]],
        more[:1],
    )
    chain, beside, ((rows_far,), (rows_one_near,), *_) = spread_chain(
        whole_root,
        [
            lambda token: [root_pull_rows(far, token)],
            lambda token: [mid_pull_rows(near, token)],
        ],
    )
    late_vectors = [vector for place in late for vector in (beside[place], chain[place])]
    early_vectors = [vector for place in early for vector in (beside[place], chain[place])]
    total = pull(rows_root_late, ids, late_vectors, 0, None)
    total = pull(rows_root_early, ids, early_vectors[1:], 1, total)
    theirs_own, theirs_over, mine_own, mine_over = pull(
        rows_root_early, ids, early_vectors[:1], 0, total, leaf_row, [(1,), (3,), (0,), (2,)], quarter
    )
    rows_one_far = mid_pull_rows(far, mine_own)
    over = add([(mine_over, None), (sibling(theirs_over), None)])
    theirs_own = sibling(theirs_own)
    own_quarter = add(
        [(mine_own, None), (theirs_own, None), (opposite(over), None)], tokens=[rows_one_far]
    )

    def corner_values(place, value, ready=()):
        (first_way, second_way), _, _ = ways(place)
        first, second = first_way(value), second_way(value)
        return [value, second, first, second_way(after(first, ready))]

    corners = {0: corner_values(0, own_quarter)}
    chain, _, _ = spread_chain(own_quarter, (), False, corners[0][1:3])
    for place in places[1:-1]:
        value = chain[place]
        if place == count // 2:
            value = after(value, corners[0][3:], copied=True)
        corners[place] = corner_values(place, value)
    def with_theirs(values):
        theirs = sibling(jnp.stack(values) if len(values) > 1 else values[0])
        theirs = [(theirs, at) for at in range(len(values))] if len(values) > 1 else [theirs]
        return [vector for both in zip(values, theirs) for vector in both]

    def pull_one(place, vectors, first, total):
        held, begin = (rows_near, 8 * place) if place in near else (rows_far, 8 * (place - len(near)))
        return pull(held, ids, vectors, begin + first, total, minus=True, hides=False)

    rest_one = solved_one_turned
    for place in places[:-1]:
        vectors = with_theirs(corners[place])
        if place == 0:
            at = 4 if ways(place)[1][1] else 2
            root_solution = settle(ids, [*vectors[:2], *vectors[at : at + 2]])
        rest_one = pull_one(place, vectors, 0, rest_one)
        if place == near[-1]:
            corners[places[-1]] = corner_values(places[-1], chain[places[-1]])
    rest_one = pull_one(places[-1], with_theirs(corners[places[-1]][:3]), 0, rest_one)
    corner = after(corners[places[-1]][3], [rest_one])
    rest_one = pull_one(places[-1], with_theirs([corner]), 6, rest_one)
    chain, beside, ((rows_near,), (rows_far, *_), *_) = spread_chain(
        rest_one,
        [
            lambda token: [leaf_pull_rows(near, token)],
            lambda token: [leaf_pull_rows(far, token), root_solution],
        ],
    )
    near_vectors = [vector for place in near for vector in (chain[place], beside[place])]
    far_vectors = [vector for place in far for vector in (chain[place], beside[place])]
    total = pull(rows_one_near, ids, near_vectors, 0, None)
    total = pull(rows_one_far, ids, far_vectors[:-1], 0, total)
    theirs, mine = pull(
        rows_one_far, ids, far_vectors[-1:], len(far_vectors) - 1, total, side_row, [(1,), (0,)], half
    )
    mid_columns, mid_solution = add([(mine, None), (sibling(theirs), None)], turned=True)

    chain, beside, ((rows_inverse,), *_) = spread_chain(
        mid_columns, [lambda token: [leaf_inverse_rows(token)]]
    )
    near_values = [value for place in near for value in (chain[place], beside[place])]
    far_values = [value for place in far for value in (chain[place], beside[place])]
    rest_two = pull(rows_near, ids, with_theirs(near_values), 0, solved_two_turned, minus=True)
    rest_two = pull(rows_far, ids, with_theirs(far_values[:-1]), 0, rest_two, minus=True)
    vectors = with_theirs([after(far_values[-1], [rest_two])])
    rest_two = pull(rows_far, ids, vectors, 2 * len(far_values) - 2, rest_two, minus=True)

    def leaf_spread(which):
        return spread(rows_inverse, ids, rest_two, two_start, chunks_of(which, pair), rows_two)

    parts, more = leaf_spread(early), leaf_spread(late)
    leaf_solution, _ = sum_chain({**paired(early, parts), **paired(late, more)}, (), more[:1])
    return (leaf_solution[None], mid_solution[None], root_solution)


def solution(mesh):
    placed = (
        P("leaf", "front", None),
        P("leaf", "front", None),
        P("front", None),
        P("leaf", None, "front", None),
        P("leaf", None, None, "front"),
        P("leaf", None, None, "front"),
        P("leaf", None, None, "front"),
        P(None, "leaf", "front"),
        P("leaf", None),
        P(),
    )
    return jax.shard_map(
        body,
        mesh=mesh,
        in_specs=placed,
        out_specs=(P("leaf", "front", None), P("leaf", "front", None), P("front", None)),
        check_vma=False,
    )
```

```python
import functools
import math

import jax
import jax.numpy as jnp
from jax import lax
from jax.experimental import pallas as pl
from jax.experimental.pallas import tpu as pltpu
from jax.sharding import PartitionSpec as P

BLOCK = 128
VMEM = pltpu.VMEM
exact_dot = functools.partial(jnp.dot, precision=lax.Precision.HIGHEST)


def halves(values):
    high = values.astype(jnp.bfloat16)
    low = (values - high.astype(jnp.float32)).astype(jnp.bfloat16)
    return high, low


def turned_columns(vectors):
    width = vectors.shape[1] // 2
    return jnp.concatenate([-vectors[:, width:], vectors[:, :width]], axis=1)


def turned_rows(vectors):
    width = vectors.shape[0] // 2
    return jnp.concatenate([-vectors[width:], vectors[:width]], axis=0)


def dot32(left, right):
    return jnp.dot(left, right, preferred_element_type=jnp.float32)


def fast(*extents):
    return all(extent % BLOCK == 0 for extent in extents)


def call(kernel, operands, outs, scratch=(), flops=0, room=10, hides=True):
    arrays, spaces = zip(*operands)
    size = lambda a: math.prod(a.shape) * a.dtype.itemsize
    held = sum(size(a) for a, space in operands if space == VMEM) + sum(size(o) for o in outs)
    scratch_bytes = sum(size(s) for s in scratch if hasattr(s, "shape") and s.memory_space == VMEM)
    moved = held if any(space == VMEM for space in spaces) else 2 * held
    flops, moved = (flops, moved) if hides else (1024, 1024)
    return pl.pallas_call(
        kernel,
        out_shape=outs,
        in_specs=[pl.BlockSpec(memory_space=space) for space in spaces],
        out_specs=[pl.BlockSpec(memory_space=VMEM)] * len(outs),
        scratch_shapes=scratch,
        compiler_params=pltpu.CompilerParams(
            vmem_limit_bytes=scratch_bytes + room * 1024 * 1024
        ),
        cost_estimate=pl.CostEstimate(flops=flops, bytes_accessed=moved, transcendentals=0),
    )(*arrays)


class Place:
    def __init__(self, ids, child):
        self.ids, self.child = ids, child

    def starts(self, start_of, chunks, rows):
        group, front = self.ids[0], self.ids[1]
        unit = rows if self.child is None else min(BLOCK, rows)
        for chunk in chunks:
            start = start_of(group, front, *chunk)
            for inner in range(0, rows, unit):
                row = start + inner
                if self.child is not None:
                    row = self.child[row // BLOCK] * BLOCK + row % BLOCK
                yield row


def orders_kernel(ids, leaf_blocks, mid_blocks, child_two, child_one):
    for index in range(leaf_blocks.shape[1]):
        child_two[leaf_blocks[0, index]] = index
    row = lax.shift_right_logical(ids[0], 1)
    for index in range(mid_blocks.shape[1]):
        child_one[mid_blocks[row, index]] = index


def orders(ids, leaf_blocks, mid_blocks):
    return pl.pallas_call(
        orders_kernel,
        out_shape=[
            jax.ShapeDtypeStruct((leaf_blocks.shape[1],), jnp.int32),
            jax.ShapeDtypeStruct((mid_blocks.shape[1],), jnp.int32),
        ],
        in_specs=[pl.BlockSpec(memory_space=pltpu.SMEM)] * 3,
        out_specs=[pl.BlockSpec(memory_space=pltpu.SMEM)] * 2,
        compiler_params=pltpu.CompilerParams(vmem_limit_bytes=1024 * 1024),
    )(ids, leaf_blocks, mid_blocks)


def fetch_kernel(start_of, chunks, rows, unit, with_child, ids, *refs):
    child = refs[0] if with_child else None
    matrix, out, sems = refs[-3:]
    copies = []
    for index, row in enumerate(Place(ids, child).starts(start_of, chunks, rows)):
        copy = pltpu.make_async_copy(
            matrix.at[:, pl.ds(pl.multiple_of(row, unit), unit), :],
            out.at[:, pl.ds(index * unit, unit), :],
            sems.at[index],
        )
        copy.start()
        copies.append(copy)
    for copy in copies:
        copy.wait()


def fetch(matrix, ids, child, start_of, chunks, rows, token):
    columns, count = matrix.shape[2], len(chunks) * rows
    unit = rows if child is None else min(BLOCK, rows)
    if not fast(rows, columns):
        starts = jnp.stack(list(Place(ids, child).starts(start_of, chunks, rows)))
        picked = (starts[:, None] + jnp.arange(unit, dtype=jnp.int32)).reshape(-1)
        return jnp.take(matrix, picked, axis=1)
    orders = [(ids, pltpu.SMEM)] + ([] if child is None else [(child, pltpu.SMEM)])
    pinned = pltpu.with_memory_space_constraint(matrix, pltpu.HBM)
    return call(
        functools.partial(fetch_kernel, start_of, chunks, rows, unit, child is not None),
        [*orders, (token, pl.ANY), (pinned, pl.ANY)],
        [jax.ShapeDtypeStruct((2, count, columns), jnp.float32)],
        [pltpu.SemaphoreType.DMA((count // unit,))],
        room=1,
    )[0]


def pass_kernel(*refs):
    del refs


def copy_kernel(*refs):
    refs[-1][...] = refs[-2][...]


def after(value, tokens, copied=False):
    if not tokens or not fast(*value.shape[-2:]):
        return value
    space = VMEM if copied else pl.ANY
    return pl.pallas_call(
        copy_kernel if copied else pass_kernel,
        out_shape=jax.ShapeDtypeStruct(value.shape, value.dtype),
        in_specs=[pl.BlockSpec(memory_space=pl.ANY)] * len(tokens)
        + [pl.BlockSpec(memory_space=space)],
        out_specs=pl.BlockSpec(memory_space=space),
        input_output_aliases={} if copied else {len(tokens): 0},
        compiler_params=pltpu.CompilerParams(vmem_limit_bytes=1024 * 1024),
        cost_estimate=pl.CostEstimate(flops=0, bytes_accessed=1024, transcendentals=0),
    )(*tokens, value)


def wide_of(real, imag):
    real_high, real_low = halves(real)
    imag_high, imag_low = halves(imag)
    return jnp.concatenate([real_high, imag_high, real_low, imag_low], axis=1)


def lift_kernel(start_of, parts, rows, begin, counts, turned, has_before, ids, *refs):
    chunk_refs, (held, *rest) = refs[: len(parts)], refs[len(parts) :]
    before = rest[: len(counts)] if has_before else [None] * len(counts)
    outs, weights = rest[-1 - len(counts) : -1], rest[-1]
    step = chunk_refs[0].shape[0]
    depth = step * len(parts)
    columns = []
    for place, (part, chunk) in enumerate(zip(parts, chunk_refs)):
        whole = held.shape[2] == step
        start = 0 if whole else pl.multiple_of(start_of(ids[0], *part), step)
        columns.append(slice(None) if whole else pl.ds(start, step))
        for half, values in enumerate((chunk[...], turned_columns(chunk[...]))):
            both = jnp.concatenate(halves(values), axis=1)
            at = half * depth + place * step
            weights[at : at + step, :] = both
            weights[2 * depth + at : 2 * depth + at + step, :] = both
    for out, earlier, count in zip(outs, before, counts):
        together = 1 if turned or count % 2 else 2
        for index in range(0, count, together):
            here = slice((begin + index) * rows, (begin + index + together) * rows)
            real, imag = (
                jnp.concatenate([held[part, here, at] for at in columns], axis=1) for part in (0, 1)
            )
            wide = dot32(wide_of(real, imag), weights[...])
            whole = wide[:, :BLOCK] + wide[:, BLOCK:]
            if turned:
                out[index] = whole.T if earlier is None else earlier[index] + whole.T
            else:
                out[index : index + together] = whole.reshape(together, rows, BLOCK)
        begin += count


def lift(
    held, ids, vectors, start_of, parts, rows, begin, counts, turned=False, tokens=(), before=()
):
    step, width = vectors[0].shape
    depth = step * len(parts)
    if not fast(rows, step):
        held = held[:, begin * rows : (begin + sum(counts)) * rows]
        result = 0
        for part, chunk in zip(parts, vectors):
            taken = lax.dynamic_slice_in_dim(held, start_of(ids[0], *part), step, 2)
            result += exact_dot(taken[0], chunk) + exact_dot(taken[1], turned_columns(chunk))
        result = result.reshape(-1, rows, width)
        result = jnp.transpose(result, (0, 2, 1)) if turned else result
        ends = [sum(counts[: i + 1]) for i in range(len(counts))]
        outs = [result[end - count : end] for end, count in zip(ends, counts)]
        return [out + earlier for out, earlier in zip(outs, before)] if before else outs
    shape = (width, rows) if turned else (rows, width)
    return call(
        functools.partial(
            lift_kernel, start_of, parts, rows, begin, counts, turned, len(before) > 0
        ),
        [
            (ids, pltpu.SMEM),
            *((chunk, VMEM) for chunk in vectors),
            (held, VMEM),
            *((array, VMEM) for array in before),
            *((token, pl.ANY) for token in tokens),
        ],
        [jax.ShapeDtypeStruct((count, *shape), jnp.float32) for count in counts],
        [VMEM((4 * depth, 2 * BLOCK), jnp.bfloat16)],
        2 * 4 * sum(counts) * rows * depth * 2 * BLOCK,
    )


def fold_kernel(start_of, chunks, has_total, turned, ids, *refs):
    chunk_refs, (held, *rest) = refs[: len(chunks)], refs[len(chunks) :]
    outs = rest[-2:] if turned else rest[-1:]
    total = rest[0][...] if has_total else None
    depth = chunk_refs[0].shape[0]
    for chunk, chunk_ref in zip(chunks, chunk_refs):
        values = chunk_ref[...]
        high, low = halves(values)
        turned_high, turned_low = halves(turned_columns(values))
        both = jnp.concatenate(
            [
                jnp.concatenate([high, low], axis=1),
                jnp.concatenate([turned_high, turned_low], axis=1),
            ],
            axis=0,
        )
        here = pl.ds(pl.multiple_of(start_of(ids[0], ids[1], *chunk), depth), depth)
        tile = wide_of(held[0, :, here], held[1, :, here])
        wide = dot32(tile, jnp.concatenate([both, both], axis=0))
        term = wide[:, :BLOCK] + wide[:, BLOCK:]
        total = term if total is None else total + term
    outs[0][...] = total
    if turned:
        outs[1][...] = total.T


def fold(held, ids, vectors, start_of, chunks, total, turned=False):
    rows, (depth, width) = held.shape[1], vectors[0].shape
    if not fast(rows, depth):
        for chunk, values in zip(chunks, vectors):
            column = start_of(ids[0], ids[1], *chunk)
            taken = lax.dynamic_slice(held, (0, 0, column), (2, rows, depth))
            term = exact_dot(taken[0], values) + exact_dot(taken[1], turned_columns(values))
            total = term if total is None else total + term
        return (total, total.T) if turned else total
    before = [] if total is None else [(total, VMEM)]
    shapes = [(rows, width), (width, rows)] if turned else [(rows, width)]
    outs = call(
        functools.partial(fold_kernel, start_of, chunks, total is not None, turned),
        [(ids, pltpu.SMEM), *((chunk, VMEM) for chunk in vectors), (held, VMEM), *before],
        [jax.ShapeDtypeStruct(shape, jnp.float32) for shape in shapes],
        [],
        2 * 4 * len(chunks) * rows * depth * 2 * BLOCK,
    )
    return outs if turned else outs[0]


def pull_kernel(begin, picks, arrays, has_total, minus, start_of, pieces, ids, *refs):
    array_refs, (held, *rest) = refs[:arrays], refs[arrays:]
    outs, total = rest[has_total:-1], rest[-1]
    count, depth, columns = len(picks), array_refs[0].shape[-1], held.shape[2]
    chunk_refs = [
        array_refs[at] if index is None else array_refs[at].at[index] for at, index in picks
    ]
    lefts = []
    for chunk in chunk_refs:
        values = chunk[...]
        high, low = halves(values)
        turned_high, turned_low = halves(turned_rows(values))
        lefts.append(
            (
                jnp.concatenate([high, low], axis=0),
                jnp.concatenate([turned_high, turned_low], axis=0),
            )
        )
    left = [jnp.concatenate(side, axis=1) for side in zip(*lefts)]
    rows = slice(begin * depth, (begin + count) * depth)
    for at in range(0, columns, 256):
        here = slice(at, min(at + 256, columns))
        term = rest[0][:, here] if has_total else None
        for part in (0, 1):
            high, low = halves(held[part, rows, here])
            wide = dot32(left[part], high)
            thin = dot32(left[part][:BLOCK], low)
            both = wide[:BLOCK] + wide[BLOCK:] + thin
            term = both if term is None else term - both if minus else term + both
        total[:, here] = term
    if not pieces:
        outs[0][...] = total[...]
    for piece, out in zip(pieces, outs):
        place = pl.multiple_of(start_of(ids[0], *piece), out.shape[1])
        out[...] = total[:, pl.ds(place, out.shape[1])]


def pull(
    held, ids, vectors, begin, total, start_of=None, pieces=(), size=0, minus=False, hides=True
):
    vectors = [vector if isinstance(vector, tuple) else (vector, None) for vector in vectors]
    columns, (width, depth) = held.shape[2], vectors[0][0].shape[-2:]
    if not fast(columns, depth):
        values = jnp.concatenate(
            [array if index is None else array[index] for array, index in vectors], axis=1
        )
        held = held[:, begin * depth : (begin + len(vectors)) * depth]
        term = exact_dot(values, held[0]) + exact_dot(turned_rows(values), held[1])
        total = term if total is None else total - term if minus else total + term
        if not pieces:
            return total
        return [
            lax.dynamic_slice(total, (0, start_of(ids[0], *piece)), (width, size))
            for piece in pieces
        ]
    before = [] if total is None else [(total, VMEM)]
    shapes = [(width, size)] * len(pieces) if pieces else [(width, columns)]
    arrays = list({id(array): array for array, _ in vectors}.values())
    at = {id(array): place for place, array in enumerate(arrays)}
    picks = [(at[id(array)], index) for array, index in vectors]
    outs = call(
        functools.partial(
            pull_kernel, begin, picks, len(arrays), total is not None, minus, start_of, pieces
        ),
        [(ids, pltpu.SMEM), *((array, VMEM) for array in arrays), (held, VMEM), *before],
        [jax.ShapeDtypeStruct(shape, jnp.float32) for shape in shapes],
        [VMEM((width, columns), jnp.float32)],
        2 * 3 * len(vectors) * depth * columns * 2 * BLOCK,
        hides=hides,
    )
    return outs if pieces else outs[0]


def spread_kernel(start_of, chunks, ids, vectors, held, *refs):
    outs = refs[-len(chunks) :]
    size = outs[0].shape[0]
    values = vectors[...]
    high, low = halves(values)
    turned_high, turned_low = halves(turned_rows(values))
    left = (
        jnp.concatenate([high, low], axis=0),
        jnp.concatenate([turned_high, turned_low], axis=0),
    )
    for chunk, out in zip(chunks, outs):
        here = pl.ds(pl.multiple_of(start_of(ids[0], ids[1], *chunk), size), size)
        term = None
        for part in (0, 1):
            high, low = halves(held[part, :, here])
            wide = dot32(left[part], high)
            thin = dot32(left[part][:BLOCK], low)
            both = wide[:BLOCK] + wide[BLOCK:] + thin
            term = both if term is None else term + both
        out[...] = term.T


def spread(held, ids, vectors, start_of, chunks, size):
    width, depth = vectors.shape
    if not fast(depth, size):
        whole = exact_dot(vectors, held[0]) + exact_dot(turned_rows(vectors), held[1])
        return [
            lax.dynamic_slice(whole, (0, start_of(ids[0], ids[1], *chunk)), (width, size)).T
            for chunk in chunks
        ]
    return call(
        functools.partial(spread_kernel, start_of, chunks),
        [(ids, pltpu.SMEM), (vectors, VMEM), (held, VMEM)],
        [jax.ShapeDtypeStruct((size, width), jnp.float32)] * len(chunks),
        [],
        2 * 3 * len(chunks) * depth * size * 2 * BLOCK,
    )


def add_kernel(indices, base_start, turned, *refs):
    outs = refs[-2:] if turned else refs[-1:]
    ids, base, *arrays = refs if base_start is not None else (None, None, *refs)
    total = None
    for index, ref in zip(indices, arrays):
        term = ref[...] if index is None else ref[index]
        total = term if total is None else total + term
    if base_start is not None:
        rows = total.shape[0]
        start = pl.multiple_of(base_start(ids[0]), rows)
        total = base[pl.ds(start, rows), :] - total
    outs[0][...] = total
    if turned:
        outs[1][...] = total.T


def add(terms, base=None, tokens=(), turned=False):
    arrays, indices = zip(*terms)
    shape = arrays[0].shape[-2:]
    if isinstance(indices[0], slice):
        shape = (indices[0].stop, *shape)
    if not fast(*shape[-2:]):
        total = sum(array if index is None else array[index] for array, index in terms)
        if base is not None:
            total = lax.dynamic_slice(base[1], (base[2](base[0][0]), 0), shape) - total
        return (total, total.T) if turned else total
    bases = [] if base is None else [(base[0], pltpu.SMEM), (base[1], VMEM)]
    shapes = [shape, shape[::-1]] if turned else [shape]
    outs = call(
        functools.partial(add_kernel, indices, None if base is None else base[2], turned),
        [*bases, *((array, VMEM) for array in arrays), *((token, pl.ANY) for token in tokens)],
        [jax.ShapeDtypeStruct(extent, jnp.float32) for extent in shapes],
        room=2,
    )
    return outs if turned else outs[0]


def settle_kernel(indices, ids, *refs):
    out = refs[-1]
    for leaf, (index, chunk) in enumerate(zip(indices, refs[:-1])):
        rows = chunk.shape[-1]
        place = pl.multiple_of((ids[0] ^ leaf) * rows, rows)
        out[pl.ds(place, rows), :] = (chunk[...] if index is None else chunk[index]).T


def settle(ids, chunks):
    chunks = [chunk if isinstance(chunk, tuple) else (chunk, None) for chunk in chunks]
    width, rows = chunks[0][0].shape[-2:]
    if not fast(width, rows):
        chunks = [array if index is None else array[index] for array, index in chunks]
        natural = jnp.take(jnp.stack(chunks), jnp.arange(len(chunks), dtype=jnp.int32) ^ ids[0], axis=0)
        return jnp.transpose(natural, (0, 2, 1)).reshape(-1, width)
    return call(
        functools.partial(settle_kernel, [index for _, index in chunks]),
        [(ids, pltpu.SMEM), *((array, VMEM) for array, _ in chunks)],
        [jax.ShapeDtypeStruct((len(chunks) * rows, width), jnp.float32)],
    )[0]


def swap(value, leaf_bits, front_bits):
    groups, fronts = lax.axis_size("leaf"), lax.axis_size("front")
    pairs = [
        (leaf * fronts + front, (leaf ^ leaf_bits) * fronts + (front ^ front_bits))
        for leaf in range(groups)
        for front in range(fronts)
    ]
    return lax.ppermute(value, ("leaf", "front"), pairs)


def across(value):
    return swap(value, 0, 1)


def along(value, apart):
    return swap(value, 0, 2 * apart)


def sibling(value):
    return swap(value, 1, 0)


def opposite(value):
    return swap(value, 2, 0)


def spread_chain(own, errands=(), with_beside=True, first_ready=()):
    held, apart = {0: own}, lax.axis_size("front") // 4
    errands, done, beside = list(errands), [], {}
    while apart:
        far = {place | apart: along(value, apart) for place, value in held.items()}
        ready = list(errands.pop(0)(own)) if errands else []
        done.append(list(ready))
        if len(done) == 1:
            ready += first_ready
        if with_beside:
            place = apart if len(done) > 1 else 0
            beside[place] = across(held[place] if place in held else far[place])
            ready.append(beside[place])
        if len(done) == 1 and apart > 1:
            near = along(own, apart // 2)
            ready.append(near)
        far[max(far)] = after(far[max(far)], ready)
        if len(done) == 2:
            far[apart] = near
        held.update(far)
        apart //= 2
    if with_beside:
        beside = {place: beside[place] if place in beside else across(held[place]) for place in held}
    return held, beside, done


def sum_chain(pieces, errands=(), first=(), **last):
    count, errands, done = len(pieces), list(errands), []
    terms = {
        place: kept if given is None else [*kept, (across(given), None)]
        for place, (kept, given) in pieces.items()
    }
    apart, ready = 1, list(first)
    while apart < count:
        top = max(place for place in range(apart, count, 2 * apart))
        for place in reversed(range(apart, count, 2 * apart)):
            summed = add(terms[place], tokens=ready)
            if place == top:
                ready = errands.pop(0)(summed) if errands else []
                done.append(ready)
            terms[place - apart] = [*terms[place - apart], (along(summed, apart), None)]
        apart *= 2
    return add(terms[0], tokens=ready, **last), done


def ways(place):
    return ((across, opposite), (1, 0), (0, 2)) if place % 2 else ((opposite, across), (0, 2), (1, 0))


def body(
    leaf_source,
    mid_source,
    root_source,
    leaf_inverse,
    leaf_coupling,
    mid_inverse,
    mid_coupling,
    root_inverse,
    leaf_blocks,
    mid_blocks,
):
    fronts = lax.axis_size("front")
    places = list(range(fronts // 2))
    downward = places[::-1]
    group, front = lax.axis_index("leaf"), lax.axis_index("front")
    ids = jnp.stack([group, front]).astype(jnp.int32)
    source_two, source_one = leaf_source[0], mid_source[0]
    inverse_two, coupling_two = leaf_inverse[0], leaf_coupling[0]
    inverse_one, coupling_one = mid_inverse[0], mid_coupling[0]
    rows_two = source_two.shape[0]
    half = source_one.shape[0]
    root_block = root_source.shape[0]
    quarter = root_block // lax.axis_size("leaf")
    root_rows = root_inverse.shape[1] // fronts

    child_two, child_one = orders(ids, leaf_blocks, mid_blocks)

    def two_start(group, front, leaf_bits, front_bits):
        return (front ^ front_bits) * rows_two

    def half_start(group, front, leaf_bits, front_bits):
        return (front ^ front_bits) * (2 * half) + ((group ^ leaf_bits) % 2) * half

    def one_start(group, front, leaf_bits, front_bits):
        return (front ^ front_bits) * half

    def quarter_start(group, front, leaf_bits, front_bits):
        return (front ^ front_bits) * root_block + (group ^ leaf_bits) * quarter

    def root_start(group, front, leaf_bits, front_bits):
        return (front ^ front_bits) * root_rows

    def whole_start(group, front):
        return 0

    def first_row(group):
        return 0

    def own_row(group):
        return group * quarter

    def side_row(group, bits):
        return ((group ^ bits) % 2) * half

    def leaf_row(group, bits):
        return (group ^ bits) * quarter

    def pair(place, leaf_bits=0):
        return [(leaf_bits, 2 * place + 1), (leaf_bits, 2 * place)]

    def arrivals(place, groups=(0,)):
        return [(leaf_bits, 2 * place + other) for other in (0, 1) for leaf_bits in groups]

    def square(place):
        _, first, second = ways(place)
        return [
            (first[1] | second[1], 2 * place + (first[0] | second[0])),
            (first[1], 2 * place + first[0]),
            (second[1], 2 * place + second[0]),
            (0, 2 * place),
        ]

    def square_both(place):
        return [(bits ^ 1, other) for bits, other in square(place)] + square(place)

    def square_arrivals(place):
        return [(bits ^ other, at) for bits, at in square(place)[::-1] for other in (0, 1)]

    count = len(places)
    early, late = downward[: count // 2], downward[count // 2 :]
    near, far = places[: count // 2], places[count // 2 :]

    def chunks_of(which, chunks):
        return [chunk for place in which for chunk in chunks(place)]

    def leaf_inverse_rows(token):
        return fetch(inverse_two, ids, None, whole_start, [()], inverse_two.shape[1], token)

    def leaf_lift_rows(which, token):
        chunks = chunks_of(which, lambda place: pair(place, 1)) + chunks_of(which, pair)
        return fetch(coupling_two, ids, child_two, half_start, chunks, half, token)

    def mid_lift_rows(which, token):
        return fetch(inverse_one, ids, None, one_start, chunks_of(which, pair), half, token)

    def root_lift_rows(which, token):
        chunks = chunks_of(which, square_both)
        return fetch(coupling_one, ids, child_one, quarter_start, chunks, quarter, token)

    def root_rows_of(which, token):
        return fetch(root_inverse, ids, None, root_start, chunks_of(which, pair), root_rows, token)

    def root_pull_rows(which, token):
        chunks = chunks_of(which, square_arrivals)
        return fetch(coupling_one, ids, child_one, quarter_start, chunks, quarter, token)

    def mid_pull_rows(which, token):
        return fetch(inverse_one, ids, None, one_start, chunks_of(which, arrivals), half, token)

    def leaf_pull_rows(which, token):
        chunks = chunks_of(which, lambda place: arrivals(place, (0, 1)))
        return fetch(coupling_two, ids, child_two, half_start, chunks, half, token)

    chain, beside, ((rows_inverse,), (rows_early,), *_) = spread_chain(
        source_two,
        [
            lambda token: [leaf_inverse_rows(token)],
            lambda token: [leaf_lift_rows(early, token)],
        ],
    )
    rows_late = leaf_lift_rows(late, rows_early)
    coming = [vector for place in places for vector in (chain[place], beside[place])]
    coming_chunks = chunks_of(places, arrivals)
    total = None
    for first, end in ((0, fronts // 2), (fronts // 2, fronts - 1), (fronts - 1, fronts)):
        last = end == fronts
        if last:
            coming[-1] = after(coming[-1], [rows_late])
        total = fold(
            rows_inverse, ids, coming[first:end], two_start, coming_chunks[first:end], total, last
        )
    solved_two, solved_two_turned = total

    def leaf_lift(held, which):
        size = 2 * len(which)
        theirs, mine = lift(held, ids, [solved_two], first_row, [()], half, 0, [size, size])
        theirs, terms = sibling(theirs), {}
        for at, place in enumerate(which):
            given = add([(mine, 2 * at), (theirs, 2 * at)])
            terms[place] = [(mine, 2 * at + 1), (theirs, 2 * at + 1)], given
        return terms, mine

    terms, _ = leaf_lift(rows_early, early)
    more, token = leaf_lift(rows_late, late)
    rows_one_early = mid_lift_rows(early, token)
    own_half, (_, (rows_one_late,), *_) = sum_chain(
        {**terms, **more},
        [lambda token: [], lambda token: [mid_lift_rows(late, token)]],
        [rows_one_early],
        base=(ids, source_one, first_row),
    )

    halves_one = [own_half, sibling(own_half)]

    def paired(which, parts):
        return {
            place: ([(kept, 0 if kept.ndim > 2 else None)], given.reshape(given.shape[-2:]))
            for place, given, kept in zip(which, parts[0::2], parts[1::2])
        }

    def mid_lift(held, which):
        ones = [1] * (2 * len(which))
        return lift(held, ids, halves_one, side_row, [(0,), (1,)], half, 0, ones)

    parts, more = mid_lift(rows_one_early, early), mid_lift(rows_one_late, late)
    (solved_one, solved_one_turned), ((rows_early,), (rows_late,), *_) = sum_chain(
        {**paired(early, parts), **paired(late, more)},
        [
            lambda token: [root_lift_rows(early, token)],
            lambda token: [root_lift_rows(late, token)],
        ],
        more[:1],
        turned=True,
    )

    def root_lift(held, begin, which, tokens=()):
        fours = [4] * (2 * len(which))
        return lift(
            held,
            ids,
            [solved_one],
            first_row,
            [()],
            quarter,
            8 * begin,
            fours,
            tokens=tokens,
        )

    def corner_terms(place, theirs, mine):
        (first_way, second_way), _, _ = ways(place)
        outer = first_way(add([(mine, slice(0, 2)), (theirs, slice(0, 2))]))
        inner = second_way(add([(mine, 2), (theirs, 2), (outer, 0)]))
        return [(mine, 3), (theirs, 3), (outer, 1), (inner, None)], None

    top, *rest = early
    (first_way, second_way), _, _ = ways(top)
    theirs, mine = root_lift(rows_early, 0, [top])
    theirs = sibling(theirs)
    parts = [part for at, place in enumerate(rest) for part in root_lift(rows_early, at + 1, [place])]
    corner = add([(mine, 0), (theirs, 0)], tokens=parts[-1:])
    parts += root_lift(rows_late, 0, late, [corner])
    first = first_way(add([(mine, 1), (theirs, 1)]))
    inner = add([(mine, 2), (theirs, 2), (first_way(corner), None)], tokens=parts[-1:])
    corners = {top: ([(mine, 3), (theirs, 3), (first, None), (second_way(inner), None)], None)}
    for place, theirs, mine in zip(rest + late, parts[0::2], parts[1::2]):
        corners[place] = corner_terms(place, sibling(theirs), mine)
    own_quarter, ((rows_root_early,), (rows_root_late,), *_) = sum_chain(
        corners,
        [
            lambda token: [root_rows_of(early, token)],
            lambda token: [root_rows_of(late, token)],
        ],
        base=(ids, root_source, own_row),
    )
    over_quarter = opposite(own_quarter)

    def root_apply(held, which, values, parts, before=()):
        ones = [1] * (2 * len(which))
        return lift(
            held, ids, values, leaf_row, parts, root_rows, 0, ones, turned=True, before=before
        )

    here = [own_quarter, sibling(own_quarter)]
    parts = root_apply(rows_root_early, early, here, [(0,), (1,)])
    more = root_apply(rows_root_late, late, here, [(0,), (1,)])
    over_quarter = after(over_quarter, [parts[0], more[0]])
    there = [over_quarter, sibling(over_quarter)]
    parts = root_apply(rows_root_early, early, there, [(2,), (3,)], parts)
    more = root_apply(rows_root_late, late, there, [(2,), (3,)], more)
    whole_root, (_, (rows_near,), *_) = sum_chain(
        {**paired(early, parts), **paired(late, more)},
        [lambda token: [], lambda token: [root_pull_rows(near, token)]],
        more[:1],
    )
    chain, beside, ((rows_far,), (rows_one_near,), *_) = spread_chain(
        whole_root,
        [
            lambda token: [root_pull_rows(far, token)],
            lambda token: [mid_pull_rows(near, token)],
        ],
    )
    late_vectors = [vector for place in late for vector in (beside[place], chain[place])]
    early_vectors = [vector for place in early for vector in (beside[place], chain[place])]
    total = pull(rows_root_late, ids, late_vectors, 0, None)
    total = pull(rows_root_early, ids, early_vectors[1:], 1, total)
    theirs_own, theirs_over, mine_own, mine_over = pull(
        rows_root_early, ids, early_vectors[:1], 0, total, leaf_row, [(1,), (3,), (0,), (2,)], quarter
    )
    rows_one_far = mid_pull_rows(far, mine_own)
    over = add([(mine_over, None), (sibling(theirs_over), None)])
    theirs_own = sibling(theirs_own)
    own_quarter = add(
        [(mine_own, None), (theirs_own, None), (opposite(over), None)], tokens=[rows_one_far]
    )

    def corner_values(place, value, ready=()):
        (first_way, second_way), _, _ = ways(place)
        first, second = first_way(value), second_way(value)
        return [value, second, first, second_way(after(first, ready))]

    corners = {0: corner_values(0, own_quarter)}
    chain, _, _ = spread_chain(own_quarter, (), False, corners[0][1:3])
    for place in places[1:-1]:
        value = chain[place]
        if place == count // 2:
            value = after(value, corners[0][3:], copied=True)
        corners[place] = corner_values(place, value)
    def with_theirs(values):
        theirs = sibling(jnp.stack(values) if len(values) > 1 else values[0])
        theirs = [(theirs, at) for at in range(len(values))] if len(values) > 1 else [theirs]
        return [vector for both in zip(values, theirs) for vector in both]

    def pull_one(held, vectors, first, total):
        return pull(held, ids, vectors, first, total, minus=True, hides=False)

    vectors = {}
    for place in places[:-1]:
        vectors[place] = with_theirs(corners[place])
        if place == near[-1]:
            corners[places[-1]] = corner_values(places[-1], chain[places[-1]])
    at = 4 if ways(0)[1][1] else 2
    root_solution = settle(ids, [*vectors[0][:2], *vectors[0][at : at + 2]])
    vectors[places[-1]] = with_theirs(corners[places[-1]][:3])
    rest_one = pull_one(rows_near, sum((vectors[place] for place in near), []), 0, solved_one_turned)
    rest_one = pull_one(rows_far, sum((vectors[place] for place in far), []), 0, rest_one)
    corner = after(corners[places[-1]][3], [rest_one])
    rest_one = pull_one(rows_far, with_theirs([corner]), 8 * len(far) - 2, rest_one)
    chain, beside, ((rows_near,), (rows_far, *_), *_) = spread_chain(
        rest_one,
        [
            lambda token: [leaf_pull_rows(near, token)],
            lambda token: [leaf_pull_rows(far, token), root_solution],
        ],
    )
    near_vectors = [vector for place in near for vector in (chain[place], beside[place])]
    far_vectors = [vector for place in far for vector in (chain[place], beside[place])]
    total = pull(rows_one_near, ids, near_vectors, 0, None)
    total = pull(rows_one_far, ids, far_vectors[:-1], 0, total)
    theirs, mine = pull(
        rows_one_far, ids, far_vectors[-1:], len(far_vectors) - 1, total, side_row, [(1,), (0,)], half
    )
    mid_columns, mid_solution = add([(mine, None), (sibling(theirs), None)], turned=True)

    chain, beside, ((rows_inverse,), *_) = spread_chain(
        mid_columns, [lambda token: [leaf_inverse_rows(token)]]
    )
    near_values = [value for place in near for value in (chain[place], beside[place])]
    far_values = [value for place in far for value in (chain[place], beside[place])]
    rest_two = pull(rows_near, ids, with_theirs(near_values), 0, solved_two_turned, minus=True)
    rest_two = pull(rows_far, ids, with_theirs(far_values[:-1]), 0, rest_two, minus=True)
    vectors = with_theirs([after(far_values[-1], [rest_two])])
    rest_two = pull(rows_far, ids, vectors, 2 * len(far_values) - 2, rest_two, minus=True)

    def leaf_spread(which):
        return spread(rows_inverse, ids, rest_two, two_start, chunks_of(which, pair), rows_two)

    parts, more = leaf_spread(early), leaf_spread(late)
    leaf_solution, _ = sum_chain({**paired(early, parts), **paired(late, more)}, (), more[:1])
    return (leaf_solution[None], mid_solution[None], root_solution)


def solution(mesh):
    placed = (
        P("leaf", "front", None),
        P("leaf", "front", None),
        P("front", None),
        P("leaf", None, "front", None),
        P("leaf", None, None, "front"),
        P("leaf", None, None, "front"),
        P("leaf", None, None, "front"),
        P(None, "leaf", "front"),
        P("leaf", None),
        P(),
    )
    return jax.shard_map(
        body,
        mesh=mesh,
        in_specs=placed,
        out_specs=(P("leaf", "front", None), P("leaf", "front", None), P("front", None)),
        check_vma=False,
    )
```

```python
import functools
import math

import jax
import jax.numpy as jnp
from jax import lax
from jax.experimental import pallas as pl
from jax.experimental.pallas import tpu as pltpu
from jax.sharding import PartitionSpec as P

BLOCK = 128
VMEM = pltpu.VMEM
exact_dot = functools.partial(jnp.dot, precision=lax.Precision.HIGHEST)


def halves(values):
    high = values.astype(jnp.bfloat16)
    low = (values - high.astype(jnp.float32)).astype(jnp.bfloat16)
    return high, low


def turned_columns(vectors):
    width = vectors.shape[1] // 2
    return jnp.concatenate([-vectors[:, width:], vectors[:, :width]], axis=1)


def turned_rows(vectors):
    width = vectors.shape[0] // 2
    return jnp.concatenate([-vectors[width:], vectors[:width]], axis=0)


def dot32(left, right):
    return jnp.dot(left, right, preferred_element_type=jnp.float32)


def fast(*extents):
    return all(extent % BLOCK == 0 for extent in extents)


def call(kernel, operands, outs, scratch=(), flops=0, room=10, hides=True):
    arrays, spaces = zip(*operands)
    size = lambda a: math.prod(a.shape) * a.dtype.itemsize
    held = sum(size(a) for a, space in operands if space == VMEM) + sum(size(o) for o in outs)
    scratch_bytes = sum(size(s) for s in scratch if hasattr(s, "shape") and s.memory_space == VMEM)
    moved = held if any(space == VMEM for space in spaces) else 2 * held
    flops, moved = (flops, moved) if hides else (1024, 1024)
    return pl.pallas_call(
        kernel,
        out_shape=outs,
        in_specs=[pl.BlockSpec(memory_space=space) for space in spaces],
        out_specs=[pl.BlockSpec(memory_space=VMEM)] * len(outs),
        scratch_shapes=scratch,
        compiler_params=pltpu.CompilerParams(
            vmem_limit_bytes=scratch_bytes + room * 1024 * 1024
        ),
        cost_estimate=pl.CostEstimate(flops=flops, bytes_accessed=moved, transcendentals=0),
    )(*arrays)


class Place:
    def __init__(self, ids, child):
        self.ids, self.child = ids, child

    def starts(self, start_of, chunks, rows):
        group, front = self.ids[0], self.ids[1]
        unit = rows if self.child is None else min(BLOCK, rows)
        for chunk in chunks:
            start = start_of(group, front, *chunk)
            for inner in range(0, rows, unit):
                row = start + inner
                if self.child is not None:
                    row = self.child[row // BLOCK] * BLOCK + row % BLOCK
                yield row


def orders_kernel(ids, leaf_blocks, mid_blocks, child_two, child_one):
    for index in range(leaf_blocks.shape[1]):
        child_two[leaf_blocks[0, index]] = index
    row = lax.shift_right_logical(ids[0], 1)
    for index in range(mid_blocks.shape[1]):
        child_one[mid_blocks[row, index]] = index


def orders(ids, leaf_blocks, mid_blocks):
    return pl.pallas_call(
        orders_kernel,
        out_shape=[
            jax.ShapeDtypeStruct((leaf_blocks.shape[1],), jnp.int32),
            jax.ShapeDtypeStruct((mid_blocks.shape[1],), jnp.int32),
        ],
        in_specs=[pl.BlockSpec(memory_space=pltpu.SMEM)] * 3,
        out_specs=[pl.BlockSpec(memory_space=pltpu.SMEM)] * 2,
        compiler_params=pltpu.CompilerParams(vmem_limit_bytes=1024 * 1024),
    )(ids, leaf_blocks, mid_blocks)


def fetch_kernel(start_of, chunks, rows, unit, with_child, ids, *refs):
    child = refs[0] if with_child else None
    matrix, out, sems = refs[-3:]
    copies = []
    for index, row in enumerate(Place(ids, child).starts(start_of, chunks, rows)):
        copy = pltpu.make_async_copy(
            matrix.at[:, pl.ds(pl.multiple_of(row, unit), unit), :],
            out.at[:, pl.ds(index * unit, unit), :],
            sems.at[index],
        )
        copy.start()
        copies.append(copy)
    for copy in copies:
        copy.wait()


def fetch(matrix, ids, child, start_of, chunks, rows, token):
    columns, count = matrix.shape[2], len(chunks) * rows
    unit = rows if child is None else min(BLOCK, rows)
    if not fast(rows, columns):
        starts = jnp.stack(list(Place(ids, child).starts(start_of, chunks, rows)))
        picked = (starts[:, None] + jnp.arange(unit, dtype=jnp.int32)).reshape(-1)
        return jnp.take(matrix, picked, axis=1)
    orders = [(ids, pltpu.SMEM)] + ([] if child is None else [(child, pltpu.SMEM)])
    pinned = pltpu.with_memory_space_constraint(matrix, pltpu.HBM)
    return call(
        functools.partial(fetch_kernel, start_of, chunks, rows, unit, child is not None),
        [*orders, (token, pl.ANY), (pinned, pl.ANY)],
        [jax.ShapeDtypeStruct((2, count, columns), jnp.float32)],
        [pltpu.SemaphoreType.DMA((count // unit,))],
        room=1,
    )[0]


def pass_kernel(*refs):
    del refs


def copy_kernel(*refs):
    refs[-1][...] = refs[-2][...]


def after(value, tokens, copied=False):
    if not tokens or not fast(*value.shape[-2:]):
        return value
    space = VMEM if copied else pl.ANY
    return pl.pallas_call(
        copy_kernel if copied else pass_kernel,
        out_shape=jax.ShapeDtypeStruct(value.shape, value.dtype),
        in_specs=[pl.BlockSpec(memory_space=pl.ANY)] * len(tokens)
        + [pl.BlockSpec(memory_space=space)],
        out_specs=pl.BlockSpec(memory_space=space),
        input_output_aliases={} if copied else {len(tokens): 0},
        compiler_params=pltpu.CompilerParams(vmem_limit_bytes=1024 * 1024),
        cost_estimate=pl.CostEstimate(flops=0, bytes_accessed=1024, transcendentals=0),
    )(*tokens, value)


def wide_of(real, imag):
    real_high, real_low = halves(real)
    imag_high, imag_low = halves(imag)
    return jnp.concatenate([real_high, imag_high, real_low, imag_low], axis=1)


def lift_kernel(start_of, parts, rows, begin, counts, turned, has_before, ids, *refs):
    chunk_refs, (held, *rest) = refs[: len(parts)], refs[len(parts) :]
    before = rest[: len(counts)] if has_before else [None] * len(counts)
    outs, weights = rest[-1 - len(counts) : -1], rest[-1]
    step = chunk_refs[0].shape[0]
    depth = step * len(parts)
    columns = []
    for place, (part, chunk) in enumerate(zip(parts, chunk_refs)):
        whole = held.shape[2] == step
        start = 0 if whole else pl.multiple_of(start_of(ids[0], *part), step)
        columns.append(slice(None) if whole else pl.ds(start, step))
        for half, values in enumerate((chunk[...], turned_columns(chunk[...]))):
            both = jnp.concatenate(halves(values), axis=1)
            at = half * depth + place * step
            weights[at : at + step, :] = both
            weights[2 * depth + at : 2 * depth + at + step, :] = both
    for out, earlier, count in zip(outs, before, counts):
        together = 1 if turned or count % 2 else 2
        for index in range(0, count, together):
            here = slice((begin + index) * rows, (begin + index + together) * rows)
            real, imag = (
                jnp.concatenate([held[part, here, at] for at in columns], axis=1) for part in (0, 1)
            )
            wide = dot32(wide_of(real, imag), weights[...])
            whole = wide[:, :BLOCK] + wide[:, BLOCK:]
            if turned:
                out[index] = whole.T if earlier is None else earlier[index] + whole.T
            else:
                out[index : index + together] = whole.reshape(together, rows, BLOCK)
        begin += count


def lift(
    held, ids, vectors, start_of, parts, rows, begin, counts, turned=False, tokens=(), before=()
):
    step, width = vectors[0].shape
    depth = step * len(parts)
    if not fast(rows, step):
        held = held[:, begin * rows : (begin + sum(counts)) * rows]
        result = 0
        for part, chunk in zip(parts, vectors):
            taken = lax.dynamic_slice_in_dim(held, start_of(ids[0], *part), step, 2)
            result += exact_dot(taken[0], chunk) + exact_dot(taken[1], turned_columns(chunk))
        result = result.reshape(-1, rows, width)
        result = jnp.transpose(result, (0, 2, 1)) if turned else result
        ends = [sum(counts[: i + 1]) for i in range(len(counts))]
        outs = [result[end - count : end] for end, count in zip(ends, counts)]
        return [out + earlier for out, earlier in zip(outs, before)] if before else outs
    shape = (width, rows) if turned else (rows, width)
    return call(
        functools.partial(
            lift_kernel, start_of, parts, rows, begin, counts, turned, len(before) > 0
        ),
        [
            (ids, pltpu.SMEM),
            *((chunk, VMEM) for chunk in vectors),
            (held, VMEM),
            *((array, VMEM) for array in before),
            *((token, pl.ANY) for token in tokens),
        ],
        [jax.ShapeDtypeStruct((count, *shape), jnp.float32) for count in counts],
        [VMEM((4 * depth, 2 * BLOCK), jnp.bfloat16)],
        2 * 4 * sum(counts) * rows * depth * 2 * BLOCK,
    )


def fold_kernel(start_of, chunks, has_total, turned, ids, *refs):
    chunk_refs, (held, *rest) = refs[: len(chunks)], refs[len(chunks) :]
    outs = rest[-2:] if turned else rest[-1:]
    total = rest[0][...] if has_total else None
    depth = chunk_refs[0].shape[0]
    for chunk, chunk_ref in zip(chunks, chunk_refs):
        values = chunk_ref[...]
        high, low = halves(values)
        turned_high, turned_low = halves(turned_columns(values))
        both = jnp.concatenate(
            [
                jnp.concatenate([high, low], axis=1),
                jnp.concatenate([turned_high, turned_low], axis=1),
            ],
            axis=0,
        )
        here = pl.ds(pl.multiple_of(start_of(ids[0], ids[1], *chunk), depth), depth)
        tile = wide_of(held[0, :, here], held[1, :, here])
        wide = dot32(tile, jnp.concatenate([both, both], axis=0))
        term = wide[:, :BLOCK] + wide[:, BLOCK:]
        total = term if total is None else total + term
    outs[0][...] = total
    if turned:
        outs[1][...] = total.T


def fold(held, ids, vectors, start_of, chunks, total, turned=False):
    rows, (depth, width) = held.shape[1], vectors[0].shape
    if not fast(rows, depth):
        for chunk, values in zip(chunks, vectors):
            column = start_of(ids[0], ids[1], *chunk)
            taken = lax.dynamic_slice(held, (0, 0, column), (2, rows, depth))
            term = exact_dot(taken[0], values) + exact_dot(taken[1], turned_columns(values))
            total = term if total is None else total + term
        return (total, total.T) if turned else total
    before = [] if total is None else [(total, VMEM)]
    shapes = [(rows, width), (width, rows)] if turned else [(rows, width)]
    outs = call(
        functools.partial(fold_kernel, start_of, chunks, total is not None, turned),
        [(ids, pltpu.SMEM), *((chunk, VMEM) for chunk in vectors), (held, VMEM), *before],
        [jax.ShapeDtypeStruct(shape, jnp.float32) for shape in shapes],
        [],
        2 * 4 * len(chunks) * rows * depth * 2 * BLOCK,
    )
    return outs if turned else outs[0]


def pull_kernel(begin, picks, arrays, has_total, minus, start_of, pieces, ids, *refs):
    array_refs, (held, *rest) = refs[:arrays], refs[arrays:]
    outs, total = rest[has_total:-1], rest[-1]
    count, depth, columns = len(picks), array_refs[0].shape[-1], held.shape[2]
    chunk_refs = [
        array_refs[at] if index is None else array_refs[at].at[index] for at, index in picks
    ]
    lefts = []
    for chunk in chunk_refs:
        values = chunk[...]
        high, low = halves(values)
        turned_high, turned_low = halves(turned_rows(values))
        lefts.append(
            (
                jnp.concatenate([high, low], axis=0),
                jnp.concatenate([turned_high, turned_low], axis=0),
            )
        )
    left = [jnp.concatenate(side, axis=1) for side in zip(*lefts)]
    rows = slice(begin * depth, (begin + count) * depth)
    for at in range(0, columns, 256):
        here = slice(at, min(at + 256, columns))
        term = rest[0][:, here] if has_total else None
        for part in (0, 1):
            high, low = halves(held[part, rows, here])
            wide = dot32(left[part], high)
            thin = dot32(left[part][:BLOCK], low)
            both = wide[:BLOCK] + wide[BLOCK:] + thin
            term = both if term is None else term - both if minus else term + both
        total[:, here] = term
    if not pieces:
        outs[0][...] = total[...]
    for piece, out in zip(pieces, outs):
        place = pl.multiple_of(start_of(ids[0], *piece), out.shape[1])
        out[...] = total[:, pl.ds(place, out.shape[1])]


def pull(
    held, ids, vectors, begin, total, start_of=None, pieces=(), size=0, minus=False, hides=True
):
    vectors = [vector if isinstance(vector, tuple) else (vector, None) for vector in vectors]
    columns, (width, depth) = held.shape[2], vectors[0][0].shape[-2:]
    if not fast(columns, depth):
        values = jnp.concatenate(
            [array if index is None else array[index] for array, index in vectors], axis=1
        )
        held = held[:, begin * depth : (begin + len(vectors)) * depth]
        term = exact_dot(values, held[0]) + exact_dot(turned_rows(values), held[1])
        total = term if total is None else total - term if minus else total + term
        if not pieces:
            return total
        return [
            lax.dynamic_slice(total, (0, start_of(ids[0], *piece)), (width, size))
            for piece in pieces
        ]
    before = [] if total is None else [(total, VMEM)]
    shapes = [(width, size)] * len(pieces) if pieces else [(width, columns)]
    arrays = list({id(array): array for array, _ in vectors}.values())
    at = {id(array): place for place, array in enumerate(arrays)}
    picks = [(at[id(array)], index) for array, index in vectors]
    outs = call(
        functools.partial(
            pull_kernel, begin, picks, len(arrays), total is not None, minus, start_of, pieces
        ),
        [(ids, pltpu.SMEM), *((array, VMEM) for array in arrays), (held, VMEM), *before],
        [jax.ShapeDtypeStruct(shape, jnp.float32) for shape in shapes],
        [VMEM((width, columns), jnp.float32)],
        2 * 3 * len(vectors) * depth * columns * 2 * BLOCK,
        hides=hides,
    )
    return outs if pieces else outs[0]


def spread_kernel(start_of, chunks, ids, vectors, held, *refs):
    outs = refs[-len(chunks) :]
    size = outs[0].shape[0]
    values = vectors[...]
    high, low = halves(values)
    turned_high, turned_low = halves(turned_rows(values))
    left = (
        jnp.concatenate([high, low], axis=0),
        jnp.concatenate([turned_high, turned_low], axis=0),
    )
    for chunk, out in zip(chunks, outs):
        here = pl.ds(pl.multiple_of(start_of(ids[0], ids[1], *chunk), size), size)
        term = None
        for part in (0, 1):
            high, low = halves(held[part, :, here])
            wide = dot32(left[part], high)
            thin = dot32(left[part][:BLOCK], low)
            both = wide[:BLOCK] + wide[BLOCK:] + thin
            term = both if term is None else term + both
        out[...] = term.T


def spread(held, ids, vectors, start_of, chunks, size):
    width, depth = vectors.shape
    if not fast(depth, size):
        whole = exact_dot(vectors, held[0]) + exact_dot(turned_rows(vectors), held[1])
        return [
            lax.dynamic_slice(whole, (0, start_of(ids[0], ids[1], *chunk)), (width, size)).T
            for chunk in chunks
        ]
    return call(
        functools.partial(spread_kernel, start_of, chunks),
        [(ids, pltpu.SMEM), (vectors, VMEM), (held, VMEM)],
        [jax.ShapeDtypeStruct((size, width), jnp.float32)] * len(chunks),
        [],
        2 * 3 * len(chunks) * depth * size * 2 * BLOCK,
    )


def add_kernel(indices, base_start, turned, *refs):
    outs = refs[-2:] if turned else refs[-1:]
    ids, base, *arrays = refs if base_start is not None else (None, None, *refs)
    total = None
    for index, ref in zip(indices, arrays):
        term = ref[...] if index is None else ref[index]
        total = term if total is None else total + term
    if base_start is not None:
        rows = total.shape[0]
        start = pl.multiple_of(base_start(ids[0]), rows)
        total = base[pl.ds(start, rows), :] - total
    outs[0][...] = total
    if turned:
        outs[1][...] = total.T


def add(terms, base=None, tokens=(), turned=False):
    arrays, indices = zip(*terms)
    shape = arrays[0].shape[-2:]
    if isinstance(indices[0], slice):
        shape = (indices[0].stop, *shape)
    if not fast(*shape[-2:]):
        total = sum(array if index is None else array[index] for array, index in terms)
        if base is not None:
            total = lax.dynamic_slice(base[1], (base[2](base[0][0]), 0), shape) - total
        return (total, total.T) if turned else total
    bases = [] if base is None else [(base[0], pltpu.SMEM), (base[1], VMEM)]
    shapes = [shape, shape[::-1]] if turned else [shape]
    outs = call(
        functools.partial(add_kernel, indices, None if base is None else base[2], turned),
        [*bases, *((array, VMEM) for array in arrays), *((token, pl.ANY) for token in tokens)],
        [jax.ShapeDtypeStruct(extent, jnp.float32) for extent in shapes],
        room=2,
    )
    return outs if turned else outs[0]


def settle_kernel(indices, ids, *refs):
    out = refs[-1]
    for leaf, (index, chunk) in enumerate(zip(indices, refs[:-1])):
        rows = chunk.shape[-1]
        place = pl.multiple_of((ids[0] ^ leaf) * rows, rows)
        out[pl.ds(place, rows), :] = (chunk[...] if index is None else chunk[index]).T


def settle(ids, chunks):
    chunks = [chunk if isinstance(chunk, tuple) else (chunk, None) for chunk in chunks]
    width, rows = chunks[0][0].shape[-2:]
    if not fast(width, rows):
        chunks = [array if index is None else array[index] for array, index in chunks]
        natural = jnp.take(jnp.stack(chunks), jnp.arange(len(chunks), dtype=jnp.int32) ^ ids[0], axis=0)
        return jnp.transpose(natural, (0, 2, 1)).reshape(-1, width)
    return call(
        functools.partial(settle_kernel, [index for _, index in chunks]),
        [(ids, pltpu.SMEM), *((array, VMEM) for array, _ in chunks)],
        [jax.ShapeDtypeStruct((len(chunks) * rows, width), jnp.float32)],
    )[0]


def swap(value, leaf_bits, front_bits):
    groups, fronts = lax.axis_size("leaf"), lax.axis_size("front")
    pairs = [
        (leaf * fronts + front, (leaf ^ leaf_bits) * fronts + (front ^ front_bits))
        for leaf in range(groups)
        for front in range(fronts)
    ]
    return lax.ppermute(value, ("leaf", "front"), pairs)


def across(value):
    return swap(value, 0, 1)


def along(value, apart):
    return swap(value, 0, 2 * apart)


def sibling(value):
    return swap(value, 1, 0)


def opposite(value):
    return swap(value, 2, 0)


def spread_chain(own, errands=(), with_beside=True, first_ready=()):
    held, apart = {0: own}, lax.axis_size("front") // 4
    errands, done, beside = list(errands), [], {}
    while apart:
        far = {place | apart: along(value, apart) for place, value in held.items()}
        ready = list(errands.pop(0)(own)) if errands else []
        done.append(list(ready))
        if len(done) == 1:
            ready += first_ready
        if with_beside:
            place = apart if len(done) > 1 else 0
            beside[place] = across(held[place] if place in held else far[place])
            ready.append(beside[place])
        if len(done) == 1 and apart > 1:
            near = along(own, apart // 2)
            ready.append(near)
        far[max(far)] = after(far[max(far)], ready)
        if len(done) == 2:
            far[apart] = near
        held.update(far)
        apart //= 2
    if with_beside:
        beside = {place: beside[place] if place in beside else across(held[place]) for place in held}
    return held, beside, done


def sum_chain(pieces, errands=(), first=(), **last):
    count, errands, done = len(pieces), list(errands), []
    terms = {
        place: kept if given is None else [*kept, (across(given), None)]
        for place, (kept, given) in pieces.items()
    }
    apart, ready = 1, list(first)
    while apart < count:
        top = max(place for place in range(apart, count, 2 * apart))
        for place in reversed(range(apart, count, 2 * apart)):
            summed = add(terms[place], tokens=ready)
            if place == top:
                ready = errands.pop(0)(summed) if errands else []
                done.append(ready)
            terms[place - apart] = [*terms[place - apart], (along(summed, apart), None)]
        apart *= 2
    return add(terms[0], tokens=ready, **last), done


def ways(place):
    return ((across, opposite), (1, 0), (0, 2)) if place % 2 else ((opposite, across), (0, 2), (1, 0))


def body(
    leaf_source,
    mid_source,
    root_source,
    leaf_inverse,
    leaf_coupling,
    mid_inverse,
    mid_coupling,
    root_inverse,
    leaf_blocks,
    mid_blocks,
):
    fronts = lax.axis_size("front")
    places = list(range(fronts // 2))
    downward = places[::-1]
    group, front = lax.axis_index("leaf"), lax.axis_index("front")
    ids = jnp.stack([group, front]).astype(jnp.int32)
    source_two, source_one = leaf_source[0], mid_source[0]
    inverse_two, coupling_two = leaf_inverse[0], leaf_coupling[0]
    inverse_one, coupling_one = mid_inverse[0], mid_coupling[0]
    rows_two = source_two.shape[0]
    half = source_one.shape[0]
    root_block = root_source.shape[0]
    quarter = root_block // lax.axis_size("leaf")
    root_rows = root_inverse.shape[1] // fronts

    child_two, child_one = orders(ids, leaf_blocks, mid_blocks)

    def two_start(group, front, leaf_bits, front_bits):
        return (front ^ front_bits) * rows_two

    def half_start(group, front, leaf_bits, front_bits):
        return (front ^ front_bits) * (2 * half) + ((group ^ leaf_bits) % 2) * half

    def one_start(group, front, leaf_bits, front_bits):
        return (front ^ front_bits) * half

    def quarter_start(group, front, leaf_bits, front_bits):
        return (front ^ front_bits) * root_block + (group ^ leaf_bits) * quarter

    def root_start(group, front, leaf_bits, front_bits):
        return (front ^ front_bits) * root_rows

    def whole_start(group, front):
        return 0

    def first_row(group):
        return 0

    def own_row(group):
        return group * quarter

    def side_row(group, bits):
        return ((group ^ bits) % 2) * half

    def leaf_row(group, bits):
        return (group ^ bits) * quarter

    def pair(place, leaf_bits=0):
        return [(leaf_bits, 2 * place + 1), (leaf_bits, 2 * place)]

    def arrivals(place, groups=(0,)):
        return [(leaf_bits, 2 * place + other) for other in (0, 1) for leaf_bits in groups]

    def square(place):
        _, first, second = ways(place)
        return [
            (first[1] | second[1], 2 * place + (first[0] | second[0])),
            (first[1], 2 * place + first[0]),
            (second[1], 2 * place + second[0]),
            (0, 2 * place),
        ]

    def square_both(place):
        return [(bits ^ 1, other) for bits, other in square(place)] + square(place)

    def square_arrivals(place):
        return [(bits ^ other, at) for bits, at in square(place)[::-1] for other in (0, 1)]

    count = len(places)
    early, late = downward[: count // 2], downward[count // 2 :]
    near, far = places[: count // 2], places[count // 2 :]

    def chunks_of(which, chunks):
        return [chunk for place in which for chunk in chunks(place)]

    def leaf_inverse_rows(token):
        return fetch(inverse_two, ids, None, whole_start, [()], inverse_two.shape[1], token)

    def leaf_lift_rows(which, token):
        chunks = chunks_of(which, lambda place: pair(place, 1)) + chunks_of(which, pair)
        return fetch(coupling_two, ids, child_two, half_start, chunks, half, token)

    def mid_lift_rows(which, token):
        return fetch(inverse_one, ids, None, one_start, chunks_of(which, pair), half, token)

    def root_lift_rows(which, token):
        chunks = chunks_of(which, square_both)
        return fetch(coupling_one, ids, child_one, quarter_start, chunks, quarter, token)

    def root_rows_of(which, token):
        return fetch(root_inverse, ids, None, root_start, chunks_of(which, pair), root_rows, token)

    def root_pull_rows(which, token):
        chunks = chunks_of(which, square_arrivals)
        return fetch(coupling_one, ids, child_one, quarter_start, chunks, quarter, token)

    def mid_pull_rows(which, token):
        return fetch(inverse_one, ids, None, one_start, chunks_of(which, arrivals), half, token)

    def leaf_pull_rows(which, token):
        chunks = chunks_of(which, lambda place: arrivals(place, (0, 1)))
        return fetch(coupling_two, ids, child_two, half_start, chunks, half, token)

    chain, beside, ((rows_inverse,), (rows_early,), *_) = spread_chain(
        source_two,
        [
            lambda token: [leaf_inverse_rows(token)],
            lambda token: [leaf_lift_rows(early, token)],
        ],
    )
    rows_late = leaf_lift_rows(late, rows_early)
    coming = [vector for place in places for vector in (chain[place], beside[place])]
    coming_chunks = chunks_of(places, arrivals)
    total = None
    for first, end in ((0, fronts // 2), (fronts // 2, fronts - 1), (fronts - 1, fronts)):
        last = end == fronts
        if last:
            coming[-1] = after(coming[-1], [rows_late])
        total = fold(
            rows_inverse, ids, coming[first:end], two_start, coming_chunks[first:end], total, last
        )
    solved_two, solved_two_turned = total

    def leaf_lift(held, which):
        size = 2 * len(which)
        theirs, mine = lift(held, ids, [solved_two], first_row, [()], half, 0, [size, size])
        theirs, terms = sibling(theirs), {}
        for at, place in enumerate(which):
            given = add([(mine, 2 * at), (theirs, 2 * at)])
            terms[place] = [(mine, 2 * at + 1), (theirs, 2 * at + 1)], given
        return terms, mine

    terms, _ = leaf_lift(rows_early, early)
    more, token = leaf_lift(rows_late, late)
    rows_one_early = mid_lift_rows(early, token)
    own_half, (_, (rows_one_late,), *_) = sum_chain(
        {**terms, **more},
        [lambda token: [], lambda token: [mid_lift_rows(late, token)]],
        [rows_one_early],
        base=(ids, source_one, first_row),
    )

    halves_one = [own_half, sibling(own_half)]

    def paired(which, parts):
        return {
            place: ([(kept, 0 if kept.ndim > 2 else None)], given.reshape(given.shape[-2:]))
            for place, given, kept in zip(which, parts[0::2], parts[1::2])
        }

    def mid_lift(held, which):
        ones = [1] * (2 * len(which))
        return lift(held, ids, halves_one, side_row, [(0,), (1,)], half, 0, ones)

    parts, more = mid_lift(rows_one_early, early), mid_lift(rows_one_late, late)
    (solved_one, solved_one_turned), ((rows_early,), (rows_late,), *_) = sum_chain(
        {**paired(early, parts), **paired(late, more)},
        [
            lambda token: [root_lift_rows(early, token)],
            lambda token: [root_lift_rows(late, token)],
        ],
        more[:1],
        turned=True,
    )

    def root_lift(held, begin, which, tokens=()):
        fours = [4] * (2 * len(which))
        return lift(
            held,
            ids,
            [solved_one],
            first_row,
            [()],
            quarter,
            8 * begin,
            fours,
            tokens=tokens,
        )

    def corner_terms(place, theirs, mine):
        (first_way, second_way), _, _ = ways(place)
        outer = first_way(add([(mine, slice(0, 2)), (theirs, slice(0, 2))]))
        inner = second_way(add([(mine, 2), (theirs, 2), (outer, 0)]))
        return [(mine, 3), (theirs, 3), (outer, 1), (inner, None)], None

    top, *rest = early
    (first_way, second_way), _, _ = ways(top)
    theirs, mine = root_lift(rows_early, 0, [top])
    theirs = sibling(theirs)
    parts = [part for at, place in enumerate(rest) for part in root_lift(rows_early, at + 1, [place])]
    corner = add([(mine, 0), (theirs, 0)], tokens=parts[-1:])
    parts += root_lift(rows_late, 0, late, [corner])
    first = first_way(add([(mine, 1), (theirs, 1)]))
    inner = add([(mine, 2), (theirs, 2), (first_way(corner), None)], tokens=parts[-1:])
    corners = {top: ([(mine, 3), (theirs, 3), (first, None), (second_way(inner), None)], None)}
    for place, theirs, mine in zip(rest + late, parts[0::2], parts[1::2]):
        corners[place] = corner_terms(place, sibling(theirs), mine)
    own_quarter, ((rows_root_early,), (rows_root_late,), *_) = sum_chain(
        corners,
        [
            lambda token: [root_rows_of(early, token)],
            lambda token: [root_rows_of(late, token)],
        ],
        base=(ids, root_source, own_row),
    )
    over_quarter = opposite(own_quarter)

    def root_apply(held, which, values, parts, before=(), begin=0):
        ones = [1] * (2 * len(which))
        return lift(
            held, ids, values, leaf_row, parts, root_rows, begin, ones, turned=True, before=before
        )

    here = [own_quarter, sibling(own_quarter)]
    parts = root_apply(rows_root_early, early, here, [(0,), (1,)])
    more = root_apply(rows_root_late, late, here, [(0,), (1,)])
    over_quarter = after(over_quarter, [parts[0], more[0]])
    there = [over_quarter, sibling(over_quarter)]
    ends = [(2,), (3,)]
    parts = [
        *root_apply(rows_root_early, early[:1], there, ends, parts[:2]),
        *root_apply(rows_root_early, early[1:], there, ends, parts[2:], 2),
    ]
    more = root_apply(rows_root_late, late, there, ends, more)
    whole_root, (_, (rows_near,), *_) = sum_chain(
        {**paired(early, parts), **paired(late, more)},
        [lambda token: [], lambda token: [root_pull_rows(near, token)]],
        more[:1],
    )
    chain, beside, ((rows_far,), (rows_one_near,), *_) = spread_chain(
        whole_root,
        [
            lambda token: [root_pull_rows(far, token)],
            lambda token: [mid_pull_rows(near, token)],
        ],
    )
    late_vectors = [vector for place in late for vector in (beside[place], chain[place])]
    early_vectors = [vector for place in early for vector in (beside[place], chain[place])]
    total = pull(rows_root_late, ids, late_vectors, 0, None)
    total = pull(rows_root_early, ids, early_vectors[1:], 1, total)
    theirs_own, theirs_over, mine_own, mine_over = pull(
        rows_root_early, ids, early_vectors[:1], 0, total, leaf_row, [(1,), (3,), (0,), (2,)], quarter
    )
    rows_one_far = mid_pull_rows(far, mine_own)
    over = add([(mine_over, None), (sibling(theirs_over), None)])
    theirs_own = sibling(theirs_own)
    own_quarter = add(
        [(mine_own, None), (theirs_own, None), (opposite(over), None)], tokens=[rows_one_far]
    )

    def corner_values(place, value, ready=()):
        (first_way, second_way), _, _ = ways(place)
        first, second = first_way(value), second_way(value)
        return [value, second, first, second_way(after(first, ready))]

    corners = {0: corner_values(0, own_quarter)}
    chain, _, _ = spread_chain(own_quarter, (), False, corners[0][1:3])
    for place in places[1:-1]:
        value = chain[place]
        if place == count // 2:
            value = after(value, corners[0][3:], copied=True)
        corners[place] = corner_values(place, value)
    def with_theirs(values):
        theirs = sibling(jnp.stack(values) if len(values) > 1 else values[0])
        theirs = [(theirs, at) for at in range(len(values))] if len(values) > 1 else [theirs]
        return [vector for both in zip(values, theirs) for vector in both]

    def pull_one(held, vectors, first, total):
        return pull(held, ids, vectors, first, total, minus=True, hides=False)

    vectors = {}
    for place in places[:-1]:
        vectors[place] = with_theirs(corners[place])
        if place == near[-1]:
            corners[places[-1]] = corner_values(places[-1], chain[places[-1]])
    at = 4 if ways(0)[1][1] else 2
    root_solution = settle(ids, [*vectors[0][:2], *vectors[0][at : at + 2]])
    vectors[places[-1]] = with_theirs(corners[places[-1]][:3])
    rest_one = pull_one(rows_near, sum((vectors[place] for place in near), []), 0, solved_one_turned)
    rest_one = pull_one(rows_far, sum((vectors[place] for place in far), []), 0, rest_one)
    corner = after(corners[places[-1]][3], [rest_one])
    rest_one = pull_one(rows_far, with_theirs([corner]), 8 * len(far) - 2, rest_one)
    chain, beside, ((rows_near,), (rows_far, *_), *_) = spread_chain(
        rest_one,
        [
            lambda token: [leaf_pull_rows(near, token)],
            lambda token: [leaf_pull_rows(far, token), root_solution],
        ],
    )
    near_vectors = [vector for place in near for vector in (chain[place], beside[place])]
    far_vectors = [vector for place in far for vector in (chain[place], beside[place])]
    total = pull(rows_one_near, ids, near_vectors, 0, None)
    total = pull(rows_one_far, ids, far_vectors[:-1], 0, total)
    theirs, mine = pull(
        rows_one_far, ids, far_vectors[-1:], len(far_vectors) - 1, total, side_row, [(1,), (0,)], half
    )
    mid_columns, mid_solution = add([(mine, None), (sibling(theirs), None)], turned=True)

    chain, beside, ((rows_inverse,), *_) = spread_chain(
        mid_columns, [lambda token: [leaf_inverse_rows(token)]]
    )
    near_values = [value for place in near for value in (chain[place], beside[place])]
    far_values = [value for place in far for value in (chain[place], beside[place])]
    rest_two = pull(rows_near, ids, with_theirs(near_values), 0, solved_two_turned, minus=True)
    rest_two = pull(rows_far, ids, with_theirs(far_values[:-1]), 0, rest_two, minus=True)
    vectors = with_theirs([after(far_values[-1], [rest_two])])
    rest_two = pull(rows_far, ids, vectors, 2 * len(far_values) - 2, rest_two, minus=True)

    def leaf_spread(which):
        return spread(rows_inverse, ids, rest_two, two_start, chunks_of(which, pair), rows_two)

    parts, more = leaf_spread(early[:1]), leaf_spread(early[1:] + late)
    leaf_solution, _ = sum_chain(
        {**paired(early[:1], parts), **paired(early[1:] + late, more)}, (), more[:1]
    )
    return (leaf_solution[None], mid_solution[None], root_solution)


def solution(mesh):
    placed = (
        P("leaf", "front", None),
        P("leaf", "front", None),
        P("front", None),
        P("leaf", None, "front", None),
        P("leaf", None, None, "front"),
        P("leaf", None, None, "front"),
        P("leaf", None, None, "front"),
        P(None, "leaf", "front"),
        P("leaf", None),
        P(),
    )
    return jax.shard_map(
        body,
        mesh=mesh,
        in_specs=placed,
        out_specs=(P("leaf", "front", None), P("leaf", "front", None), P("front", None)),
        check_vma=False,
    )
```
